32 devices in a mesh: dp: 4 (over y, x), mp: 8 (over z, core).
Axes of the slice: x: 2, y: 2, z: 4, core: 2. Of those that a mesh axis runs over, the one named last changes fastest.
Arguments:
- tokens: bfloat16 [3072, 2048], P(('dp', 'mp')), may hold values from -6 to 6
- lengths: int32 [4, 3], P('dp'), may hold values from 64 to 624, as said below
- first_gain: float32 [2048], replicated, may hold values from 0.25 to 1.75
- branch_gate: bfloat16 [2048, 2560], P(None, 'mp'), may hold values from -0.125 to 0.125
- branch_input: bfloat16 [2048, 2560], P(None, 'mp'), may hold values from -0.125 to 0.125
- conv_weight: float32 [4, 2560], P(None, 'mp'), may hold values from -3 to 3
- conv_bias: float32 [2560], P('mp'), may hold values from -3 to 3
- rate_weight: bfloat16 [16, 160, 160], P('mp'), may hold values from -0.5 to 0.5
- rate_bias: float32 [2560], P('mp'), may hold values from -3 to 3
- inlet_weight: bfloat16 [16, 160, 160], P('mp'), may hold values from -0.5 to 0.5
- inlet_bias: float32 [2560], P('mp'), may hold values from -3 to 3
- decay_param: float32 [2560], P('mp'), may hold values from -9 to -1
- block_out: bfloat16 [2560, 2048], P('mp'), may hold values from -0.3125 to 0.3125
- second_gain: float32 [2048], replicated, may hold values from 0.25 to 1.75
- gate_weight: bfloat16 [2048, 6144], P(None, 'mp'), may hold values from -0.125 to 0.125
- up_weight: bfloat16 [2048, 6144], P(None, 'mp'), may hold values from -0.125 to 0.125
- down_weight: bfloat16 [6144, 2048], P('mp'), may hold values from -0.125 to 0.125
- out_grad: bfloat16 [3072, 2048], P(('dp', 'mp')), may hold values from -6 to 6
Outputs:
- output: bfloat16 [3072, 2048], P(('dp', 'mp'))
- input_grad: float32 [3072, 2048], P(('dp', 'mp'))
- first_gain_grad: float32 [2048], replicated
- branch_gate_grad: float32 [2048, 2560], P(None, 'mp')
- branch_input_grad: float32 [2048, 2560], P(None, 'mp')
- conv_weight_grad: float32 [4, 2560], P(None, 'mp')
- conv_bias_grad: float32 [2560], P('mp')
- rate_weight_grad: float32 [16, 160, 160], P('mp')
- rate_bias_grad: float32 [2560], P('mp')
- inlet_weight_grad: float32 [16, 160, 160], P('mp')
- inlet_bias_grad: float32 [2560], P('mp')
- decay_param_grad: float32 [2560], P('mp')
- block_out_grad: float32 [2560, 2048], P('mp')
- second_gain_grad: float32 [2048], replicated
- gate_weight_grad: float32 [2048, 6144], P(None, 'mp')
- up_weight_grad: float32 [2048, 6144], P(None, 'mp')
- down_weight_grad: float32 [6144, 2048], P('mp')
The draws below stay inside these ranges and needn't reach their ends.
Inputs may be any that keep to these rules, and one draw needn't show every extreme that they name: Each row lists in order the lengths of the 3 sequences packed into one bucket of 768 rows; they sum to 768; the middle one has 624 tokens, and the first and last have 96 * 2 // 3 and 80 tokens, in either order.
All inputs are finite; a program needn't handle non-finite values.
Results may differ from the reference program's by a relative error of at most 0.018.
Values may be sent and summed in bfloat16 or wider, within the bound.
No kernel may reach another device: no remote copies, remote signals or barrier semaphores. Data moves between devices by JAX's collectives and lax.ppermute only.
A program may use at most 256 MiB of HBM per device.

```python
import jax
import jax.numpy as jnp
from jax import lax

D = 2048
RR = 2560
HEADS = 16
FF = 6144
KW = 4
TOK_DEV = 96
BW = 160
BUCKET = 768
NBUCKETS = 4
TOKENS = 3072


def draw_lengths(key, part):
    key = jax.random.fold_in(key, 11)
    flipped = jax.random.randint(key, (NBUCKETS, 1), 0, 2)
    short_low = TOK_DEV * 2 // 3
    short_high = TOK_DEV * 5 // 6
    first_short = jnp.where(flipped == 0, short_low, short_high)
    last_short = short_low + short_high - first_short
    middle_long = jnp.full((NBUCKETS, 1), BUCKET - short_low - short_high, jnp.int32)
    return jnp.concatenate([first_short, middle_long, last_short], axis=1).astype(jnp.int32)


def block_scale(key, extent, split, smallest, top_value):
    level = 1.0
    for axis_at, parts in split:
        draws = jax.random.uniform(jax.random.fold_in(jax.random.fold_in(key, 6), axis_at), (parts,), jnp.float32, smallest / len(split), top_value / len(split))
        level = level * jnp.repeat(jnp.exp(draws), extent[axis_at] // parts).reshape((-1,) + (1,) * (len(extent) - 1 - axis_at))
    return level


def bell_draw(key, dims, deviation, bound, pieces=(), kind=jnp.bfloat16):
    values = deviation * jax.random.normal(key, dims, jnp.float32)
    if pieces:
        values = values * block_scale(key, dims, pieces, -0.22, 0.18)
    return jnp.clip(values, -bound, bound).astype(kind)


def setup_inputs(seed: int = 0) -> dict:
    streams_of = jax.random.split(jax.random.key(seed), 19)
    tokens = bell_draw(streams_of[0], (TOKENS, D), 1.0, 6.0, ((0, 32),))
    lengths = draw_lengths(jax.random.fold_in(streams_of[18], 71), 0)
    first_gain = jnp.clip(1.0 + 0.15 * jax.random.normal(streams_of[2], (D,), jnp.float32), 0.25, 1.75)
    branch_gate = bell_draw(streams_of[3], (D, RR), D ** -0.5, 0.125, ((1, 8),))
    branch_input = bell_draw(streams_of[4], (D, RR), D ** -0.5, 0.125, ((1, 8),))
    conv_weight = bell_draw(streams_of[5], (KW, RR), KW ** -0.5, 3.0, ((1, 8),), jnp.float32)
    conv_bias = bell_draw(streams_of[6], (RR,), 0.5, 3.0, ((0, 8),), jnp.float32)
    rate_weight = bell_draw(streams_of[7], (HEADS, BW, BW), BW ** -0.5, 0.5, ((0, 8),))
    rate_bias = bell_draw(streams_of[8], (RR,), 1.0, 3.0, ((0, 8),), jnp.float32)
    inlet_weight = bell_draw(streams_of[9], (HEADS, BW, BW), BW ** -0.5, 0.5, ((0, 8),))
    inlet_bias = bell_draw(streams_of[10], (RR,), 1.0, 3.0, ((0, 8),), jnp.float32)
    decay_param = jnp.clip(-9.0 + 8.0 * jax.random.uniform(streams_of[11], (RR,), jnp.float32) ** block_scale(streams_of[11], (RR,), ((0, 8),), -0.2, 0.2), -9.0, -1.0)
    block_out = bell_draw(streams_of[12], (RR, D), (RR // 8) ** -0.5, 0.3125, ((0, 8),))
    second_gain = jnp.clip(1.0 + 0.15 * jax.random.normal(streams_of[13], (D,), jnp.float32), 0.25, 1.75)
    gate_weight = bell_draw(streams_of[14], (D, FF), D ** -0.5, 0.125, ((1, 8),))
    up_weight = bell_draw(streams_of[15], (D, FF), D ** -0.5, 0.125, ((1, 8),))
    down_weight = bell_draw(streams_of[16], (FF, D), (FF // 3) ** -0.5, 0.125, ((0, 8),))
    out_grad = bell_draw(streams_of[17], (TOKENS, D), 1.0, 6.0, ((0, 32),))
    return {"tokens": tokens, "lengths": lengths, "first_gain": first_gain, "branch_gate": branch_gate, "branch_input": branch_input, "conv_weight": conv_weight, "conv_bias": conv_bias, "rate_weight": rate_weight, "rate_bias": rate_bias, "inlet_weight": inlet_weight, "inlet_bias": inlet_bias, "decay_param": decay_param, "block_out": block_out, "second_gain": second_gain, "gate_weight": gate_weight, "up_weight": up_weight, "down_weight": down_weight, "out_grad": out_grad}


EPS = 1e-06
DECAY_SCALE = 8.0
HIGHEST = lax.Precision.HIGHEST

@jax.custom_vjp
def low(v):
    return lax.optimization_barrier(v.astype(jnp.bfloat16)).astype(jnp.float32)

@jax.custom_vjp
def low_back(v):
    return v

def low_keep(v):
    return (low(v), None)

def low_pass(kept, grad):
    return (grad,)

def back_keep(v):
    return (v, None)

def back_low(kept, grad):
    return (low(grad),)
low.defvjp(low_keep, low_pass)
low_back.defvjp(back_keep, back_low)

def root_norm(values, gain):
    return values * lax.rsqrt(lax.optimization_barrier(jnp.mean(values * values, axis=-1, keepdims=True)) + EPS) * gain

def sequence_positions(lengths_row, count):
    ends = jnp.cumsum(lengths_row).astype(jnp.int32)
    starts = ends - lengths_row.astype(jnp.int32)
    places = jnp.arange(count, dtype=jnp.int32)
    inside = places[:, None] >= starts[None, :]
    first = lax.optimization_barrier(jnp.max(jnp.where(inside, starts[None, :], 0), axis=1)).astype(jnp.int32)
    return places - first

def temporal_mix(input_pre, conv_weight, conv_bias, positions):
    total = conv_bias[None, :] + conv_weight[0][None, :] * input_pre
    for delay_steps in range(1, conv_weight.shape[0]):
        moved = jnp.pad(input_pre, ((delay_steps, 0), (0, 0)))[:-delay_steps]
        keep = (positions >= delay_steps)[:, None]
        total = total + jnp.where(keep, conv_weight[delay_steps][None, :] * moved, 0.0)
    return total

def combine_steps(early, late):
    return (early[0] * late[0], late[0] * early[1] + late[1])

def gated_recurrence(rate_pre, inlet_pre, conv_in, decay_param, positions):
    rate = jax.nn.sigmoid(rate_pre)
    inlet = jax.nn.sigmoid(inlet_pre)
    log_a = -DECAY_SCALE * rate * jax.nn.softplus(decay_param)[None, :]
    fresh = (positions == 0)[:, None]
    carry = jnp.where(fresh, 0.0, jnp.exp(log_a))
    scale = jnp.where(fresh, 1.0, jnp.sqrt(-jnp.expm1(2.0 * log_a)))
    drive = scale * inlet * conv_in
    return lax.associative_scan(combine_steps, (carry, drive), axis=0)[1]

def matrix(left, right):
    return jnp.dot(left, right, precision=HIGHEST)

def block_product(values, weights):
    rows = values.reshape(values.shape[0], weights.shape[0], weights.shape[1])
    mixed = jnp.einsum('thi,hij->thj', rows, weights, precision=HIGHEST)
    return mixed.reshape(values.shape[0], -1)

def bucket_forward(inputs, positions, params):
    first_gain, branch_gate, branch_input, conv_weight, conv_bias, rate_weight, rate_bias, inlet_weight, inlet_bias, decay_param, block_out, second_gain, gate_weight, up_weight, down_weight = params
    first_rows = low(root_norm(inputs, first_gain))
    gate_pre = low_back(matrix(first_rows, branch_gate))
    input_pre = low_back(matrix(first_rows, branch_input))
    conv_in = low(temporal_mix(input_pre, conv_weight, conv_bias, positions))
    rate_pre = low_back(block_product(conv_in, rate_weight) + rate_bias)
    inlet_pre = low_back(block_product(conv_in, inlet_weight) + inlet_bias)
    state = gated_recurrence(rate_pre, inlet_pre, conv_in, decay_param, positions)
    mixed = low(state * jax.nn.gelu(gate_pre))
    middle = inputs + low_back(matrix(mixed, block_out))
    second_rows = low(root_norm(middle, second_gain))
    gate_act = low_back(matrix(second_rows, gate_weight))
    up_act = low_back(matrix(second_rows, up_weight))
    hidden = low(jax.nn.gelu(gate_act) * up_act)
    return middle + low_back(matrix(hidden, down_weight))

def reference(tokens, lengths, first_gain, branch_gate, branch_input, conv_weight, conv_bias, rate_weight, rate_bias, inlet_weight, inlet_bias, decay_param, block_out, second_gain, gate_weight, up_weight, down_weight, out_grad):
    params = tuple((weight.astype(jnp.float32) for weight in (first_gain, branch_gate, branch_input, conv_weight, conv_bias, rate_weight, rate_bias, inlet_weight, inlet_bias, decay_param, block_out, second_gain, gate_weight, up_weight, down_weight)))
    inputs = tokens.astype(jnp.float32).reshape(NBUCKETS, BUCKET, D)
    cotangent = out_grad.astype(jnp.float32).reshape(NBUCKETS, BUCKET, D)

    def whole(inputs, params):

        def step(carry, item):
            rows, row_lengths = item
            positions = sequence_positions(row_lengths, BUCKET)
            return (carry, jax.checkpoint(bucket_forward)(rows, positions, params))
        return lax.scan(step, jnp.zeros((), jnp.float32), (inputs, lengths))[1]
    result, pull = jax.vjp(whole, inputs, params)
    input_grad, grads = pull(cotangent)
    output = result.astype(jnp.bfloat16).reshape(TOKENS, D)
    return (output, input_grad.reshape(TOKENS, D), grads[0], grads[1], grads[2], grads[3], grads[4], grads[5], grads[6], grads[7], grads[8], grads[9], grads[10], grads[11], grads[12], grads[13], grads[14])
```

```python
import jax
import jax.numpy as jnp
from jax import lax
from jax.experimental import pallas as pl
from jax.experimental.pallas import tpu as pltpu
from jax.sharding import PartitionSpec as P

EPS = 1e-06
DECAY_SCALE = 8.0
GELU_RATE = 0.7978845608028654
GELU_CUBE = 0.044715
CHUNK = 48
SUB = 8
LOW = jnp.bfloat16
WIDE = jnp.float32


def times(left, right):
    return jnp.dot(left, right, preferred_element_type=WIDE)


def times_transposed(left, right):
    return lax.dot_general(left, right, (((1,), (1,)), ((), ())), preferred_element_type=WIDE)


def transposed_times(left, right):
    return lax.dot_general(left, right, (((0,), (0,)), ((), ())), preferred_element_type=WIDE)


def gelu(v):
    return 0.5 * v * (1.0 + jnp.tanh(GELU_RATE * (v + GELU_CUBE * v * v * v)))


def gelu_pair(v):
    square = v * v
    bend = jnp.tanh(GELU_RATE * v * (1.0 + GELU_CUBE * square))
    half = 0.5 * (1.0 + bend)
    slope = half + 0.5 * v * (1.0 - bend * bend) * (GELU_RATE + 3.0 * GELU_RATE * GELU_CUBE * square)
    return v * half, slope


def norm_scale(values):
    return lax.rsqrt(jnp.mean(values * values, axis=-1, keepdims=True) + EPS)


def norm_back(values, scale, gain, grad):
    unit = values * scale
    lifted = gain * grad
    back = scale * (lifted - unit * jnp.mean(lifted * unit, axis=-1, keepdims=True))
    return back, jnp.sum(grad * unit, axis=0)


def one_minus_exp(y):
    series = 1.0 - y * (1.0 / 9.0)
    for order in range(8, 1, -1):
        series = 1.0 - y * (1.0 / order) * series
    return jnp.where(y < 0.5, y * series, 1.0 - jnp.exp(-y))


def row_positions(lengths_ref, base, rows, width):
    places = base + lax.broadcasted_iota(jnp.int32, (rows, width), 0)
    first = jnp.zeros_like(places)
    start = jnp.int32(0)
    for at in range(lengths_ref.shape[1] - 1):
        start = start + lengths_ref[0, at]
        first = jnp.where(places >= start, start, first)
    return places - first


def gates(rate, inlet, soft, fresh):
    log_a = -rate * soft
    carry = jnp.where(fresh, 0.0, jnp.exp(log_a))
    scale = jnp.where(fresh, 1.0, jnp.sqrt(one_minus_exp(-2.0 * log_a)))
    return carry, scale


def forward_kernel(
    lengths_ref, gate_ref, input_ref, taps_ref, rate_w_ref, inlet_w_ref, extra_ref,
    mixed_ref, conv_ref, rate_ref, inlet_ref, state_ref, padded_ref,
):
    count, width = input_ref.shape
    padded_ref[pl.ds(0, SUB), :] = jnp.zeros((SUB, width), WIDE)
    padded_ref[pl.ds(SUB, count), :] = input_ref[...]
    state_ref[pl.ds(0, SUB), :] = jnp.zeros((SUB, width), WIDE)
    taps = taps_ref[...]
    bias, rate_b, inlet_b, soft = (extra_ref[k : k + 1, :] for k in range(4))
    lanes = lax.broadcasted_iota(jnp.int32, (CHUNK, width), 0) % SUB

    def step(at, before):
        base = pl.multiple_of(at * CHUNK, SUB)
        pos = row_positions(lengths_ref, base, CHUNK, width)
        window = padded_ref[pl.ds(base, CHUNK + SUB), :]
        total = bias + taps[0:1] * window[SUB:]
        for k in range(1, taps.shape[0]):
            moved = window[SUB - k : SUB - k + CHUNK]
            total = total + jnp.where(pos >= k, taps[k : k + 1] * moved, 0.0)
        low = total.astype(LOW)
        conv_ref[pl.ds(base, CHUNK), :] = low
        rate = jax.nn.sigmoid(times(low, rate_w_ref[...]) + rate_b)
        inlet = jax.nn.sigmoid(times(low, inlet_w_ref[...]) + inlet_b)
        rate_ref[pl.ds(base, CHUNK), :] = rate
        inlet_ref[pl.ds(base, CHUNK), :] = inlet
        a, scale = gates(rate, inlet, soft, pos == 0)
        b = scale * inlet * low.astype(WIDE)
        for k in (1, 2, 4):
            inside = lanes >= k
            b = b + jnp.where(inside, a * pltpu.roll(b, k, 0), 0.0)
            a = jnp.where(inside, a * pltpu.roll(a, k, 0), a)
        tiles = []
        for j in range(CHUNK // SUB):
            part = slice(j * SUB, (j + 1) * SUB)
            tile = a[part] * before + b[part]
            before = tile[SUB - 1 : SUB]
            tiles.append(tile)
        state = jnp.concatenate(tiles, axis=0)
        state_ref[pl.ds(base + SUB, CHUNK), :] = state
        mixed_ref[pl.ds(base, CHUNK), :] = (state * gelu(gate_ref[pl.ds(base, CHUNK), :])).astype(LOW)
        return before

    lax.fori_loop(0, count // CHUNK, step, jnp.zeros((1, width), WIDE))


def backward_kernel(
    lengths_ref, grad_ref, gate_ref, input_ref, conv_ref, rate_ref, inlet_ref, state_ref,
    taps_ref, rate_w_ref, inlet_w_ref, extra_ref,
    gate_back_ref, input_back_ref, rate_w_grad_ref, inlet_w_grad_ref, small_ref,
    padded_ref, rate_low_ref, inlet_low_ref,
):
    count, width = input_ref.shape
    padded_ref[pl.ds(0, SUB), :] = jnp.zeros((SUB, width), WIDE)
    padded_ref[pl.ds(SUB, count), :] = input_ref[...]
    taps = taps_ref[...]
    soft = extra_ref[3:4, :]
    slope = extra_ref[4:5, :]
    lanes = lax.broadcasted_iota(jnp.int32, (CHUNK, width), 0) % SUB
    steps = count // CHUNK
    zero = jnp.zeros((1, width), WIDE)

    def column(values):
        return jnp.sum(values, axis=0, keepdims=True)

    def step(turn, held):
        after, late, beyond, sums = held
        base = pl.multiple_of((steps - 1 - turn) * CHUNK, SUB)
        here = pl.ds(base, CHUNK)
        wide_pos = row_positions(lengths_ref, base, CHUNK + SUB, width)
        pos = wide_pos[:CHUNK]
        fresh = pos == 0
        grad = grad_ref[here, :]
        value, bend = gelu_pair(gate_ref[here, :])
        window = state_ref[pl.ds(base, CHUNK + SUB), :]
        state = window[SUB:]
        earlier = window[SUB - 1 : SUB - 1 + CHUNK]
        gate_back_ref[here, :] = (grad * state * bend).astype(LOW)
        rate = rate_ref[here, :]
        inlet = inlet_ref[here, :]
        conv = conv_ref[here, :]
        conv_wide = conv.astype(WIDE)
        carry, scale = gates(rate, inlet, soft, fresh)
        b = grad * value
        a = jnp.concatenate([carry[1:], late], axis=0)
        for k in (1, 2, 4):
            inside = lanes < SUB - k
            b = b + jnp.where(inside, a * pltpu.roll(b, CHUNK - k, 0), 0.0)
            a = jnp.where(inside, a * pltpu.roll(a, CHUNK - k, 0), a)
        tiles = []
        for j in reversed(range(CHUNK // SUB)):
            part = slice(j * SUB, (j + 1) * SUB)
            tile = a[part] * after + b[part]
            after = tile[0:1]
            tiles.append(tile)
        total = jnp.concatenate(tiles[::-1], axis=0)
        late = carry[0:1]
        scaled = total * scale
        d_inlet = scaled * conv_wide
        d_scale = total * inlet * conv_wide
        d_log = jnp.where(fresh, 0.0, total * earlier * carry - d_scale * (carry * carry) / scale)
        leak = rate * d_log
        rate_low = (-soft * leak * (1.0 - rate)).astype(LOW)
        inlet_low = (d_inlet * inlet * (1.0 - inlet)).astype(LOW)
        rate_low_ref[here, :] = rate_low
        inlet_low_ref[here, :] = inlet_low
        spread = (
            scaled * inlet
            + times_transposed(rate_low, rate_w_ref[...])
            + times_transposed(inlet_low, inlet_w_ref[...])
        )
        ahead = jnp.concatenate([spread, beyond], axis=0)
        back = taps[0:1] * spread
        source = padded_ref[pl.ds(base, CHUNK + SUB), :]
        new = [column(spread), column(rate_low.astype(WIDE)), column(inlet_low.astype(WIDE)), column(leak)]
        new.append(column(spread * source[SUB:]))
        for k in range(1, taps.shape[0]):
            kept = jnp.where(wide_pos >= k, ahead, 0.0)
            back = back + taps[k : k + 1] * kept[k : k + CHUNK]
            new.append(column(kept[:CHUNK] * source[SUB - k : SUB - k + CHUNK]))
        input_back_ref[here, :] = back.astype(LOW)
        return after, late, spread[:SUB], tuple(x + y for x, y in zip(sums, new))

    start = tuple(zero for _ in range(4 + taps.shape[0]))
    sums = lax.fori_loop(0, steps, step, (zero, zero, jnp.zeros((SUB, width), WIDE), start))[3]
    rows = list(sums)
    rows[3] = -slope * rows[3]
    small_ref[...] = jnp.concatenate(rows, axis=0)
    rate_w_grad_ref[...] = transposed_times(conv_ref[...], rate_low_ref[...])
    inlet_w_grad_ref[...] = transposed_times(conv_ref[...], inlet_low_ref[...])


def in_vmem():
    return pl.BlockSpec(memory_space=pltpu.VMEM)


def run_kernel(body, outs, scratch, operands, cost):
    return pl.pallas_call(
        body,
        in_specs=[pl.BlockSpec(memory_space=pltpu.SMEM)] + [in_vmem()] * (len(operands) - 1),
        out_specs=[in_vmem()] * len(outs),
        out_shape=outs,
        scratch_shapes=scratch,
        compiler_params=pltpu.CompilerParams(vmem_limit_bytes=48 * 1024 * 1024),
        cost_estimate=cost,
    )(*operands)


def forward_mix(lengths, gate_pre, input_pre, taps, rate_w, inlet_w, extra):
    count, width = input_pre.shape
    wide = jax.ShapeDtypeStruct((count, width), WIDE)
    low = jax.ShapeDtypeStruct((count, width), LOW)
    state = jax.ShapeDtypeStruct((count + SUB, width), WIDE)
    cost = pl.CostEstimate(
        flops=60 * count * width + 4 * count * width * width,
        bytes_accessed=26 * count * width,
        transcendentals=5 * count * width,
    )
    return run_kernel(
        forward_kernel,
        [low, low, wide, wide, state],
        [pltpu.VMEM((count + SUB, width), WIDE)],
        (lengths, gate_pre, input_pre, taps, rate_w, inlet_w, extra),
        cost,
    )


def backward_mix(lengths, grad, gate_pre, input_pre, conv, rate, inlet, state, taps, rate_w, inlet_w, extra):
    count, width = input_pre.shape
    low = jax.ShapeDtypeStruct((count, width), LOW)
    square = jax.ShapeDtypeStruct((width, width), WIDE)
    small = jax.ShapeDtypeStruct((4 + taps.shape[0], width), WIDE)
    cost = pl.CostEstimate(
        flops=150 * count * width + 8 * count * width * width,
        bytes_accessed=30 * count * width,
        transcendentals=5 * count * width,
    )
    padded = pltpu.VMEM((count + SUB, width), WIDE)
    narrow = pltpu.VMEM((count, width), LOW)
    return run_kernel(
        backward_kernel,
        [low, low, square, square, small],
        [padded, narrow, narrow],
        (lengths, grad, gate_pre, input_pre, conv, rate, inlet, state, taps, rate_w, inlet_w, extra),
        cost,
    )


def spread_blocks(weights):
    heads, size, _ = weights.shape
    full = jnp.zeros((heads, size, heads, size), weights.dtype)
    for h in range(heads):
        full = full.at[h, :, h, :].set(weights[h])
    return full.reshape(heads * size, heads * size)


def pick_blocks(full, heads):
    size = full.shape[0] // heads
    return jnp.stack([full[h * size : (h + 1) * size, h * size : (h + 1) * size] for h in range(heads)])


def sum_rows(values):
    return lax.psum_scatter(values.astype(LOW), "mp", scatter_dimension=0, tiled=True).astype(WIDE)


def all_rows(values):
    return lax.all_gather(values, "mp", axis=0, tiled=True)


def sum_buckets(values):
    return lax.psum(values.astype(LOW), "dp").astype(WIDE)


def local(
    tokens,
    lengths,
    first_gain,
    branch_gate,
    branch_input,
    conv_weight,
    conv_bias,
    rate_weight,
    rate_bias,
    inlet_weight,
    inlet_bias,
    decay_param,
    block_out,
    second_gain,
    gate_weight,
    up_weight,
    down_weight,
    out_grad,
):
    heads = rate_weight.shape[0]
    width = decay_param.shape[0]
    features = tokens.shape[1]
    taps_count = conv_weight.shape[0]
    own_input = tokens.astype(WIDE)
    own_grad = out_grad.astype(WIDE)
    first_scale = norm_scale(own_input)
    first_rows = all_rows((own_input * first_scale * first_gain).astype(LOW))
    grad_rows = all_rows(out_grad)
    soft = DECAY_SCALE * jax.nn.softplus(decay_param)
    slope = DECAY_SCALE * jax.nn.sigmoid(decay_param)
    extra = jnp.stack([conv_bias, rate_bias, inlet_bias, soft, slope])
    rate_w = spread_blocks(rate_weight)
    inlet_w = spread_blocks(inlet_weight)

    gate_pre = times(first_rows, branch_gate)
    input_pre = times(first_rows, branch_input)
    mixed, conv, rate, inlet, state = forward_mix(
        lengths, gate_pre, input_pre, conv_weight, rate_w, inlet_w, extra
    )
    own_middle = own_input + sum_rows(times(mixed, block_out))
    second_scale = norm_scale(own_middle)
    second_rows = all_rows((own_middle * second_scale * second_gain).astype(LOW))
    d_hidden = times_transposed(grad_rows, down_weight)
    gate_act = times(second_rows, gate_weight)
    up_act = times(second_rows, up_weight)
    value, bend = gelu_pair(gate_act)
    hidden = (value * up_act).astype(LOW)
    gate_low = (d_hidden * up_act * bend).astype(LOW)
    up_low = (d_hidden * value).astype(LOW)
    second_input = sum_rows(times_transposed(gate_low, gate_weight) + times_transposed(up_low, up_weight))
    down_grad = transposed_times(hidden, grad_rows)
    gate_grad = transposed_times(second_rows, gate_low)
    up_grad = transposed_times(second_rows, up_low)
    part, second_gain_grad = norm_back(own_middle, second_scale, second_gain, second_input)
    middle_grad = own_grad + part
    middle_rows = all_rows(middle_grad.astype(LOW))
    d_mixed = times_transposed(middle_rows, block_out)
    block_grad = transposed_times(mixed, middle_rows)
    output = (own_middle + sum_rows(times(hidden, down_weight))).astype(LOW)
    gate_back, input_back, rate_w_grad, inlet_w_grad, small = backward_mix(
        lengths, d_mixed, gate_pre, input_pre, conv, rate, inlet, state, conv_weight, rate_w, inlet_w, extra
    )
    first_input = sum_rows(times_transposed(gate_back, branch_gate) + times_transposed(input_back, branch_input))
    branch_gate_grad = transposed_times(gate_back, first_rows)
    branch_input_grad = transposed_times(input_back, first_rows)
    part, first_gain_grad = norm_back(own_input, first_scale, first_gain, first_input)
    input_grad = middle_grad + part

    gains = lax.psum(jnp.stack([first_gain_grad, second_gain_grad]), ("dp", "mp"))
    mlp = sum_buckets(jnp.concatenate([down_grad.reshape(-1, features), gate_grad.reshape(-1, features), up_grad.reshape(-1, features)]))
    square = jnp.stack([pick_blocks(rate_w_grad, heads), pick_blocks(inlet_w_grad, heads)])
    flat = jnp.concatenate([square.reshape(-1), small.reshape(-1)])
    flat = jnp.pad(flat, (0, -flat.shape[0] % (16 * features))).reshape(-1, features)
    rec = sum_buckets(jnp.concatenate([block_grad, branch_gate_grad, branch_input_grad, flat]))
    hidden_count = down_weight.shape[0]
    down_grad = mlp[:hidden_count]
    gate_grad = mlp[hidden_count : 2 * hidden_count].reshape(features, -1)
    up_grad = mlp[2 * hidden_count :].reshape(features, -1)
    flat = rec[3 * width :].reshape(-1)
    square = flat[: square.size].reshape(square.shape)
    small = flat[square.size : square.size + small.size].reshape(small.shape)
    return (
        output,
        input_grad,
        gains[0],
        rec[width : 2 * width].T,
        rec[2 * width : 3 * width].T,
        small[4 : 4 + taps_count],
        small[0],
        square[0],
        small[1],
        square[1],
        small[2],
        small[3],
        rec[:width],
        gains[1],
        gate_grad,
        up_grad,
        down_grad,
    )


def solution(mesh):
    rows = P(("dp", "mp"), None)
    out_columns = P(None, "mp")
    out_rows = P("mp", None)
    blocks = P("mp", None, None)
    vector = P("mp")
    in_specs = (
        rows, P("dp", None), P(), out_columns, out_columns, out_columns, vector, blocks, vector, blocks,
        vector, vector, out_rows, P(), out_columns, out_columns, out_rows, rows,
    )
    out_specs = (
        rows, rows, P(), out_columns, out_columns, out_columns, vector, blocks, vector, blocks,
        vector, vector, out_rows, P(), out_columns, out_columns, out_rows,
    )
    return jax.shard_map(local, mesh=mesh, in_specs=in_specs, out_specs=out_specs, check_vma=False)
```

```python
import itertools

import jax
import jax.numpy as jnp
from jax import lax
from jax.experimental import pallas as pl
from jax.experimental.pallas import tpu as pltpu
from jax.sharding import PartitionSpec as P

EPS = 1e-06
DECAY_SCALE = 8.0
GELU_RATE = 0.7978845608028654
GELU_CUBE = 0.044715
CHUNK = 48
SUB = 8
LOW = jnp.bfloat16
WIDE = jnp.float32
NO_COST = pl.CostEstimate(flops=0, bytes_accessed=0, transcendentals=0)
ROWS = 256
COLUMNS = 512


def times(left, right):
    return jnp.dot(left, right, preferred_element_type=WIDE)


def times_transposed(left, right):
    return lax.dot_general(left, right, (((1,), (1,)), ((), ())), preferred_element_type=WIDE)


def transposed_times(left, right):
    return lax.dot_general(left, right, (((0,), (0,)), ((), ())), preferred_element_type=WIDE)


def gelu(v):
    return 0.5 * v * (1.0 + jnp.tanh(GELU_RATE * (v + GELU_CUBE * v * v * v)))


def gelu_pair(v):
    square = v * v
    bend = jnp.tanh(GELU_RATE * v * (1.0 + GELU_CUBE * square))
    half = 0.5 * (1.0 + bend)
    slope = half + 0.5 * v * (1.0 - bend * bend) * (GELU_RATE + 3.0 * GELU_RATE * GELU_CUBE * square)
    return v * half, slope


def norm_scale(values):
    return lax.rsqrt(jnp.mean(values * values, axis=-1, keepdims=True) + EPS)


def norm_back(values, scale, gain, grad):
    unit = values * scale
    lifted = gain * grad
    return scale * (lifted - unit * jnp.mean(lifted * unit, axis=-1, keepdims=True))


def one_minus_exp(y):
    series = 1.0 - y * (1.0 / 9.0)
    for order in range(8, 1, -1):
        series = 1.0 - y * (1.0 / order) * series
    return jnp.where(y < 0.5, y * series, 1.0 - jnp.exp(-y))


def row_positions(lengths_ref, base, rows, width):
    places = base + lax.broadcasted_iota(jnp.int32, (rows, width), 0)
    first = jnp.zeros_like(places)
    start = jnp.int32(0)
    for at in range(lengths_ref.shape[1] - 1):
        start = start + lengths_ref[0, at]
        first = jnp.where(places >= start, start, first)
    return places - first


def gates(rate, inlet, soft, fresh):
    log_a = -rate * soft
    carry = jnp.where(fresh, 0.0, jnp.exp(log_a))
    scale = jnp.where(fresh, 1.0, jnp.sqrt(one_minus_exp(-2.0 * log_a)))
    return carry, scale


def forward_kernel(
    lengths_ref, both_ref, taps_ref, rate_w_ref, inlet_w_ref, extra_ref,
    mixed_ref, conv_ref, rate_ref, inlet_ref, state_ref, padded_ref,
):
    count, width = mixed_ref.shape
    padded_ref[pl.ds(0, SUB), :] = jnp.zeros((SUB, width), WIDE)
    padded_ref[pl.ds(SUB, count), :] = both_ref[:, width:]
    state_ref[pl.ds(0, SUB), :] = jnp.zeros((SUB, width), WIDE)
    taps = taps_ref[...]
    bias, rate_b, inlet_b, soft = (extra_ref[k : k + 1, :] for k in range(4))
    lanes = lax.broadcasted_iota(jnp.int32, (CHUNK, width), 0) % SUB

    def step(at, before):
        base = pl.multiple_of(at * CHUNK, SUB)
        pos = row_positions(lengths_ref, base, CHUNK, width)
        window = padded_ref[pl.ds(base, CHUNK + SUB), :]
        total = bias + taps[0:1] * window[SUB:]
        for k in range(1, taps.shape[0]):
            moved = window[SUB - k : SUB - k + CHUNK]
            total = total + jnp.where(pos >= k, taps[k : k + 1] * moved, 0.0)
        low = total.astype(LOW)
        conv_ref[pl.ds(base, CHUNK), :] = low
        rate = jax.nn.sigmoid(times(low, rate_w_ref[...]) + rate_b)
        inlet = jax.nn.sigmoid(times(low, inlet_w_ref[...]) + inlet_b)
        rate_ref[pl.ds(base, CHUNK), :] = rate
        inlet_ref[pl.ds(base, CHUNK), :] = inlet
        a, scale = gates(rate, inlet, soft, pos == 0)
        b = scale * inlet * low.astype(WIDE)
        for k in (1, 2, 4):
            inside = lanes >= k
            b = b + jnp.where(inside, a * pltpu.roll(b, k, 0), 0.0)
            a = jnp.where(inside, a * pltpu.roll(a, k, 0), a)
        tiles = []
        for j in range(CHUNK // SUB):
            part = slice(j * SUB, (j + 1) * SUB)
            tile = a[part] * before + b[part]
            before = tile[SUB - 1 : SUB]
            tiles.append(tile)
        state = jnp.concatenate(tiles, axis=0)
        state_ref[pl.ds(base + SUB, CHUNK), :] = state
        mixed_ref[pl.ds(base, CHUNK), :] = (state * gelu(both_ref[pl.ds(base, CHUNK), :width])).astype(LOW)
        return before

    lax.fori_loop(0, count // CHUNK, step, jnp.zeros((1, width), WIDE))


def backward_kernel(
    heads, lengths_ref, middle_ref, block_ref, first_ref, branches_ref, mixed_ref,
    both_ref, conv_ref, rate_ref, inlet_ref, state_ref,
    taps_ref, rate_w_ref, inlet_w_ref, extra_ref,
    partial_ref, block_grad_ref, branch_grad_ref, gain_ref,
    grad_ref, back_ref, padded_ref, rate_low_ref, inlet_low_ref, stacked_ref,
):
    count, width = grad_ref.shape
    features = middle_ref.shape[1]

    def spread_rows(turn, _):
        here = pl.ds(pl.multiple_of(turn * ROWS, ROWS), ROWS)
        grad_ref[here, :] = times_transposed(middle_ref[here, :], block_ref[...])
        return _

    lax.fori_loop(0, count // ROWS, spread_rows, 0)
    padded_ref[pl.ds(0, SUB), :] = jnp.zeros((SUB, width), WIDE)
    padded_ref[pl.ds(SUB, count), :] = both_ref[:, width:]
    taps = taps_ref[...]
    soft = extra_ref[3:4, :]
    slope = extra_ref[4:5, :]
    lanes = lax.broadcasted_iota(jnp.int32, (CHUNK, width), 0) % SUB
    steps = count // CHUNK
    zero = jnp.zeros((1, width), WIDE)

    def column(values):
        return jnp.sum(values, axis=0, keepdims=True)

    def step(turn, held):
        after, late, beyond, sums = held
        base = pl.multiple_of((steps - 1 - turn) * CHUNK, SUB)
        here = pl.ds(base, CHUNK)
        wide_pos = row_positions(lengths_ref, base, CHUNK + SUB, width)
        pos = wide_pos[:CHUNK]
        fresh = pos == 0
        grad = grad_ref[here, :]
        value, bend = gelu_pair(both_ref[here, :width])
        window = state_ref[pl.ds(base, CHUNK + SUB), :]
        state = window[SUB:]
        earlier = window[SUB - 1 : SUB - 1 + CHUNK]
        back_ref[here, :width] = (grad * state * bend).astype(LOW)
        rate = rate_ref[here, :]
        inlet = inlet_ref[here, :]
        conv = conv_ref[here, :]
        conv_wide = conv.astype(WIDE)
        carry, scale = gates(rate, inlet, soft, fresh)
        b = grad * value
        a = jnp.concatenate([carry[1:], late], axis=0)
        for k in (1, 2, 4):
            inside = lanes < SUB - k
            b = b + jnp.where(inside, a * pltpu.roll(b, CHUNK - k, 0), 0.0)
            a = jnp.where(inside, a * pltpu.roll(a, CHUNK - k, 0), a)
        tiles = []
        for j in reversed(range(CHUNK // SUB)):
            part = slice(j * SUB, (j + 1) * SUB)
            tile = a[part] * after + b[part]
            after = tile[0:1]
            tiles.append(tile)
        total = jnp.concatenate(tiles[::-1], axis=0)
        late = carry[0:1]
        scaled = total * scale
        d_inlet = scaled * conv_wide
        d_scale = total * inlet * conv_wide
        d_log = jnp.where(fresh, 0.0, total * earlier * carry - d_scale * (carry * carry) / scale)
        leak = rate * d_log
        rate_low = (-soft * leak * (1.0 - rate)).astype(LOW)
        inlet_low = (d_inlet * inlet * (1.0 - inlet)).astype(LOW)
        rate_low_ref[here, :] = rate_low
        inlet_low_ref[here, :] = inlet_low
        spread = (
            scaled * inlet
            + times_transposed(rate_low, rate_w_ref[...])
            + times_transposed(inlet_low, inlet_w_ref[...])
        )
        ahead = jnp.concatenate([spread, beyond], axis=0)
        back = taps[0:1] * spread
        source = padded_ref[pl.ds(base, CHUNK + SUB), :]
        new = [column(spread), column(rate_low.astype(WIDE)), column(inlet_low.astype(WIDE)), column(leak)]
        new.append(column(spread * source[SUB:]))
        for k in range(1, taps.shape[0]):
            kept = jnp.where(wide_pos >= k, ahead, 0.0)
            back = back + taps[k : k + 1] * kept[k : k + CHUNK]
            new.append(column(kept[:CHUNK] * source[SUB - k : SUB - k + CHUNK]))
        back_ref[here, width:] = back.astype(LOW)
        return after, late, spread[:SUB], tuple(x + y for x, y in zip(sums, new))

    start = tuple(zero for _ in range(4 + taps.shape[0]))
    sums = lax.fori_loop(0, steps, step, (zero, zero, jnp.zeros((SUB, width), WIDE), start))[3]
    rows = list(sums)
    rows[3] = -slope * rows[3]
    def spread_columns(turn, _):
        here = pl.ds(pl.multiple_of(turn * COLUMNS, COLUMNS), COLUMNS)
        block_grad_ref[:width, here] = transposed_times(mixed_ref[...], middle_ref[:, here]).astype(LOW)
        branch_grad = transposed_times(back_ref[...], first_ref[:, here])
        branch_grad_ref[:, here] = branch_grad.astype(LOW)
        gain_ref[:, here] = column(branch_grad * branches_ref[:, here].astype(WIDE))
        partial_ref[:, here] = times(back_ref[...], branches_ref[:, here]).astype(LOW)
        return _

    lax.fori_loop(0, features // COLUMNS, spread_columns, 0)
    size = width // heads
    strips, depth = strip_shape(features, heads, size, len(rows))
    stacked_ref[...] = jnp.zeros_like(stacked_ref)
    block = 0
    for low_ref in (rate_low_ref, inlet_low_ref):
        full = transposed_times(conv_ref[...], low_ref[...])
        for h in range(heads):
            part = slice(h * size, (h + 1) * size)
            stacked_ref[pl.ds(block * size, size), :] = full[part, part]
            block += 1
    small = jnp.concatenate(rows, axis=0)
    for h in range(heads):
        stacked_ref[pl.ds(block * size + h * SUB, len(rows)), :] = small[:, h * size : (h + 1) * size]
    block_grad_ref[pl.ds(width, depth), :] = jnp.zeros((depth, features), LOW)
    for k in range(strips):
        block_grad_ref[pl.ds(width, depth), k * size : (k + 1) * size] = stacked_ref[pl.ds(k * depth, depth), :].astype(LOW)


def strip_shape(features, heads, size, small):
    strips = features // size
    rows = 2 * heads * size + heads * SUB
    return strips, -(-rows // (strips * 2 * SUB)) * 2 * SUB


def unpack_strips(packed, heads, size, small):
    strips, depth = strip_shape(packed.shape[1], heads, size, small)
    stacked = jnp.concatenate([packed[:, k * size : (k + 1) * size] for k in range(strips)])
    square = stacked[: 2 * heads * size].reshape(2, heads, size, size)
    parts = [stacked[2 * heads * size + h * SUB :][:small] for h in range(heads)]
    return square, jnp.concatenate(parts, axis=1)


def in_vmem():
    return pl.BlockSpec(memory_space=pltpu.VMEM)


def run_kernel(body, outs, scratch, operands, room):
    return pl.pallas_call(
        body,
        in_specs=[pl.BlockSpec(memory_space=pltpu.SMEM)] + [in_vmem()] * (len(operands) - 1),
        out_specs=[in_vmem()] * len(outs),
        out_shape=outs,
        scratch_shapes=scratch,
        compiler_params=pltpu.CompilerParams(vmem_limit_bytes=room * 1024 * 1024),
        cost_estimate=NO_COST,
    )(*operands)


def forward_mix(lengths, both, taps, rate_w, inlet_w, extra):
    count, width = both.shape[0], both.shape[1] // 2
    wide = jax.ShapeDtypeStruct((count, width), WIDE)
    low = jax.ShapeDtypeStruct((count, width), LOW)
    state = jax.ShapeDtypeStruct((count + SUB, width), WIDE)
    return run_kernel(
        forward_kernel,
        [low, low, wide, wide, state],
        [pltpu.VMEM((count + SUB, width), WIDE)],
        (lengths, both, taps, rate_w, inlet_w, extra),
        20,
    )


def backward_mix(heads, lengths, middle, block, first, branches, mixed, both, conv, *others):
    count, width = mixed.shape
    features = middle.shape[1]
    narrow = pltpu.VMEM((count, width), LOW)
    size = width // heads
    strips, depth = strip_shape(features, heads, size, SUB)
    return run_kernel(
        lambda *refs: backward_kernel(heads, *refs),
        [
            jax.ShapeDtypeStruct((count, features), LOW),
            jax.ShapeDtypeStruct((width + depth, features), LOW),
            jax.ShapeDtypeStruct((2 * width, features), LOW),
            jax.ShapeDtypeStruct((1, features), WIDE),
        ],
        [
            pltpu.VMEM((count, width), WIDE),
            pltpu.VMEM((count, 2 * width), LOW),
            pltpu.VMEM((count + SUB, width), WIDE),
            narrow,
            narrow,
            pltpu.VMEM((strips * depth, size), WIDE),
        ],
        (lengths, middle, block, first, branches, mixed, both, conv) + others,
        44,
    )


def spread_blocks(weights):
    heads, size, _ = weights.shape
    full = jnp.zeros((heads, size, heads, size), weights.dtype)
    for h in range(heads):
        full = full.at[h, :, h, :].set(weights[h])
    return full.reshape(heads * size, heads * size)


def sum_rows(values):
    return lax.psum_scatter(values.astype(LOW), "mp", scatter_dimension=0, tiled=True).astype(WIDE)


def all_rows(values):
    return lax.all_gather(values, "mp", axis=0, tiled=True)


def place_kernel(pieces, kept, splits, where_ref, *refs):
    out_refs = refs[pieces + kept :]
    for k in range(pieces):

        @pl.when(pl.program_id(0) == k)
        def _():
            start = 0
            for out_ref, rows in zip(out_refs, splits):
                out_ref[...] = refs[k][pl.ds(start, rows), :].astype(out_ref.dtype)
                start += rows


def place(pieces, spots, total, axis, splits, kind, onto=()):
    count = len(pieces)
    rows, columns = pieces[0].shape
    splits = splits or (rows,)
    outs = [
        jax.ShapeDtypeStruct((r * total, columns) if axis == 0 else (r, columns * total), kind) for r in splits
    ]
    spot = (lambda k, at: (at[k], 0)) if axis == 0 else (lambda k, at: (0, at[k]))
    room = rows * columns * (2 * 2 * count + 4 * 2) + 4 * 1024 * 1024
    return pl.pallas_call(
        lambda *refs: place_kernel(count, len(onto), splits, *refs),
        grid_spec=pltpu.PrefetchScalarGridSpec(
            num_scalar_prefetch=1,
            grid=(count,),
            in_specs=[pl.BlockSpec((rows, columns), lambda k, at: (0, 0))] * count
            + [pl.BlockSpec(memory_space=pl.ANY)] * len(onto),
            out_specs=[pl.BlockSpec((r, columns), spot) for r in splits],
        ),
        out_shape=outs,
        input_output_aliases={1 + count + k: k for k in range(len(onto))},
        compiler_params=pltpu.CompilerParams(vmem_limit_bytes=room),
        cost_estimate=NO_COST,
    )(jnp.stack(spots).astype(jnp.int32), *pieces, *onto)


def halves(values, axis):
    size = values.shape[axis] // 2
    return lax.slice_in_dim(values, 0, size, axis=axis), lax.slice_in_dim(values, size, 2 * size, axis=axis)


def dp_bits():
    return lax.axis_size("dp").bit_length() - 1


def swap(values, bit):
    count = lax.axis_size("dp")
    return lax.ppermute(values, "dp", [(i, i ^ (1 << bit)) for i in range(count)])


def order_of(turn):
    bits = dp_bits()
    return [(turn + k) % bits for k in range(bits)]


def split_for(values, axis, bit):
    first, second = halves(values, axis)
    upper = ((lax.axis_index("dp") >> bit) & 1) == 1
    return jnp.where(upper, first, second), jnp.where(upper, second, first)


def join(kept, got):
    return (kept.astype(WIDE) + got.astype(WIDE)).astype(LOW)


class Part:
    def __init__(self, values, axis, turn):
        self.axis, self.order = axis, order_of(turn)
        self.step = 0
        self.load(values)

    def load(self, values):
        if self.step < len(self.order):
            self.send, self.kept = split_for(values, self.axis, self.order[self.step])
        else:
            self.pieces = {0: values}

    def reduce(self):
        return swap(self.send, self.order[self.step])

    def land(self, got):
        self.step += 1
        self.load(join(self.kept, got))

    def forwards(self, level):
        made = []
        for chosen in itertools.combinations(reversed(self.order), level):
            made.append((sum(1 << bit for bit in chosen[:-1]), chosen[-1]))
        return made

    def spot(self, mask):
        owner = lax.axis_index("dp") ^ mask
        bits = len(self.order)
        return sum(((owner >> self.order[k]) & 1) << (bits - 1 - k) for k in range(bits))


def start_gather(parts, level):
    return [(part, mask ^ (1 << bit), swap(part.pieces[mask], bit)) for part in parts for mask, bit in part.forwards(level)]


def exchange(reducing=(), gathered=(), extras=()):
    gots = [part.reduce() for part in reducing]
    made = lax.optimization_barrier((*gots, *[piece for _, _, piece in gathered], *extras))
    for part, got in zip(reducing, made):
        part.land(got)
    for (part, mask, _), piece in zip(gathered, made[len(gots) :]):
        part.pieces[mask] = piece
    return made[len(gots) + len(gathered) :]


def reduce_fully(parts):
    while parts[0].step < len(parts[0].order):
        exchange(parts)


def gather_fully(parts, level):
    for more in range(level, dp_bits() + 1):
        exchange(gathered=start_gather(parts, more))


def finish(parts, axis, splits=None, masks=None, onto=()):
    count = 1 << dp_bits()
    chosen = [(turn, mask) for turn, part in enumerate(parts) for mask in part.pieces if masks is None or mask in masks]
    spots = [parts[turn].spot(mask) + turn * count for turn, mask in chosen]
    blocks = [parts[turn].pieces[mask] for turn, mask in chosen]
    return place(blocks, spots, len(parts) * count, axis, splits, WIDE, onto)


def column_parts(values):
    return [Part(half, 1, turn) for turn, half in enumerate(halves(values, 1))]


def shifts_of(values, axis, shifts):
    count = lax.axis_size(axis)
    return [lax.ppermute(values, axis, [(i, (i + shift) % count) for i in range(count)]) for shift in shifts]


def tie(values, *others):
    return lax.optimization_barrier((values,) + others)[0]


def local(
    tokens,
    lengths,
    first_gain,
    branch_gate,
    branch_input,
    conv_weight,
    conv_bias,
    rate_weight,
    rate_bias,
    inlet_weight,
    inlet_bias,
    decay_param,
    block_out,
    second_gain,
    gate_weight,
    up_weight,
    down_weight,
    out_grad,
):
    heads = rate_weight.shape[0]
    width = decay_param.shape[0]
    features = tokens.shape[1]
    taps_count = conv_weight.shape[0]
    own_input = tokens.astype(WIDE)
    own_grad = out_grad.astype(WIDE)
    first_scale = norm_scale(own_input)
    first_rows = all_rows((own_input * first_scale * first_gain).astype(LOW))
    soft = DECAY_SCALE * jax.nn.softplus(decay_param)
    slope = DECAY_SCALE * jax.nn.sigmoid(decay_param)
    extra = jnp.stack([conv_bias, rate_bias, inlet_bias, soft, slope])
    rate_w = spread_blocks(rate_weight)
    inlet_w = spread_blocks(inlet_weight)
    branches = jnp.concatenate([branch_gate.T, branch_input.T])

    first_rows = tie(first_rows, rate_w, inlet_w, extra, branches)
    both = times_transposed(first_rows, branches)
    grad_rows = all_rows(tie(out_grad, first_rows))
    mixed, conv, rate, inlet, state = forward_mix(lengths, both, conv_weight, rate_w, inlet_w, extra)
    block_partial = tie(times(mixed, block_out), grad_rows)
    own_middle = own_input + sum_rows(block_partial)
    second_scale = norm_scale(own_middle)
    second_rows = all_rows((own_middle * second_scale * second_gain).astype(LOW))
    d_hidden = times_transposed(grad_rows, down_weight)
    second_rows, d_hidden = lax.optimization_barrier((second_rows, d_hidden))
    gate_act = times(second_rows, gate_weight)
    up_act = times(second_rows, up_weight)
    value, bend = gelu_pair(gate_act)
    hidden = (value * up_act).astype(LOW)
    gate_low = (d_hidden * up_act * bend).astype(LOW)
    up_low = (d_hidden * value).astype(LOW)

    down_parts = column_parts(transposed_times(hidden, grad_rows).astype(LOW))
    late_gate = tie(gate_low, *[part.send for part in down_parts])
    second_input = sum_rows(times_transposed(late_gate, gate_weight) + times_transposed(up_low, up_weight))
    gate_part = Part(transposed_times(second_rows, gate_low).astype(LOW), 0, 0)
    up_part = Part(transposed_times(second_rows, up_low).astype(LOW), 0, 1)
    wide_parts = [gate_part, up_part]
    mlp = down_parts + wide_parts

    exchange(down_parts)
    (second_input,) = exchange(down_parts + wide_parts, extras=(second_input,))
    middle_grad = own_grad + norm_back(own_middle, second_scale, second_gain, second_input)
    second_gain_grad = jnp.sum(second_input * own_middle * second_scale, axis=0)
    middle_rows = all_rows(middle_grad.astype(LOW))

    reduce_fully(down_parts)
    out_partial = times(tie(hidden, second_input), down_weight)
    middle_rows, out_partial = exchange(wide_parts, start_gather(down_parts, 1), (middle_rows, out_partial))
    out_sum = sum_rows(out_partial)

    reduce_fully(wide_parts)
    made = backward_mix(
        heads, lengths, middle_rows, block_out, first_rows, branches, mixed,
        both, conv, rate, inlet, state, conv_weight, rate_w, inlet_w, extra,
    )
    first_partial, block_grad, branch_grad, gain = exchange(gathered=start_gather(wide_parts, 1), extras=made)
    first_input = sum_rows(tie(first_partial, out_sum))
    output = (own_middle + out_sum).astype(LOW)
    gains = jnp.concatenate([gain / first_gain, second_gain_grad[None]])

    branch_parts = column_parts(branch_grad)
    block_parts = column_parts(block_grad)
    late = branch_parts + block_parts
    wide_rest = start_gather(wide_parts, 2)
    cores = lax.axis_size("mp")
    (other,) = exchange(late, extras=[lax.ppermute(gains, "mp", [(i, i ^ 1) for i in range(cores)])])
    gains = gains + other
    others = shifts_of(gains, "mp", range(2, cores, 2))
    down_rest = start_gather(down_parts, 2)
    first_input, output, *others = exchange(late, wide_rest + down_rest, (first_input, output, *others))
    gather_fully(mlp, 3)
    reduce_fully(late)
    gains = gains + sum(others)
    others = shifts_of(gains, "dp", range(1, lax.axis_size("dp")))
    input_grad = middle_grad + norm_back(own_input, first_scale, first_gain, first_input)
    (gate_grad,) = finish([gate_part], 0)
    (up_grad,) = finish([up_part], 0)
    (down_grad,) = finish(down_parts, 1)
    made = exchange(gathered=start_gather(late, 1), extras=(gate_grad, up_grad, down_grad, input_grad, *others))
    gate_grad, up_grad, down_grad, input_grad = made[:4]
    gains = gains + sum(made[4:])
    own = [0] + [1 << bit for bit in range(dp_bits())]
    depth = block_grad.shape[0] - width
    halfway = finish(branch_parts, 1, (width, width), own)
    block_halfway = finish(block_parts, 1, (width, depth), own)
    made = exchange(gathered=start_gather(late, 2), extras=(gains, *halfway, *block_halfway))
    gather_fully(late, 3)
    gains = made[0]
    rest = [mask for mask in branch_parts[0].pieces if mask not in own]
    branch_gate_grad, branch_input_grad = finish(branch_parts, 1, (width, width), rest, made[1:3])
    block_grad, packed = finish(block_parts, 1, (width, depth), rest, made[3:5])
    square, small = unpack_strips(packed, heads, width // heads, 4 + taps_count)
    return (
        output,
        input_grad,
        gains[0],
        branch_gate_grad.T,
        branch_input_grad.T,
        small[4 : 4 + taps_count],
        small[0],
        square[0],
        small[1],
        square[1],
        small[2],
        small[3],
        block_grad,
        gains[1],
        gate_grad,
        up_grad,
        down_grad,
    )


def solution(mesh):
    rows = P(("dp", "mp"), None)
    out_columns = P(None, "mp")
    out_rows = P("mp", None)
    blocks = P("mp", None, None)
    vector = P("mp")
    in_specs = (
        rows, P("dp", None), P(), out_columns, out_columns, out_columns, vector, blocks, vector, blocks,
        vector, vector, out_rows, P(), out_columns, out_columns, out_rows, rows,
    )
    out_specs = (
        rows, rows, P(), out_columns, out_columns, out_columns, vector, blocks, vector, blocks,
        vector, vector, out_rows, P(), out_columns, out_columns, out_rows,
    )
    return jax.shard_map(local, mesh=mesh, in_specs=in_specs, out_specs=out_specs, check_vma=False)
```

```python
import itertools

import jax
import jax.numpy as jnp
from jax import lax
from jax.experimental import pallas as pl
from jax.experimental.pallas import tpu as pltpu
from jax.sharding import PartitionSpec as P

EPS = 1e-06
DECAY_SCALE = 8.0
GELU_RATE = 0.7978845608028654
GELU_CUBE = 0.044715
CHUNK = 48
SUB = 8
LOW = jnp.bfloat16
WIDE = jnp.float32
NO_COST = pl.CostEstimate(flops=0, bytes_accessed=0, transcendentals=0)
ROWS = 256
SPARE = 16
ROOM = 60
TILE = 512
LOAD = 192


def times(left, right):
    return jnp.dot(left, right, preferred_element_type=WIDE)


def times_transposed(left, right):
    return lax.dot_general(left, right, (((1,), (1,)), ((), ())), preferred_element_type=WIDE)


def transposed_times(left, right):
    return lax.dot_general(left, right, (((0,), (0,)), ((), ())), preferred_element_type=WIDE)


def gelu(v):
    return 0.5 * v * (1.0 + jnp.tanh(GELU_RATE * (v + GELU_CUBE * v * v * v)))


def gelu_pair(v):
    square = v * v
    bend = jnp.tanh(GELU_RATE * v * (1.0 + GELU_CUBE * square))
    half = 0.5 * (1.0 + bend)
    slope = half + 0.5 * v * (1.0 - bend * bend) * (GELU_RATE + 3.0 * GELU_RATE * GELU_CUBE * square)
    return v * half, slope


def norm_scale(values):
    return lax.rsqrt(jnp.mean(values * values, axis=-1, keepdims=True) + EPS)


def norm_back(values, scale, gain, grad):
    unit = values * scale
    lifted = gain * grad
    return scale * (lifted - unit * jnp.mean(lifted * unit, axis=-1, keepdims=True))


def one_minus_exp(y):
    series = 1.0 - y * (1.0 / 9.0)
    for order in range(8, 1, -1):
        series = 1.0 - y * (1.0 / order) * series
    return jnp.where(y < 0.5, y * series, 1.0 - jnp.exp(-y))


def row_positions(scalars_ref, base, rows, width):
    places = base + lax.broadcasted_iota(jnp.int32, (rows, width), 0)
    first = jnp.zeros_like(places)
    start = jnp.int32(0)
    for at in range(4, scalars_ref.shape[1] - 1):
        start = start + scalars_ref[0, at]
        first = jnp.where(places >= start, start, first)
    return places - first


def gates(rate, inlet, soft, fresh):
    log_a = -rate * soft
    carry = jnp.where(fresh, 0.0, jnp.exp(log_a))
    scale = jnp.where(fresh, 1.0, jnp.sqrt(one_minus_exp(-2.0 * log_a)))
    return carry, scale


def forward_kernel(scalars_ref, *refs):
    sources, (taps_ref, rate_w_ref, inlet_w_ref, extra_ref), refs = refs[:3], refs[3:7], refs[7:]
    out_refs, refs = refs[:7], refs[7:]
    first_ref, branches_ref, block_ref = refs[:3]
    partial_ref, mixed_ref, conv_ref, rate_ref, inlet_ref, state_ref, both_ref = refs[3:10]
    padded_ref, in_sems, out_sems = refs[10:]
    count, width = mixed_ref.shape
    features = first_ref.shape[1]
    pieces = count // LOAD
    arrivals = [
        pltpu.make_async_copy(sources[1], branches_ref, in_sems.at[pieces]),
        *[
            pltpu.make_async_copy(sources[0].at[pl.ds(k * LOAD, LOAD), :], first_ref.at[pl.ds(k * LOAD, LOAD), :], in_sems.at[k])
            for k in range(pieces)
        ],
        pltpu.make_async_copy(sources[2], block_ref, in_sems.at[pieces + 1]),
    ]
    for arrival in arrivals:
        arrival.start()
    arrivals[0].wait()
    for k in range(pieces):
        arrivals[1 + k].wait()
        here = pl.ds(k * LOAD, LOAD)
        both_ref[here, :] = times_transposed(first_ref[here, :], branches_ref[...])
    departures = [pltpu.make_async_copy(both_ref, out_refs[6], out_sems.at[0])]
    departures[0].start()

    padded_ref[pl.ds(0, SUB), :] = jnp.zeros((SUB, width), WIDE)
    padded_ref[pl.ds(SUB, count), :] = both_ref[:, width:]
    state_ref[pl.ds(0, SUB), :] = jnp.zeros((SUB, width), WIDE)
    taps = taps_ref[...]
    bias, rate_b, inlet_b, soft = (extra_ref[k : k + 1, :] for k in range(4))
    lanes = lax.broadcasted_iota(jnp.int32, (CHUNK, width), 0) % SUB

    def convolve(at, _):
        base = pl.multiple_of(at * CHUNK, SUB)
        pos = row_positions(scalars_ref, base, CHUNK, width)
        window = padded_ref[pl.ds(base, CHUNK + SUB), :]
        total = bias + taps[0:1] * window[SUB:]
        for k in range(1, taps.shape[0]):
            moved = window[SUB - k : SUB - k + CHUNK]
            total = total + jnp.where(pos >= k, taps[k : k + 1] * moved, 0.0)
        conv_ref[pl.ds(base, CHUNK), :] = total.astype(LOW)
        return _

    lax.fori_loop(0, count // CHUNK, convolve, 0)

    def open_gates(at, _):
        here = pl.ds(pl.multiple_of(at * ROWS, ROWS), ROWS)
        rate_ref[here, :] = jax.nn.sigmoid(times(conv_ref[here, :], rate_w_ref[...]) + rate_b)
        inlet_ref[here, :] = jax.nn.sigmoid(times(conv_ref[here, :], inlet_w_ref[...]) + inlet_b)
        return _

    lax.fori_loop(0, count // ROWS, open_gates, 0)
    for k, (ref, out_ref) in enumerate(((conv_ref, out_refs[2]), (rate_ref, out_refs[3]), (inlet_ref, out_refs[4]))):
        departures.append(pltpu.make_async_copy(ref, out_ref, out_sems.at[1 + k]))
        departures[-1].start()

    def step(at, before):
        base = pl.multiple_of(at * CHUNK, SUB)
        here = pl.ds(base, CHUNK)
        pos = row_positions(scalars_ref, base, CHUNK, width)
        a, scale = gates(rate_ref[here, :], inlet_ref[here, :], soft, pos == 0)
        b = scale * inlet_ref[here, :] * conv_ref[here, :].astype(WIDE)
        for k in (1, 2, 4):
            inside = lanes >= k
            b = b + jnp.where(inside, a * pltpu.roll(b, k, 0), 0.0)
            a = jnp.where(inside, a * pltpu.roll(a, k, 0), a)
        tiles = []
        for j in range(CHUNK // SUB):
            part = slice(j * SUB, (j + 1) * SUB)
            tile = a[part] * before + b[part]
            before = tile[SUB - 1 : SUB]
            tiles.append(tile)
        state = jnp.concatenate(tiles, axis=0)
        state_ref[pl.ds(base + SUB, CHUNK), :] = state
        mixed_ref[here, :] = (state * gelu(both_ref[here, :width])).astype(LOW)
        return before

    lax.fori_loop(0, count // CHUNK, step, jnp.zeros((1, width), WIDE))
    for k, (ref, out_ref) in enumerate(((mixed_ref, out_refs[1]), (state_ref, out_refs[5]))):
        departures.append(pltpu.make_async_copy(ref, out_ref, out_sems.at[4 + k]))
        departures[-1].start()
    arrivals[-1].wait()
    for k in range(features // TILE):
        here = pl.ds(k * TILE, TILE)
        partial_ref[:, here] = times(mixed_ref[...], block_ref[:, here]).astype(LOW)
        departures.append(pltpu.make_async_copy(partial_ref.at[:, here], out_refs[0].at[:, here], out_sems.at[6 + k]))
        departures[-1].start()
    for departure in departures:
        departure.wait()


def backward_kernel(heads, owners, scalars_ref, *refs):
    sources, small_refs, refs = refs[:10], refs[10:16], refs[16:]
    partial_out_ref, quarter_out_refs, held, refs = refs[0], refs[1:5], refs[5:15], refs[15:]
    grad_ref, back_ref, padded_ref, rate_low_ref, inlet_low_ref, stacked_ref, strips_ref = refs[:7]
    partials_ref, quarters_ref, in_sems, out_sems = refs[7:]
    taps_ref, rate_w_ref, inlet_w_ref, extra_ref, first_gain_ref, second_grad_ref = small_refs
    middle_ref, block_ref, both_ref, conv_ref, rate_ref, inlet_ref, state_ref, mixed_ref, first_ref, branches_ref = held
    arrivals = [pltpu.make_async_copy(*pair, in_sems.at[k]) for k, pair in enumerate(zip(sources, held))]
    for arrival in arrivals:
        arrival.start()
    for arrival in arrivals[:2]:
        arrival.wait()
    count, width = grad_ref.shape
    features = middle_ref.shape[1]

    def spread_rows(turn, _):
        here = pl.ds(pl.multiple_of(turn * ROWS, ROWS), ROWS)
        grad_ref[here, :] = times_transposed(middle_ref[here, :], block_ref[...])
        return _

    lax.fori_loop(0, count // ROWS, spread_rows, 0)
    for arrival in arrivals[2:7]:
        arrival.wait()
    padded_ref[pl.ds(0, SUB), :] = jnp.zeros((SUB, width), WIDE)
    padded_ref[pl.ds(SUB, count), :] = both_ref[:, width:]
    taps = taps_ref[...]
    soft = extra_ref[3:4, :]
    slope = extra_ref[4:5, :]
    lanes = lax.broadcasted_iota(jnp.int32, (CHUNK, width), 0) % SUB
    steps = count // CHUNK
    zero = jnp.zeros((1, width), WIDE)

    def column(values):
        return jnp.sum(values, axis=0, keepdims=True)

    def step(turn, held):
        after, late, beyond, sums = held
        base = pl.multiple_of((steps - 1 - turn) * CHUNK, SUB)
        here = pl.ds(base, CHUNK)
        wide_pos = row_positions(scalars_ref, base, CHUNK + SUB, width)
        pos = wide_pos[:CHUNK]
        fresh = pos == 0
        grad = grad_ref[here, :]
        value, bend = gelu_pair(both_ref[here, :width])
        window = state_ref[pl.ds(base, CHUNK + SUB), :]
        state = window[SUB:]
        earlier = window[SUB - 1 : SUB - 1 + CHUNK]
        back_ref[here, :width] = (grad * state * bend).astype(LOW)
        rate = rate_ref[here, :]
        inlet = inlet_ref[here, :]
        conv = conv_ref[here, :]
        conv_wide = conv.astype(WIDE)
        carry, scale = gates(rate, inlet, soft, fresh)
        b = grad * value
        a = jnp.concatenate([carry[1:], late], axis=0)
        for k in (1, 2, 4):
            inside = lanes < SUB - k
            b = b + jnp.where(inside, a * pltpu.roll(b, CHUNK - k, 0), 0.0)
            a = jnp.where(inside, a * pltpu.roll(a, CHUNK - k, 0), a)
        tiles = []
        for j in reversed(range(CHUNK // SUB)):
            part = slice(j * SUB, (j + 1) * SUB)
            tile = a[part] * after + b[part]
            after = tile[0:1]
            tiles.append(tile)
        total = jnp.concatenate(tiles[::-1], axis=0)
        late = carry[0:1]
        scaled = total * scale
        d_inlet = scaled * conv_wide
        d_scale = total * inlet * conv_wide
        d_log = jnp.where(fresh, 0.0, total * earlier * carry - d_scale * (carry * carry) / scale)
        leak = rate * d_log
        rate_low = (-soft * leak * (1.0 - rate)).astype(LOW)
        inlet_low = (d_inlet * inlet * (1.0 - inlet)).astype(LOW)
        rate_low_ref[here, :] = rate_low
        inlet_low_ref[here, :] = inlet_low
        spread = (
            scaled * inlet
            + times_transposed(rate_low, rate_w_ref[...])
            + times_transposed(inlet_low, inlet_w_ref[...])
        )
        ahead = jnp.concatenate([spread, beyond], axis=0)
        back = taps[0:1] * spread
        source = padded_ref[pl.ds(base, CHUNK + SUB), :]
        new = [column(spread), column(rate_low.astype(WIDE)), column(inlet_low.astype(WIDE)), column(leak)]
        new.append(column(spread * source[SUB:]))
        for k in range(1, taps.shape[0]):
            kept = jnp.where(wide_pos >= k, ahead, 0.0)
            back = back + taps[k : k + 1] * kept[k : k + CHUNK]
            new.append(column(kept[:CHUNK] * source[SUB - k : SUB - k + CHUNK]))
        back_ref[here, width:] = back.astype(LOW)
        return after, late, spread[:SUB], tuple(x + y for x, y in zip(sums, new))

    start = tuple(zero for _ in range(4 + taps.shape[0]))
    sums = lax.fori_loop(0, steps, step, (zero, zero, jnp.zeros((SUB, width), WIDE), start))[3]
    rows = list(sums)
    rows[3] = -slope * rows[3]
    size = width // heads
    strips, depth = strip_shape(features, heads, size, len(rows))
    stacked_ref[...] = jnp.zeros_like(stacked_ref)
    block = 0
    for low_ref in (rate_low_ref, inlet_low_ref):
        full = transposed_times(conv_ref[...], low_ref[...])
        for h in range(heads):
            part = slice(h * size, (h + 1) * size)
            stacked_ref[pl.ds(block * size, size), :] = full[part, part]
            block += 1
    small = jnp.concatenate(rows, axis=0)
    for h in range(heads):
        stacked_ref[pl.ds(block * size + h * SUB, len(rows)), :] = small[:, h * size : (h + 1) * size]
    strips_ref[...] = jnp.zeros_like(strips_ref)
    for k in range(strips):
        strips_ref[:, k * size : (k + 1) * size] = stacked_ref[pl.ds(k * depth, depth), :].astype(LOW)

    for arrival in arrivals[7:]:
        arrival.wait()
    share = count // owners
    quarter = features // 4
    departures = []
    for slot in range(4):
        if slot >= 2:
            for departure in departures[slot - 2]:
                departure.wait()
        partial_ref, quarter_ref = partials_ref.at[slot % 2], quarters_ref.at[slot % 2]
        here = pl.ds(pl.multiple_of(scalars_ref[0, slot] * quarter, quarter), quarter)
        branch_grad = transposed_times(back_ref[...], first_ref[:, here])
        quarter_ref[: 2 * width, :] = branch_grad.astype(LOW)
        quarter_ref[2 * width : 3 * width, :] = transposed_times(mixed_ref[...], middle_ref[:, here]).astype(LOW)
        quarter_ref[3 * width :, :] = strips_ref[:, here]
        gain = column(branch_grad * branches_ref[:, here].astype(WIDE)) / first_gain_ref[:, here]
        tops = []
        for value in (gain, second_grad_ref[:, here]):
            top = value.astype(LOW).astype(WIDE)
            tops += [top, value - top]
        tops = jnp.concatenate(tops + [jnp.zeros((SPARE - len(tops), quarter), WIDE)], axis=0).astype(LOW)
        partial = times(back_ref[...], branches_ref[:, here]).astype(LOW)
        for k in range(owners):
            base = k * (share + SPARE)
            partial_ref[base : base + share, :] = partial[k * share : (k + 1) * share]
            partial_ref[base + share : base + share + SPARE, :] = tops
        departures.append(
            [
                pltpu.make_async_copy(quarter_ref, quarter_out_refs[slot], out_sems.at[2 * slot]),
                pltpu.make_async_copy(partial_ref, partial_out_ref.at[:, here], out_sems.at[2 * slot + 1]),
            ]
        )
        for departure in departures[slot]:
            departure.start()
    for slot in (2, 3):
        for departure in departures[slot]:
            departure.wait()


def strip_shape(features, heads, size, small):
    strips = features // size
    rows = 2 * heads * size + heads * SUB
    return strips, -(-rows // (strips * 2 * SUB)) * 2 * SUB


def unpack_kernel(heads, strips, packed_ref, square_ref, small_ref, stacked_ref):
    depth, size = packed_ref.shape[0], square_ref.shape[-1]
    for k in range(strips):
        stacked_ref[pl.ds(k * depth, depth), :] = packed_ref[:, k * size : (k + 1) * size]
    for k in range(2 * heads):
        square_ref[k] = stacked_ref[pl.ds(k * size, size), :]
    small_ref[...] = jnp.concatenate(
        [stacked_ref[pl.ds(2 * heads * size + h * SUB, SUB), :] for h in range(heads)], axis=1
    )


def unpack_strips(packed, heads, size):
    strips, depth = strip_shape(packed.shape[1], heads, size, SUB)
    return pl.pallas_call(
        lambda *refs: unpack_kernel(heads, strips, *refs),
        out_shape=[
            jax.ShapeDtypeStruct((2 * heads, size, size), WIDE),
            jax.ShapeDtypeStruct((SUB, heads * size), WIDE),
        ],
        scratch_shapes=[pltpu.VMEM((strips * depth, size), WIDE)],
        compiler_params=pltpu.CompilerParams(vmem_limit_bytes=16 * 1024 * 1024),
        cost_estimate=NO_COST,
    )(packed)


def in_vmem():
    return pl.BlockSpec(memory_space=pltpu.VMEM)


def run_kernel(body, outs, scratch, operands, room):
    return pl.pallas_call(
        body,
        in_specs=[pl.BlockSpec(memory_space=pltpu.SMEM)] + [in_vmem()] * (len(operands) - 1),
        out_specs=[in_vmem()] * len(outs),
        out_shape=outs,
        scratch_shapes=scratch,
        compiler_params=pltpu.CompilerParams(vmem_limit_bytes=room * 1024 * 1024),
        cost_estimate=NO_COST,
    )(*operands)


def forward_mix(scalars, first, branches, block, taps, rate_w, inlet_w, extra):
    count, features = first.shape
    width = block.shape[0]
    made = [
        ((count, features), LOW),
        ((count, width), LOW),
        ((count, width), LOW),
        ((count, width), WIDE),
        ((count, width), WIDE),
        ((count + SUB, width), WIDE),
        ((count, 2 * width), WIDE),
    ]
    anywhere = pl.BlockSpec(memory_space=pl.ANY)
    return pl.pallas_call(
        forward_kernel,
        in_specs=[pl.BlockSpec(memory_space=pltpu.SMEM)] + [anywhere] * 3 + [in_vmem()] * 4,
        out_specs=[anywhere] * len(made),
        out_shape=[jax.ShapeDtypeStruct(*one) for one in made],
        scratch_shapes=[pltpu.VMEM(array.shape, array.dtype) for array in (first, branches, block)]
        + [pltpu.VMEM(*one) for one in made]
        + [
            pltpu.VMEM((count + SUB, width), WIDE),
            pltpu.SemaphoreType.DMA((count // LOAD + 2,)),
            pltpu.SemaphoreType.DMA((6 + features // TILE,)),
        ],
        compiler_params=pltpu.CompilerParams(vmem_limit_bytes=ROOM * 1024 * 1024),
        cost_estimate=NO_COST,
    )(scalars, first, branches, block, taps, rate_w, inlet_w, extra)


def backward_mix(heads, owners, scalars, large, small):
    middle, block = large[:2]
    count, features = middle.shape
    width = block.shape[0]
    size = width // heads
    strips, depth = strip_shape(features, heads, size, SUB)
    rows, lines = count + owners * SPARE, 3 * width + depth
    narrow = pltpu.VMEM((count, width), LOW)
    anywhere = pl.BlockSpec(memory_space=pl.ANY)
    return pl.pallas_call(
        lambda *refs: backward_kernel(heads, owners, *refs),
        in_specs=[pl.BlockSpec(memory_space=pltpu.SMEM)] + [anywhere] * len(large) + [in_vmem()] * len(small),
        out_specs=[anywhere] * 5,
        out_shape=[jax.ShapeDtypeStruct((rows, features), LOW)] + [jax.ShapeDtypeStruct((lines, features // 4), LOW)] * 4,
        scratch_shapes=[pltpu.VMEM(array.shape, array.dtype) for array in large]
        + [
            pltpu.VMEM((count, width), WIDE),
            pltpu.VMEM((count, 2 * width), LOW),
            pltpu.VMEM((count + SUB, width), WIDE),
            narrow,
            narrow,
            pltpu.VMEM((strips * depth, size), WIDE),
            pltpu.VMEM((depth, features), LOW),
            pltpu.VMEM((2, rows, features // 4), LOW),
            pltpu.VMEM((2, lines, features // 4), LOW),
            pltpu.SemaphoreType.DMA((len(large),)),
            pltpu.SemaphoreType.DMA((8,)),
        ],
        compiler_params=pltpu.CompilerParams(vmem_limit_bytes=ROOM * 1024 * 1024),
        cost_estimate=NO_COST,
    )(scalars, *large, *small)


def call_blocks(body, grid, spots, inputs, outputs, operands, room):
    return pl.pallas_call(
        body,
        grid_spec=pltpu.PrefetchScalarGridSpec(
            num_scalar_prefetch=1,
            grid=(grid,),
            in_specs=[pl.BlockSpec(shape, index) for shape, index in inputs],
            out_specs=[pl.BlockSpec(shape, index) for _, shape, index in outputs],
        ),
        out_shape=[made for made, _, _ in outputs],
        compiler_params=pltpu.CompilerParams(vmem_limit_bytes=room * 1024 * 1024),
        cost_estimate=NO_COST,
    )(spots, *operands)


def whole(_, at):
    return (0, 0)


def across(k, at):
    return (0, k)


def down(k, at):
    return (k, 0)


def across_spot(k, at):
    return (0, at[k])


def down_spot(k, at):
    return (at[k], 0)


def second_kernel(_, gate_low_ref, up_low_ref, gate_w_ref, up_w_ref, out_ref):
    total = times_transposed(gate_low_ref[...], gate_w_ref[...]) + times_transposed(up_low_ref[...], up_w_ref[...])
    out_ref[...] = total.astype(LOW)


def second_partial(gate_low, up_low, gate_weight, up_weight):
    count, units = gate_low.shape
    features = gate_weight.shape[0]
    return call_blocks(
        second_kernel,
        features // TILE,
        jnp.zeros((1,), jnp.int32),
        [((count, units), whole)] * 2 + [((TILE, units), down)] * 2,
        [(jax.ShapeDtypeStruct((count, features), LOW), (count, TILE), across)],
        (gate_low, up_low, gate_weight, up_weight),
        ROOM,
    )[0]


def gradient_kernel(_, left_ref, right_ref, out_ref):
    out_ref[...] = transposed_times(left_ref[...], right_ref[...]).astype(LOW)


def gradient_half(left, right, which):
    count, features = left.shape
    units = right.shape[1]
    block = features // 4
    spots = jnp.stack([2 * which, 2 * which + 1]).astype(jnp.int32)
    return call_blocks(
        gradient_kernel,
        2,
        spots,
        [((count, block), across_spot), ((count, units), whole)],
        [(jax.ShapeDtypeStruct((2 * block, units), LOW), (block, units), down)],
        (left, right),
        ROOM,
    )[0]


def norm_kernel(_, start_ref, added_ref, gain_ref, *out_refs):
    values = start_ref[...].astype(WIDE)
    if len(out_refs) == 2:
        values = values + added_ref[...].astype(WIDE)
        out_refs[1][...] = values
    out_refs[0][...] = (values * norm_scale(values) * gain_ref[...]).astype(LOW)


def normed(start, gain, added=None):
    rows, features = start.shape
    block = (rows // 2, features)
    outs = [(jax.ShapeDtypeStruct((rows, features), kind), block, down) for kind in (LOW, WIDE)]
    return call_blocks(
        norm_kernel,
        2,
        jnp.zeros((1,), jnp.int32),
        [(block, down), (block, down), ((1, features), whole)],
        outs if added is not None else outs[:1],
        (start, start if added is None else added, gain[None]),
        16,
    )


def norm_back_kernel(_, start_ref, grad_ref, added_ref, gain_ref, low_ref, total_ref, gain_grad_ref):
    values, grad = start_ref[...], grad_ref[...].astype(WIDE)
    scale = norm_scale(values)
    total = added_ref[...].astype(WIDE) + norm_back(values, scale, gain_ref[...], grad)
    total_ref[...] = total
    low_ref[...] = total.astype(LOW)
    part = jnp.sum(grad * values * scale, axis=0, keepdims=True)

    @pl.when(pl.program_id(0) == 0)
    def _():
        gain_grad_ref[...] = part

    @pl.when(pl.program_id(0) > 0)
    def _():
        gain_grad_ref[...] += part


def normed_back(start, grad, added, gain):
    rows, features = start.shape
    block = (rows // 2, features)
    line = (1, features)
    return call_blocks(
        norm_back_kernel,
        2,
        jnp.zeros((1,), jnp.int32),
        [(block, down)] * 3 + [(line, whole)],
        [(jax.ShapeDtypeStruct((rows, features), kind), block, down) for kind in (LOW, WIDE)]
        + [(jax.ShapeDtypeStruct(line, WIDE), line, whole)],
        (start, grad, added, gain[None]),
        16,
    )


def spread_blocks(weights):
    heads, size, _ = weights.shape
    full = jnp.zeros((heads, size, heads, size), weights.dtype)
    for h in range(heads):
        full = full.at[h, :, h, :].set(weights[h])
    return full.reshape(heads * size, heads * size)


def sum_rows(values):
    return lax.psum_scatter(values.astype(LOW), "mp", scatter_dimension=0, tiled=True)


def all_rows(values):
    return lax.all_gather(values, "mp", axis=0, tiled=True)


def place_kernel(pieces, kept, splits, where_ref, *refs):
    out_refs = refs[pieces + kept :]
    for k in range(pieces):

        @pl.when(pl.program_id(0) == k)
        def _():
            start = 0
            for out_ref, rows in zip(out_refs, splits):
                out_ref[...] = refs[k][pl.ds(start, rows), :].astype(out_ref.dtype)
                start += rows


def place(pieces, spots, total, axis, splits, kind, onto=()):
    count = len(pieces)
    rows, columns = pieces[0].shape
    splits = splits or (rows,)
    outs = [
        jax.ShapeDtypeStruct((r * total, columns) if axis == 0 else (r, columns * total), kind) for r in splits
    ]
    spot = (lambda k, at: (at[k], 0)) if axis == 0 else (lambda k, at: (0, at[k]))
    room = rows * columns * (2 * 2 * count + 4 * 2) + 3 * 1024 * 1024
    return pl.pallas_call(
        lambda *refs: place_kernel(count, len(onto), splits, *refs),
        grid_spec=pltpu.PrefetchScalarGridSpec(
            num_scalar_prefetch=1,
            grid=(count,),
            in_specs=[pl.BlockSpec((rows, columns), lambda k, at: (0, 0))] * count
            + [pl.BlockSpec(memory_space=pl.ANY)] * len(onto),
            out_specs=[pl.BlockSpec((r, columns), spot) for r in splits],
        ),
        out_shape=outs,
        input_output_aliases={1 + count + k: k for k in range(len(onto))},
        compiler_params=pltpu.CompilerParams(vmem_limit_bytes=room),
        cost_estimate=NO_COST,
    )(jnp.stack(spots).astype(jnp.int32), *pieces, *onto)


def dp_bits():
    return lax.axis_size("dp").bit_length() - 1


def swap(values, bit):
    count = lax.axis_size("dp")
    return lax.ppermute(values, "dp", [(i, i ^ (1 << bit)) for i in range(count)])


def order_of(turn):
    bits = dp_bits()
    return [(turn + k) % bits for k in range(bits)]


def upper_of(bit):
    return (lax.axis_index("dp") >> bit) & 1


def quarter_spots():
    left, right = (upper_of(order_of(turn)[0]) for turn in range(2))
    return jnp.stack([1 - left, left, 3 - right, 2 + right]).astype(jnp.int32)


def halves(values, axis):
    size = values.shape[axis] // 2
    return lax.slice_in_dim(values, 0, size, axis=axis), lax.slice_in_dim(values, size, 2 * size, axis=axis)


def split_for(values, axis, bit):
    first, second = halves(values, axis)
    upper = upper_of(bit) == 1
    return jnp.where(upper, first, second), jnp.where(upper, second, first)


class Part:
    def __init__(self, send, kept, axis, turn):
        self.send, self.kept = send, kept
        self.axis, self.order = axis, order_of(turn)
        self.step = 0

    def reduce(self):
        return swap(self.send, self.order[self.step])

    def land(self, got):
        self.step += 1
        total = (self.kept.astype(WIDE) + got.astype(WIDE)).astype(LOW)
        if self.step < len(self.order):
            self.send, self.kept = split_for(total, self.axis, self.order[self.step])
        else:
            self.pieces = {0: total}

    def forwards(self, level):
        made = []
        for chosen in itertools.combinations(reversed(self.order), level):
            made.append((sum(1 << bit for bit in chosen[:-1]), chosen[-1]))
        return made

    def spot(self, mask):
        owner = lax.axis_index("dp") ^ mask
        bits = len(self.order)
        return sum(((owner >> self.order[k]) & 1) << (bits - 1 - k) for k in range(bits))


def start_gather(parts, level):
    return [(part, mask ^ (1 << bit), swap(part.pieces[mask], bit)) for part in parts for mask, bit in part.forwards(level)]


def exchange(reducing=(), gathered=(), extras=()):
    gots = [part.reduce() for part in reducing]
    kepts = [part.kept for part in reducing]
    made = lax.optimization_barrier((*gots, *[piece for _, _, piece in gathered], *extras, *kepts))
    for part, got, kept in zip(reducing, made, made[len(made) - len(kepts) :]):
        part.kept = kept
        part.land(got)
    for (part, mask, _), piece in zip(gathered, made[len(gots) :]):
        part.pieces[mask] = piece
    return made[len(gots) + len(gathered) : len(made) - len(kepts)]


def reduce_fully(parts):
    while parts[0].step < len(parts[0].order):
        exchange(parts)


def gather_fully(parts, level):
    for more in range(level, dp_bits() + 1):
        exchange(gathered=start_gather(parts, more))


def finish(parts, axis, splits=None, masks=None, onto=()):
    count = 1 << dp_bits()
    chosen = [(turn, mask) for turn, part in enumerate(parts) for mask in part.pieces if masks is None or mask in masks]
    spots = [parts[turn].spot(mask) + turn * count for turn, mask in chosen]
    blocks = [parts[turn].pieces[mask] for turn, mask in chosen]
    return place(blocks, spots, len(parts) * count, axis, splits, WIDE, onto)


def column_parts(quarters):
    return [Part(quarters[2 * turn], quarters[2 * turn + 1], 1, turn) for turn in range(2)]


def next_chip(values, step):
    count = lax.axis_size("mp")
    return lax.ppermute(values, "mp", [(i, (i + 2 * step) % count) for i in range(count)])


def other_core(values):
    return lax.ppermute(values, "mp", [(i, i ^ 1) for i in range(lax.axis_size("mp"))])


def tie(values, *others):
    return lax.optimization_barrier((values,) + others)[0]


def local(
    tokens,
    lengths,
    first_gain,
    branch_gate,
    branch_input,
    conv_weight,
    conv_bias,
    rate_weight,
    rate_bias,
    inlet_weight,
    inlet_bias,
    decay_param,
    block_out,
    second_gain,
    gate_weight,
    up_weight,
    down_weight,
    out_grad,
):
    heads = rate_weight.shape[0]
    width = decay_param.shape[0]
    features = tokens.shape[1]
    taps_count = conv_weight.shape[0]
    own_count = tokens.shape[0]
    own_input = tokens.astype(WIDE)
    own_grad = out_grad.astype(WIDE)
    first_rows = all_rows(normed(tokens, first_gain)[0])
    soft = DECAY_SCALE * jax.nn.softplus(decay_param)
    slope = DECAY_SCALE * jax.nn.sigmoid(decay_param)
    extra = jnp.stack([conv_bias, rate_bias, inlet_bias, soft, slope])
    rate_w = spread_blocks(rate_weight)
    inlet_w = spread_blocks(inlet_weight)
    branches = jnp.concatenate([branch_gate.T, branch_input.T])

    first_rows = tie(first_rows, rate_w, inlet_w, extra, branches)
    spots = quarter_spots()
    scalars = jnp.concatenate([spots, lengths[0]])[None]
    block_partial, mixed, conv, rate, inlet, state, both = forward_mix(
        scalars, first_rows, branches, block_out, conv_weight, rate_w, inlet_w, extra
    )
    chips = lax.axis_size("mp") // 2
    onward, backward = {0: tie(out_grad, first_rows)}, {}
    onward[1], backward[1] = next_chip(onward[0], 1), next_chip(onward[0], -1)
    block_partial, onward[1], backward[1] = lax.optimization_barrier((block_partial, onward[1], backward[1]))

    block_sum = sum_rows(block_partial)
    for hop in range(2, chips // 2 + 1):
        onward[hop] = next_chip(onward[hop - 1], 1)
        if 2 * hop < chips:
            backward[hop] = next_chip(backward[hop - 1], -1)
    shards = {hop: piece for hop, piece in onward.items()} | {-hop: piece for hop, piece in backward.items()}
    near_hops = [hop for hop in shards if abs(hop) < 2]
    far_hops = [hop for hop in shards if abs(hop) >= 2]
    made = lax.optimization_barrier(
        (block_sum, *[shards[hop] for hop in far_hops], *[other_core(shards[hop]) for hop in near_hops])
    )
    block_sum = made[0]
    shards |= dict(zip(far_hops, made[1:]))
    others = dict(zip(near_hops, made[1 + len(far_hops) :])) | {hop: other_core(shards[hop]) for hop in far_hops}
    own_second, own_middle = normed(tokens, second_gain, block_sum)
    second_rows = all_rows(own_second)
    me = lax.axis_index("mp")
    blocks, places = [], []
    for hop in shards:
        base = 2 * ((me // 2 + chips - hop) % chips)
        blocks += [shards[hop], others[hop]]
        places += [base + me % 2, base + 1 - me % 2]
    (grad_rows,) = place(blocks, places, 2 * chips, 0, None, LOW)
    d_hidden = times_transposed(grad_rows, down_weight)
    second_rows, d_hidden = lax.optimization_barrier((second_rows, d_hidden))
    gate_act = times(second_rows, gate_weight)
    up_act = times(second_rows, up_weight)
    value, bend = gelu_pair(gate_act)
    hidden = (value * up_act).astype(LOW)
    gate_low = (d_hidden * up_act * bend).astype(LOW)
    up_low = (d_hidden * value).astype(LOW)

    down_parts = []
    for turn, half in enumerate(halves(transposed_times(hidden, grad_rows).astype(LOW), 1)):
        down_parts.append(Part(*split_for(half, 1, order_of(turn)[0]), 1, turn))
    late_rows = tie(second_rows, *[part.send for part in down_parts])
    uppers = [upper_of(order_of(turn)[0]) for turn in range(2)]
    gate_send = gradient_half(late_rows, gate_low, 1 - uppers[0])
    up_send = gradient_half(tie(late_rows, gate_send), up_low, 1 - uppers[1])
    partial = second_partial(tie(gate_low, gate_send, up_send), up_low, gate_weight, up_weight)
    partial, gate_send, up_send = exchange(down_parts, extras=(partial, gate_send, up_send))

    second_input = sum_rows(partial)
    late_rows = tie(second_rows, partial)
    wide_parts = [
        Part(gate_send, gradient_half(late_rows, gate_low, uppers[0]), 0, 0),
        Part(up_send, gradient_half(late_rows, up_low, uppers[1]), 0, 1),
    ]
    mlp = down_parts + wide_parts
    middle_low, middle_grad, second_gain_grad = normed_back(own_middle, second_input, out_grad, second_gain)
    made = exchange(down_parts + wide_parts, extras=(middle_low, middle_grad, second_gain_grad))
    middle_low, middle_grad, second_gain_grad = made
    middle_rows = all_rows(middle_low)

    reduce_fully(down_parts)
    out_partial = times(tie(hidden, middle_low), down_weight)
    middle_rows, out_partial = exchange(wide_parts, start_gather(down_parts, 1), (middle_rows, out_partial))
    out_sum = sum_rows(out_partial)

    reduce_fully(wide_parts)
    owners = lax.axis_size("mp")
    made = backward_mix(
        heads,
        owners,
        scalars,
        (middle_rows, block_out, both, conv, rate, inlet, state, mixed, first_rows, branches),
        (conv_weight, rate_w, inlet_w, extra, first_gain[None], second_gain_grad),
    )
    first_partial, *quarters = exchange(gathered=start_gather(wide_parts, 1), extras=made)
    first_input = sum_rows(tie(first_partial, out_sum))
    output = (own_middle + out_sum.astype(WIDE)).astype(LOW)

    late = column_parts(quarters)
    wide_rest = start_gather(wide_parts, 2)
    exchange(late)
    down_rest = start_gather(down_parts, 2)
    first_input, output = exchange(late, wide_rest + down_rest, (first_input, output))
    gather_fully(mlp, 3)
    reduce_fully(late)
    first_input = first_input.astype(WIDE)
    first_scale = norm_scale(own_input)
    sums = first_input[own_count:]
    gains = jnp.stack([sums[0] + sums[1], sums[2] + sums[3]])
    input_grad = middle_grad + norm_back(own_input, first_scale, first_gain, first_input[:own_count])
    (gate_grad,) = finish([wide_parts[0]], 0)
    (up_grad,) = finish([wide_parts[1]], 0)
    (down_grad,) = finish(down_parts, 1)
    gate_grad, down_grad, input_grad, other = exchange(
        gathered=start_gather(late, 1), extras=(gate_grad, down_grad, input_grad, swap(gains, 0))
    )
    gains = gains + other
    own = [0] + [1 << bit for bit in range(dp_bits())]
    splits = (width, width, width, quarters[0].shape[0] - 3 * width)
    halfway = finish(late, 1, splits, own)
    made = exchange(gathered=start_gather(late, 2), extras=(swap(gains, 1), up_grad, *halfway))
    gather_fully(late, 3)
    gains, up_grad = gains + made[0], made[1]
    for bit in range(2, dp_bits()):
        gains = gains + swap(gains, bit)
    rest = [mask for mask in late[0].pieces if mask not in own]
    branch_gate_grad, branch_input_grad, block_grad, packed = finish(late, 1, splits, rest, made[2:])
    square, small = unpack_strips(packed, heads, width // heads)
    square = square.reshape(2, heads, *square.shape[1:])
    return (
        output,
        input_grad,
        gains[0],
        branch_gate_grad.T,
        branch_input_grad.T,
        small[4 : 4 + taps_count],
        small[0],
        square[0],
        small[1],
        square[1],
        small[2],
        small[3],
        block_grad,
        gains[1],
        gate_grad,
        up_grad,
        down_grad,
    )


def solution(mesh):
    rows = P(("dp", "mp"), None)
    out_columns = P(None, "mp")
    out_rows = P("mp", None)
    blocks = P("mp", None, None)
    vector = P("mp")
    in_specs = (
        rows, P("dp", None), P(), out_columns, out_columns, out_columns, vector, blocks, vector, blocks,
        vector, vector, out_rows, P(), out_columns, out_columns, out_rows, rows,
    )
    out_specs = (
        rows, rows, P(), out_columns, out_columns, out_columns, vector, blocks, vector, blocks,
        vector, vector, out_rows, P(), out_columns, out_columns, out_rows,
    )
    return jax.shard_map(local, mesh=mesh, in_specs=in_specs, out_specs=out_specs, check_vma=False)
```

```python
import itertools

import jax
import jax.numpy as jnp
from jax import lax
from jax.experimental import pallas as pl
from jax.experimental.pallas import tpu as pltpu
from jax.sharding import PartitionSpec as P

EPS = 1e-06
DECAY_SCALE = 8.0
GELU_RATE = 0.7978845608028654
GELU_CUBE = 0.044715
CHUNK = 48
SUB = 8
LOW = jnp.bfloat16
WIDE = jnp.float32
NO_COST = pl.CostEstimate(flops=0, bytes_accessed=0, transcendentals=0)
ROWS = 256
SPARE = 16
ROOM = 60
TILE = 512
LOAD = 192


def times(left, right):
    return jnp.dot(left, right, preferred_element_type=WIDE)


def times_transposed(left, right):
    return lax.dot_general(left, right, (((1,), (1,)), ((), ())), preferred_element_type=WIDE)


def transposed_times(left, right):
    return lax.dot_general(left, right, (((0,), (0,)), ((), ())), preferred_element_type=WIDE)


def gelu(v):
    return 0.5 * v * (1.0 + jnp.tanh(GELU_RATE * (v + GELU_CUBE * v * v * v)))


def gelu_pair(v):
    square = v * v
    bend = jnp.tanh(GELU_RATE * v * (1.0 + GELU_CUBE * square))
    half = 0.5 * (1.0 + bend)
    slope = half + 0.5 * v * (1.0 - bend * bend) * (GELU_RATE + 3.0 * GELU_RATE * GELU_CUBE * square)
    return v * half, slope


def norm_scale(values):
    return lax.rsqrt(jnp.mean(values * values, axis=-1, keepdims=True) + EPS)


def norm_back(values, scale, gain, grad):
    unit = values * scale
    lifted = gain * grad
    return scale * (lifted - unit * jnp.mean(lifted * unit, axis=-1, keepdims=True))


def one_minus_exp(y):
    series = 1.0 - y * (1.0 / 9.0)
    for order in range(8, 1, -1):
        series = 1.0 - y * (1.0 / order) * series
    return jnp.where(y < 0.5, y * series, 1.0 - jnp.exp(-y))


def row_positions(scalars_ref, base, rows, width):
    places = base + lax.broadcasted_iota(jnp.int32, (rows, width), 0)
    first = jnp.zeros_like(places)
    start = jnp.int32(0)
    for at in range(4, scalars_ref.shape[1] - 1):
        start = start + scalars_ref[0, at]
        first = jnp.where(places >= start, start, first)
    return places - first


def gates(rate, inlet, soft, fresh):
    log_a = -rate * soft
    carry = jnp.where(fresh, 0.0, jnp.exp(log_a))
    scale = jnp.where(fresh, 1.0, jnp.sqrt(one_minus_exp(-2.0 * log_a)))
    return carry, scale


def forward_kernel(scalars_ref, *refs):
    sources, (taps_ref, rate_w_ref, inlet_w_ref, extra_ref), refs = refs[:3], refs[3:7], refs[7:]
    out_refs, refs = refs[:7], refs[7:]
    first_ref, branches_ref, block_ref = refs[:3]
    partial_ref, mixed_ref, conv_ref, rate_ref, inlet_ref, state_ref, both_ref = refs[3:10]
    padded_ref, in_sems, out_sems = refs[10:]
    count, width = mixed_ref.shape
    features = first_ref.shape[1]
    pieces = count // LOAD
    arrivals = [
        pltpu.make_async_copy(sources[1], branches_ref, in_sems.at[pieces]),
        *[
            pltpu.make_async_copy(sources[0].at[pl.ds(k * LOAD, LOAD), :], first_ref.at[pl.ds(k * LOAD, LOAD), :], in_sems.at[k])
            for k in range(pieces)
        ],
        pltpu.make_async_copy(sources[2], block_ref, in_sems.at[pieces + 1]),
    ]
    for arrival in arrivals:
        arrival.start()
    arrivals[0].wait()
    for k in range(pieces):
        arrivals[1 + k].wait()
        here = pl.ds(k * LOAD, LOAD)
        both_ref[here, :] = times_transposed(first_ref[here, :], branches_ref[...])
    departures = [pltpu.make_async_copy(both_ref, out_refs[6], out_sems.at[0])]
    departures[0].start()

    padded_ref[pl.ds(0, SUB), :] = jnp.zeros((SUB, width), WIDE)
    padded_ref[pl.ds(SUB, count), :] = both_ref[:, width:]
    state_ref[pl.ds(0, SUB), :] = jnp.zeros((SUB, width), WIDE)
    taps = taps_ref[...]
    bias, rate_b, inlet_b, soft = (extra_ref[k : k + 1, :] for k in range(4))
    lanes = lax.broadcasted_iota(jnp.int32, (CHUNK, width), 0) % SUB

    def convolve(at, _):
        base = pl.multiple_of(at * CHUNK, SUB)
        pos = row_positions(scalars_ref, base, CHUNK, width)
        window = padded_ref[pl.ds(base, CHUNK + SUB), :]
        total = bias + taps[0:1] * window[SUB:]
        for k in range(1, taps.shape[0]):
            moved = window[SUB - k : SUB - k + CHUNK]
            total = total + jnp.where(pos >= k, taps[k : k + 1] * moved, 0.0)
        conv_ref[pl.ds(base, CHUNK), :] = total.astype(LOW)
        return _

    lax.fori_loop(0, count // CHUNK, convolve, 0)

    def open_gates(at, _):
        here = pl.ds(pl.multiple_of(at * ROWS, ROWS), ROWS)
        rate_ref[here, :] = jax.nn.sigmoid(times(conv_ref[here, :], rate_w_ref[...]) + rate_b)
        inlet_ref[here, :] = jax.nn.sigmoid(times(conv_ref[here, :], inlet_w_ref[...]) + inlet_b)
        return _

    lax.fori_loop(0, count // ROWS, open_gates, 0)
    for k, (ref, out_ref) in enumerate(((conv_ref, out_refs[2]), (rate_ref, out_refs[3]), (inlet_ref, out_refs[4]))):
        departures.append(pltpu.make_async_copy(ref, out_ref, out_sems.at[1 + k]))
        departures[-1].start()

    def step(at, before):
        base = pl.multiple_of(at * CHUNK, SUB)
        here = pl.ds(base, CHUNK)
        pos = row_positions(scalars_ref, base, CHUNK, width)
        a, scale = gates(rate_ref[here, :], inlet_ref[here, :], soft, pos == 0)
        b = scale * inlet_ref[here, :] * conv_ref[here, :].astype(WIDE)
        for k in (1, 2, 4):
            inside = lanes >= k
            b = b + jnp.where(inside, a * pltpu.roll(b, k, 0), 0.0)
            a = jnp.where(inside, a * pltpu.roll(a, k, 0), a)
        tiles = []
        for j in range(CHUNK // SUB):
            part = slice(j * SUB, (j + 1) * SUB)
            tile = a[part] * before + b[part]
            before = tile[SUB - 1 : SUB]
            tiles.append(tile)
        state = jnp.concatenate(tiles, axis=0)
        state_ref[pl.ds(base + SUB, CHUNK), :] = state
        mixed_ref[here, :] = (state * gelu(both_ref[here, :width])).astype(LOW)
        return before

    lax.fori_loop(0, count // CHUNK, step, jnp.zeros((1, width), WIDE))
    for k, (ref, out_ref) in enumerate(((mixed_ref, out_refs[1]), (state_ref, out_refs[5]))):
        departures.append(pltpu.make_async_copy(ref, out_ref, out_sems.at[4 + k]))
        departures[-1].start()
    arrivals[-1].wait()
    for k in range(features // TILE):
        here = pl.ds(k * TILE, TILE)
        partial_ref[:, here] = times(mixed_ref[...], block_ref[:, here]).astype(LOW)
        departures.append(pltpu.make_async_copy(partial_ref.at[:, here], out_refs[0].at[:, here], out_sems.at[6 + k]))
        departures[-1].start()
    for departure in departures:
        departure.wait()


def backward_kernel(heads, owners, scalars_ref, *refs):
    sources, small_refs, refs = refs[:10], refs[10:16], refs[16:]
    partial_out_ref, quarter_out_refs, held, refs = refs[0], refs[1:5], refs[5:15], refs[15:]
    grad_ref, back_ref, padded_ref, rate_low_ref, inlet_low_ref, stacked_ref, strips_ref = refs[:7]
    partials_ref, quarters_ref, in_sems, out_sems = refs[7:]
    taps_ref, rate_w_ref, inlet_w_ref, extra_ref, first_gain_ref, second_grad_ref = small_refs
    middle_ref, block_ref, both_ref, conv_ref, rate_ref, inlet_ref, state_ref, mixed_ref, first_ref, branches_ref = held
    arrivals = [pltpu.make_async_copy(*pair, in_sems.at[k]) for k, pair in enumerate(zip(sources, held))]
    for arrival in arrivals:
        arrival.start()
    for arrival in arrivals[:2]:
        arrival.wait()
    count, width = grad_ref.shape
    features = middle_ref.shape[1]

    def spread_rows(turn, _):
        here = pl.ds(pl.multiple_of(turn * ROWS, ROWS), ROWS)
        grad_ref[here, :] = times_transposed(middle_ref[here, :], block_ref[...])
        return _

    lax.fori_loop(0, count // ROWS, spread_rows, 0)
    for arrival in arrivals[2:7]:
        arrival.wait()
    padded_ref[pl.ds(0, SUB), :] = jnp.zeros((SUB, width), WIDE)
    padded_ref[pl.ds(SUB, count), :] = both_ref[:, width:]
    taps = taps_ref[...]
    soft = extra_ref[3:4, :]
    slope = extra_ref[4:5, :]
    lanes = lax.broadcasted_iota(jnp.int32, (CHUNK, width), 0) % SUB
    steps = count // CHUNK
    zero = jnp.zeros((1, width), WIDE)

    def column(values):
        return jnp.sum(values, axis=0, keepdims=True)

    def step(turn, held):
        after, late, beyond, sums = held
        base = pl.multiple_of((steps - 1 - turn) * CHUNK, SUB)
        here = pl.ds(base, CHUNK)
        wide_pos = row_positions(scalars_ref, base, CHUNK + SUB, width)
        pos = wide_pos[:CHUNK]
        fresh = pos == 0
        grad = grad_ref[here, :]
        value, bend = gelu_pair(both_ref[here, :width])
        window = state_ref[pl.ds(base, CHUNK + SUB), :]
        state = window[SUB:]
        earlier = window[SUB - 1 : SUB - 1 + CHUNK]
        back_ref[here, :width] = (grad * state * bend).astype(LOW)
        rate = rate_ref[here, :]
        inlet = inlet_ref[here, :]
        conv = conv_ref[here, :]
        conv_wide = conv.astype(WIDE)
        carry, scale = gates(rate, inlet, soft, fresh)
        b = grad * value
        a = jnp.concatenate([carry[1:], late], axis=0)
        for k in (1, 2, 4):
            inside = lanes < SUB - k
            b = b + jnp.where(inside, a * pltpu.roll(b, CHUNK - k, 0), 0.0)
            a = jnp.where(inside, a * pltpu.roll(a, CHUNK - k, 0), a)
        tiles = []
        for j in reversed(range(CHUNK // SUB)):
            part = slice(j * SUB, (j + 1) * SUB)
            tile = a[part] * after + b[part]
            after = tile[0:1]
            tiles.append(tile)
        total = jnp.concatenate(tiles[::-1], axis=0)
        late = carry[0:1]
        scaled = total * scale
        d_inlet = scaled * conv_wide
        d_scale = total * inlet * conv_wide
        d_log = jnp.where(fresh, 0.0, total * earlier * carry - d_scale * (carry * carry) / scale)
        leak = rate * d_log
        rate_low = (-soft * leak * (1.0 - rate)).astype(LOW)
        inlet_low = (d_inlet * inlet * (1.0 - inlet)).astype(LOW)
        rate_low_ref[here, :] = rate_low
        inlet_low_ref[here, :] = inlet_low
        spread = (
            scaled * inlet
            + times_transposed(rate_low, rate_w_ref[...])
            + times_transposed(inlet_low, inlet_w_ref[...])
        )
        ahead = jnp.concatenate([spread, beyond], axis=0)
        back = taps[0:1] * spread
        source = padded_ref[pl.ds(base, CHUNK + SUB), :]
        new = [column(spread), column(rate_low.astype(WIDE)), column(inlet_low.astype(WIDE)), column(leak)]
        new.append(column(spread * source[SUB:]))
        for k in range(1, taps.shape[0]):
            kept = jnp.where(wide_pos >= k, ahead, 0.0)
            back = back + taps[k : k + 1] * kept[k : k + CHUNK]
            new.append(column(kept[:CHUNK] * source[SUB - k : SUB - k + CHUNK]))
        back_ref[here, width:] = back.astype(LOW)
        return after, late, spread[:SUB], tuple(x + y for x, y in zip(sums, new))

    start = tuple(zero for _ in range(4 + taps.shape[0]))
    sums = lax.fori_loop(0, steps, step, (zero, zero, jnp.zeros((SUB, width), WIDE), start))[3]
    rows = list(sums)
    rows[3] = -slope * rows[3]
    size = width // heads
    strips, depth = strip_shape(features, heads, size, len(rows))
    stacked_ref[...] = jnp.zeros_like(stacked_ref)
    block = 0
    for low_ref in (rate_low_ref, inlet_low_ref):
        full = transposed_times(conv_ref[...], low_ref[...])
        for h in range(heads):
            part = slice(h * size, (h + 1) * size)
            stacked_ref[pl.ds(block * size, size), :] = full[part, part]
            block += 1
    small = jnp.concatenate(rows, axis=0)
    for h in range(heads):
        stacked_ref[pl.ds(block * size + h * SUB, len(rows)), :] = small[:, h * size : (h + 1) * size]
    strips_ref[...] = jnp.zeros_like(strips_ref)
    for k in range(strips):
        strips_ref[:, k * size : (k + 1) * size] = stacked_ref[pl.ds(k * depth, depth), :].astype(LOW)

    for arrival in arrivals[7:]:
        arrival.wait()
    share = count // owners
    quarter = features // 4
    departures = []
    for slot in range(4):
        if slot >= 2:
            for departure in departures[slot - 2]:
                departure.wait()
        partial_ref, quarter_ref = partials_ref.at[slot % 2], quarters_ref.at[slot % 2]
        here = pl.ds(pl.multiple_of(scalars_ref[0, slot] * quarter, quarter), quarter)
        branch_grad = transposed_times(back_ref[...], first_ref[:, here])
        quarter_ref[: 2 * width, :] = branch_grad.astype(LOW)
        quarter_ref[2 * width : 3 * width, :] = transposed_times(mixed_ref[...], middle_ref[:, here]).astype(LOW)
        quarter_ref[3 * width :, :] = strips_ref[:, here]
        gain = column(branch_grad * branches_ref[:, here].astype(WIDE)) / first_gain_ref[:, here]
        tops = []
        for value in (gain, second_grad_ref[:, here]):
            top = value.astype(LOW).astype(WIDE)
            tops += [top, value - top]
        tops = jnp.concatenate(tops + [jnp.zeros((SPARE - len(tops), quarter), WIDE)], axis=0).astype(LOW)
        partial = times(back_ref[...], branches_ref[:, here]).astype(LOW)
        for k in range(owners):
            base = k * (share + SPARE)
            partial_ref[base : base + share, :] = partial[k * share : (k + 1) * share]
            partial_ref[base + share : base + share + SPARE, :] = tops
        departures.append(
            [
                pltpu.make_async_copy(quarter_ref, quarter_out_refs[slot], out_sems.at[2 * slot]),
                pltpu.make_async_copy(partial_ref, partial_out_ref.at[:, here], out_sems.at[2 * slot + 1]),
            ]
        )
        for departure in departures[slot]:
            departure.start()
    for slot in (2, 3):
        for departure in departures[slot]:
            departure.wait()


def strip_shape(features, heads, size, small):
    strips = features // size
    rows = 2 * heads * size + heads * SUB
    return strips, -(-rows // (strips * 2 * SUB)) * 2 * SUB


def unpack_kernel(heads, strips, packed_ref, square_ref, taps_ref, *refs):
    line_refs, stacked_ref = refs[:-1], refs[-1]
    depth, size = packed_ref.shape[0], square_ref.shape[-1]
    for k in range(strips):
        stacked_ref[pl.ds(k * depth, depth), :] = packed_ref[:, k * size : (k + 1) * size]
    for k in range(2 * heads):
        square_ref[k] = stacked_ref[pl.ds(k * size, size), :]
    small = jnp.concatenate(
        [stacked_ref[pl.ds(2 * heads * size + h * SUB, SUB), :] for h in range(heads)], axis=1
    )
    taps_ref[...] = small[len(line_refs) :]
    for k, line_ref in enumerate(line_refs):
        line_ref[...] = small[k]


def unpack_strips(packed, heads, size):
    strips, depth = strip_shape(packed.shape[1], heads, size, SUB)
    return pl.pallas_call(
        lambda *refs: unpack_kernel(heads, strips, *refs),
        out_shape=[
            jax.ShapeDtypeStruct((2 * heads, size, size), WIDE),
            jax.ShapeDtypeStruct((SUB - 4, heads * size), WIDE),
        ]
        + [jax.ShapeDtypeStruct((heads * size,), WIDE)] * 4,
        scratch_shapes=[pltpu.VMEM((strips * depth, size), WIDE)],
        compiler_params=pltpu.CompilerParams(vmem_limit_bytes=16 * 1024 * 1024),
        cost_estimate=NO_COST,
    )(packed)


def in_vmem():
    return pl.BlockSpec(memory_space=pltpu.VMEM)


def run_kernel(body, outs, scratch, operands, room):
    return pl.pallas_call(
        body,
        in_specs=[pl.BlockSpec(memory_space=pltpu.SMEM)] + [in_vmem()] * (len(operands) - 1),
        out_specs=[in_vmem()] * len(outs),
        out_shape=outs,
        scratch_shapes=scratch,
        compiler_params=pltpu.CompilerParams(vmem_limit_bytes=room * 1024 * 1024),
        cost_estimate=NO_COST,
    )(*operands)


def forward_mix(scalars, first, branches, block, taps, rate_w, inlet_w, extra):
    count, features = first.shape
    width = block.shape[0]
    made = [
        ((count, features), LOW),
        ((count, width), LOW),
        ((count, width), LOW),
        ((count, width), WIDE),
        ((count, width), WIDE),
        ((count + SUB, width), WIDE),
        ((count, 2 * width), WIDE),
    ]
    anywhere = pl.BlockSpec(memory_space=pl.ANY)
    return pl.pallas_call(
        forward_kernel,
        in_specs=[pl.BlockSpec(memory_space=pltpu.SMEM)] + [anywhere] * 3 + [in_vmem()] * 4,
        out_specs=[anywhere] * len(made),
        out_shape=[jax.ShapeDtypeStruct(*one) for one in made],
        scratch_shapes=[pltpu.VMEM(array.shape, array.dtype) for array in (first, branches, block)]
        + [pltpu.VMEM(*one) for one in made]
        + [
            pltpu.VMEM((count + SUB, width), WIDE),
            pltpu.SemaphoreType.DMA((count // LOAD + 2,)),
            pltpu.SemaphoreType.DMA((6 + features // TILE,)),
        ],
        compiler_params=pltpu.CompilerParams(vmem_limit_bytes=ROOM * 1024 * 1024),
        cost_estimate=NO_COST,
    )(scalars, first, branches, block, taps, rate_w, inlet_w, extra)


def backward_mix(heads, owners, scalars, large, small):
    middle, block = large[:2]
    count, features = middle.shape
    width = block.shape[0]
    size = width // heads
    strips, depth = strip_shape(features, heads, size, SUB)
    rows, lines = count + owners * SPARE, 3 * width + depth
    narrow = pltpu.VMEM((count, width), LOW)
    anywhere = pl.BlockSpec(memory_space=pl.ANY)
    return pl.pallas_call(
        lambda *refs: backward_kernel(heads, owners, *refs),
        in_specs=[pl.BlockSpec(memory_space=pltpu.SMEM)] + [anywhere] * len(large) + [in_vmem()] * len(small),
        out_specs=[anywhere] * 5,
        out_shape=[jax.ShapeDtypeStruct((rows, features), LOW)] + [jax.ShapeDtypeStruct((lines, features // 4), LOW)] * 4,
        scratch_shapes=[pltpu.VMEM(array.shape, array.dtype) for array in large]
        + [
            pltpu.VMEM((count, width), WIDE),
            pltpu.VMEM((count, 2 * width), LOW),
            pltpu.VMEM((count + SUB, width), WIDE),
            narrow,
            narrow,
            pltpu.VMEM((strips * depth, size), WIDE),
            pltpu.VMEM((depth, features), LOW),
            pltpu.VMEM((2, rows, features // 4), LOW),
            pltpu.VMEM((2, lines, features // 4), LOW),
            pltpu.SemaphoreType.DMA((len(large),)),
            pltpu.SemaphoreType.DMA((8,)),
        ],
        compiler_params=pltpu.CompilerParams(vmem_limit_bytes=ROOM * 1024 * 1024),
        cost_estimate=NO_COST,
    )(scalars, *large, *small)


def call_blocks(body, grid, spots, inputs, outputs, operands, room):
    return pl.pallas_call(
        body,
        grid_spec=pltpu.PrefetchScalarGridSpec(
            num_scalar_prefetch=1,
            grid=(grid,),
            in_specs=[pl.BlockSpec(shape, index) for shape, index in inputs],
            out_specs=[pl.BlockSpec(shape, index) for _, shape, index in outputs],
        ),
        out_shape=[made for made, _, _ in outputs],
        compiler_params=pltpu.CompilerParams(vmem_limit_bytes=room * 1024 * 1024),
        cost_estimate=NO_COST,
    )(spots, *operands)


def whole(_, at):
    return (0, 0)


def across(k, at):
    return (0, k)


def down(k, at):
    return (k, 0)


def across_spot(k, at):
    return (0, at[k])


def down_spot(k, at):
    return (at[k], 0)


def early_kernel(spots_ref, *refs):
    rows_hbm, lows_hbm, weights_hbm, refs = refs[0], refs[1:3], refs[3:5], refs[5:]
    partial_hbm, sends_hbm, refs = refs[0], refs[1:3], refs[3:]
    rows_refs, low_refs, weight_refs, partial_ref, send_refs = refs[0:2], refs[2:4], refs[4:6], refs[6], refs[7:9]
    in_sems, out_sems = refs[9:]
    features = partial_ref.shape[1]
    tiles = features // TILE
    half = features // 2
    low_copies = [pltpu.make_async_copy(lows_hbm[k], low_refs[k], in_sems.at[k]) for k in range(2)]
    weight_copies = [
        [
            pltpu.make_async_copy(
                weights_hbm[k].at[pl.ds(t * TILE, TILE), :],
                weight_refs[k].at[pl.ds(t * TILE, TILE), :],
                in_sems.at[2 + 2 * t + k],
            )
            for k in range(2)
        ]
        for t in range(tiles)
    ]
    row_copies = [
        pltpu.make_async_copy(
            rows_hbm.at[:, pl.ds(pl.multiple_of(spots_ref[k] * half, half), half)],
            rows_refs[k],
            in_sems.at[2 + 2 * tiles + k],
        )
        for k in range(2)
    ]
    for copy in low_copies + [copy for pair in weight_copies for copy in pair] + row_copies:
        copy.start()
    for copy in low_copies:
        copy.wait()
    departures = []
    for t in range(tiles):
        here = pl.ds(t * TILE, TILE)
        for copy in weight_copies[t]:
            copy.wait()
        total = times_transposed(low_refs[0][...], weight_refs[0][here, :])
        total += times_transposed(low_refs[1][...], weight_refs[1][here, :])
        partial_ref[:, here] = total.astype(LOW)
        departures.append(pltpu.make_async_copy(partial_ref.at[:, here], partial_hbm.at[:, here], out_sems.at[t]))
        departures[-1].start()
    for k in range(2):
        row_copies[k].wait()
        for t in range(half // TILE):
            here = pl.ds(t * TILE, TILE)
            send_refs[k][here, :] = transposed_times(rows_refs[k][:, here], low_refs[k][...]).astype(LOW)
            departures.append(
                pltpu.make_async_copy(
                    send_refs[k].at[here, :], sends_hbm[k].at[here, :], out_sems.at[tiles + k * (half // TILE) + t]
                )
            )
            departures[-1].start()
    for departure in departures:
        departure.wait()


def early_products(rows, gate_low, up_low, gate_weight, up_weight, spots):
    count, features = rows.shape
    units = gate_low.shape[1]
    half = features // 2
    made = [((count, features), LOW), ((half, units), LOW), ((half, units), LOW)]
    anywhere = pl.BlockSpec(memory_space=pl.ANY)
    return pl.pallas_call(
        early_kernel,
        in_specs=[pl.BlockSpec(memory_space=pltpu.SMEM)] + [anywhere] * 5,
        out_specs=[anywhere] * 3,
        out_shape=[jax.ShapeDtypeStruct(*one) for one in made],
        scratch_shapes=[pltpu.VMEM((count, half), LOW)] * 2
        + [pltpu.VMEM((count, units), LOW)] * 2
        + [pltpu.VMEM((features, units), LOW)] * 2
        + [pltpu.VMEM(*one) for one in made]
        + [
            pltpu.SemaphoreType.DMA((4 + 2 * (features // TILE),)),
            pltpu.SemaphoreType.DMA((2 * (features // TILE),)),
        ],
        compiler_params=pltpu.CompilerParams(vmem_limit_bytes=ROOM * 1024 * 1024),
        cost_estimate=NO_COST,
    )(spots, rows, gate_low, up_low, gate_weight, up_weight)


def gradient_kernel(_, left_ref, right_ref, out_ref):
    out_ref[...] = transposed_times(left_ref[...], right_ref[...]).astype(LOW)


def gradient_half(left, right, which):
    count, features = left.shape
    units = right.shape[1]
    block = features // 4
    spots = jnp.stack([2 * which, 2 * which + 1]).astype(jnp.int32)
    return call_blocks(
        gradient_kernel,
        2,
        spots,
        [((count, block), across_spot), ((count, units), whole)],
        [(jax.ShapeDtypeStruct((2 * block, units), LOW), (block, units), down)],
        (left, right),
        ROOM,
    )[0]


def norm_kernel(_, start_ref, added_ref, gain_ref, *out_refs):
    values = start_ref[...].astype(WIDE)
    if len(out_refs) == 2:
        values = values + added_ref[...].astype(WIDE)
        out_refs[1][...] = values
    out_refs[0][...] = (values * norm_scale(values) * gain_ref[...]).astype(LOW)


def normed(start, gain, added=None):
    rows, features = start.shape
    block = (rows // 2, features)
    outs = [(jax.ShapeDtypeStruct((rows, features), kind), block, down) for kind in (LOW, WIDE)]
    return call_blocks(
        norm_kernel,
        2,
        jnp.zeros((1,), jnp.int32),
        [(block, down), (block, down), ((1, features), whole)],
        outs if added is not None else outs[:1],
        (start, start if added is None else added, gain[None]),
        ROOM,
    )


def norm_back_kernel(_, start_ref, grad_ref, added_ref, gain_ref, low_ref, total_ref, gain_grad_ref):
    values, grad = start_ref[...], grad_ref[...].astype(WIDE)
    scale = norm_scale(values)
    total = added_ref[...].astype(WIDE) + norm_back(values, scale, gain_ref[...], grad)
    total_ref[...] = total
    low_ref[...] = total.astype(LOW)
    part = jnp.sum(grad * values * scale, axis=0, keepdims=True)

    @pl.when(pl.program_id(0) == 0)
    def _():
        gain_grad_ref[...] = part

    @pl.when(pl.program_id(0) > 0)
    def _():
        gain_grad_ref[...] += part


def normed_back(start, grad, added, gain):
    rows, features = start.shape
    block = (rows // 2, features)
    line = (1, features)
    return call_blocks(
        norm_back_kernel,
        2,
        jnp.zeros((1,), jnp.int32),
        [(block, down)] * 3 + [(line, whole)],
        [(jax.ShapeDtypeStruct((rows, features), kind), block, down) for kind in (LOW, WIDE)]
        + [(jax.ShapeDtypeStruct(line, WIDE), line, whole)],
        (start, grad, added, gain[None]),
        ROOM,
    )


def spread_blocks(weights):
    heads, size, _ = weights.shape
    full = jnp.zeros((heads, size, heads, size), weights.dtype)
    for h in range(heads):
        full = full.at[h, :, h, :].set(weights[h])
    return full.reshape(heads * size, heads * size)


def sum_rows(values):
    return lax.psum_scatter(values.astype(LOW), "mp", scatter_dimension=0, tiled=True)


def all_rows(values):
    return lax.all_gather(values, "mp", axis=0, tiled=True)


def place_kernel(count, axis, splits, kept, spots_ref, *refs):
    sources, outs, refs = refs[:count], refs[count + kept : count + kept + len(splits)], refs[count + kept + len(splits) :]
    in_sems, out_sems = refs[-2:]
    size = sources[0].shape[axis]
    same = sources[0].dtype == outs[0].dtype
    held, wide = ((), ()) if same else (refs[:count], refs[count : 2 * count])
    arrivals = [pltpu.make_async_copy(sources[k], held[k], in_sems.at[k]) for k in range(len(held))]
    for arrival in arrivals:
        arrival.start()
    departures = []
    for k in range(count):
        if not same:
            arrivals[k].wait()
            wide[k][...] = held[k][...].astype(wide[k].dtype)
        here = pl.ds(pl.multiple_of(spots_ref[k] * size, size), size)
        start = 0
        for j, rows in enumerate(splits):
            part = (sources[k] if same else wide[k]).at[pl.ds(start, rows), :]
            target = outs[j].at[here, :] if axis == 0 else outs[j].at[:, here]
            departures.append(pltpu.make_async_copy(part, target, out_sems.at[k * len(splits) + j]))
            departures[-1].start()
            start += rows
    for departure in departures:
        departure.wait()


def place(pieces, spots, total, axis, splits, kind, onto=()):
    count = len(pieces)
    rows, columns = pieces[0].shape
    splits = splits or (rows,)
    outs = [
        jax.ShapeDtypeStruct((r * total, columns) if axis == 0 else (r, columns * total), kind) for r in splits
    ]
    anywhere = pl.BlockSpec(memory_space=pl.ANY)
    scratch = [] if pieces[0].dtype == kind else [pltpu.VMEM((rows, columns), LOW)] * count + [pltpu.VMEM((rows, columns), kind)] * count
    return pl.pallas_call(
        lambda *refs: place_kernel(count, axis, splits, len(onto), *refs),
        in_specs=[pl.BlockSpec(memory_space=pltpu.SMEM)] + [anywhere] * (count + len(onto)),
        out_specs=[anywhere] * len(outs),
        out_shape=outs,
        scratch_shapes=scratch
        + [pltpu.SemaphoreType.DMA((count,)), pltpu.SemaphoreType.DMA((count * len(splits),))],
        input_output_aliases={1 + count + k: k for k in range(len(onto))},
        compiler_params=pltpu.CompilerParams(vmem_limit_bytes=rows * columns * 6 * count + 4 * 1024 * 1024),
        cost_estimate=NO_COST,
    )(jnp.stack(spots).astype(jnp.int32), *pieces, *onto)


def dp_bits():
    return lax.axis_size("dp").bit_length() - 1


def swap(values, bit):
    count = lax.axis_size("dp")
    return lax.ppermute(values, "dp", [(i, i ^ (1 << bit)) for i in range(count)])


def order_of(turn):
    bits = dp_bits()
    return [(turn + k) % bits for k in range(bits)]


def upper_of(bit):
    return (lax.axis_index("dp") >> bit) & 1


def quarter_spots():
    left, right = (upper_of(order_of(turn)[0]) for turn in range(2))
    return jnp.stack([1 - left, left, 3 - right, 2 + right]).astype(jnp.int32)


def halves(values, axis):
    size = values.shape[axis] // 2
    return lax.slice_in_dim(values, 0, size, axis=axis), lax.slice_in_dim(values, size, 2 * size, axis=axis)


def split_for(values, axis, bit):
    first, second = halves(values, axis)
    upper = upper_of(bit) == 1
    return jnp.where(upper, first, second), jnp.where(upper, second, first)


class Part:
    def __init__(self, send, kept, axis, turn):
        self.send, self.kept = send, kept
        self.axis, self.order = axis, order_of(turn)
        self.step = 0

    def reduce(self):
        return swap(self.send, self.order[self.step])

    def land(self, got):
        self.step += 1
        if self.step < len(self.order):
            pairs = [split_for(values, self.axis, self.order[self.step]) for values in (self.kept, got)]
            self.send, self.kept = (
                (left.astype(WIDE) + right.astype(WIDE)).astype(LOW) for left, right in zip(*pairs)
            )
        else:
            self.pieces = {0: (self.kept.astype(WIDE) + got.astype(WIDE)).astype(LOW)}

    def forwards(self, level):
        made = []
        for chosen in itertools.combinations(reversed(self.order), level):
            made.append((sum(1 << bit for bit in chosen[:-1]), chosen[-1]))
        return made

    def spot(self, mask):
        owner = lax.axis_index("dp") ^ mask
        bits = len(self.order)
        return sum(((owner >> self.order[k]) & 1) << (bits - 1 - k) for k in range(bits))


def start_gather(parts, level):
    return [(part, mask ^ (1 << bit), swap(part.pieces[mask], bit)) for part in parts for mask, bit in part.forwards(level)]


def exchange(reducing=(), gathered=(), extras=()):
    gots = [part.reduce() for part in reducing]
    made = lax.optimization_barrier(
        (*[part.kept for part in reducing], *gots, *[piece for _, _, piece in gathered], *extras)
    )
    for part, kept in zip(reducing, made):
        part.kept = kept
    made = made[len(gots) :]
    for part, got in zip(reducing, made):
        part.land(got)
    made = made[len(gots) :]
    for (part, mask, _), piece in zip(gathered, made):
        part.pieces[mask] = piece
    return made[len(gathered) :]


def reduce_fully(parts):
    while parts[0].step < len(parts[0].order):
        exchange(parts)


def gather_fully(parts, level):
    for more in range(level, dp_bits() + 1):
        exchange(gathered=start_gather(parts, more))


def finish(parts, axis, splits=None, masks=None, onto=()):
    count = 1 << dp_bits()
    chosen = [(turn, mask) for turn, part in enumerate(parts) for mask in part.pieces if masks is None or mask in masks]
    spots = [parts[turn].spot(mask) + turn * count for turn, mask in chosen]
    blocks = [parts[turn].pieces[mask] for turn, mask in chosen]
    return place(blocks, spots, len(parts) * count, axis, splits, WIDE, onto)


def column_parts(quarters):
    return [Part(quarters[2 * turn], quarters[2 * turn + 1], 1, turn) for turn in range(2)]


def next_chip(values, step):
    count = lax.axis_size("mp")
    return lax.ppermute(values, "mp", [(i, (i + 2 * step) % count) for i in range(count)])


def other_core(values):
    return lax.ppermute(values, "mp", [(i, i ^ 1) for i in range(lax.axis_size("mp"))])


def tie(values, *others):
    return lax.optimization_barrier((values,) + others)[0]


def local(
    tokens,
    lengths,
    first_gain,
    branch_gate,
    branch_input,
    conv_weight,
    conv_bias,
    rate_weight,
    rate_bias,
    inlet_weight,
    inlet_bias,
    decay_param,
    block_out,
    second_gain,
    gate_weight,
    up_weight,
    down_weight,
    out_grad,
):
    heads = rate_weight.shape[0]
    width = decay_param.shape[0]
    features = tokens.shape[1]
    taps_count = conv_weight.shape[0]
    own_count = tokens.shape[0]
    own_input = tokens.astype(WIDE)
    own_grad = out_grad.astype(WIDE)
    first_rows = all_rows(normed(tokens, first_gain)[0])
    soft = DECAY_SCALE * jax.nn.softplus(decay_param)
    slope = DECAY_SCALE * jax.nn.sigmoid(decay_param)
    extra = jnp.stack([conv_bias, rate_bias, inlet_bias, soft, slope])
    rate_w = spread_blocks(rate_weight)
    inlet_w = spread_blocks(inlet_weight)
    branches = jnp.concatenate([branch_gate.T, branch_input.T])

    scalars = jnp.concatenate([quarter_spots(), lengths[0]])[None]
    first_rows = tie(first_rows, rate_w, inlet_w, extra, branches, scalars)
    block_partial, mixed, conv, rate, inlet, state, both = forward_mix(
        scalars, first_rows, branches, block_out, conv_weight, rate_w, inlet_w, extra
    )
    chips = lax.axis_size("mp") // 2
    onward, backward = {0: tie(out_grad, first_rows)}, {}
    onward[1], backward[1] = next_chip(onward[0], 1), next_chip(onward[0], -1)
    block_partial, onward[1], backward[1] = lax.optimization_barrier((block_partial, onward[1], backward[1]))

    block_sum = sum_rows(block_partial)
    for hop in range(2, chips // 2 + 1):
        onward[hop] = next_chip(onward[hop - 1], 1)
        if 2 * hop < chips:
            backward[hop] = next_chip(backward[hop - 1], -1)
    shards = {hop: piece for hop, piece in onward.items()} | {-hop: piece for hop, piece in backward.items()}
    near_hops = [hop for hop in shards if abs(hop) < 2]
    far_hops = [hop for hop in shards if abs(hop) >= 2]
    made = lax.optimization_barrier(
        (block_sum, *[shards[hop] for hop in far_hops], *[other_core(shards[hop]) for hop in near_hops])
    )
    block_sum = made[0]
    shards |= dict(zip(far_hops, made[1:]))
    others = dict(zip(near_hops, made[1 + len(far_hops) :])) | {hop: other_core(shards[hop]) for hop in far_hops}
    own_second, own_middle = normed(tokens, second_gain, block_sum)
    second_rows = all_rows(own_second)
    me = lax.axis_index("mp")
    blocks, places = [], []
    for hop in shards:
        base = 2 * ((me // 2 + chips - hop) % chips)
        blocks += [shards[hop], others[hop]]
        places += [base + me % 2, base + 1 - me % 2]
    (grad_rows,) = place(blocks, places, 2 * chips, 0, None, LOW)
    d_hidden = times_transposed(grad_rows, down_weight)
    second_rows, d_hidden = lax.optimization_barrier((second_rows, d_hidden))
    gate_act = times(second_rows, gate_weight)
    up_act = times(second_rows, up_weight)
    hidden = (gelu(gate_act) * up_act).astype(LOW)
    down_parts = []
    for turn, half in enumerate(halves(transposed_times(hidden, grad_rows).astype(LOW), 1)):
        down_parts.append(Part(*split_for(half, 1, order_of(turn)[0]), 1, turn))
    gate_act, up_act, d_hidden = lax.optimization_barrier(
        (gate_act, up_act, d_hidden, *[part.send for part in down_parts])
    )[:3]
    value, bend = gelu_pair(gate_act)
    gate_low = (d_hidden * up_act * bend).astype(LOW)
    up_low = (d_hidden * value).astype(LOW)

    late_rows = tie(second_rows, *[part.send for part in down_parts])
    uppers = [upper_of(order_of(turn)[0]) for turn in range(2)]
    spots = jnp.stack([1 - upper for upper in uppers]).astype(jnp.int32)
    made = early_products(late_rows, gate_low, up_low, gate_weight, up_weight, spots)
    partial, gate_send, up_send = exchange(down_parts, extras=made)

    second_input = sum_rows(partial)
    late_rows = tie(second_rows, partial)
    wide_parts = [
        Part(gate_send, gradient_half(late_rows, gate_low, uppers[0]), 0, 0),
        Part(up_send, gradient_half(late_rows, up_low, uppers[1]), 0, 1),
    ]
    mlp = down_parts + wide_parts
    middle_low, middle_grad, second_gain_grad = normed_back(own_middle, second_input, out_grad, second_gain)
    made = exchange(down_parts + wide_parts, extras=(middle_low, middle_grad, second_gain_grad))
    middle_low, middle_grad, second_gain_grad = made
    middle_rows = all_rows(middle_low)

    reduce_fully(down_parts)
    out_partial = times(tie(hidden, middle_low), down_weight)
    middle_rows, out_partial = exchange(wide_parts, start_gather(down_parts, 1), (middle_rows, out_partial))
    out_sum = sum_rows(out_partial)

    reduce_fully(wide_parts)
    owners = lax.axis_size("mp")
    made = backward_mix(
        heads,
        owners,
        scalars,
        (middle_rows, block_out, both, conv, rate, inlet, state, mixed, first_rows, branches),
        (conv_weight, rate_w, inlet_w, extra, first_gain[None], second_gain_grad),
    )
    first_partial, *quarters = made
    (first_partial,) = exchange(gathered=start_gather(wide_parts, 1), extras=(first_partial,))
    first_input = sum_rows(first_partial)
    output = (own_middle + out_sum.astype(WIDE)).astype(LOW)

    late = column_parts(quarters)
    wide_rest = start_gather(wide_parts, 2)
    exchange(late)
    down_rest = start_gather(down_parts, 2)
    (first_input,) = exchange(late, wide_rest + down_rest, (first_input,))
    gather_fully(mlp, 3)
    reduce_fully(late)
    first_input = first_input.astype(WIDE)
    first_scale = norm_scale(own_input)
    sums = first_input[own_count:]
    gains = jnp.stack([sums[0] + sums[1], sums[2] + sums[3]])
    input_grad = middle_grad + norm_back(own_input, first_scale, first_gain, first_input[:own_count])
    (gate_grad,) = finish([wide_parts[0]], 0)
    (up_grad,) = finish([wide_parts[1]], 0)
    (down_grad,) = finish(down_parts, 1)
    gate_grad, down_grad, input_grad, other = exchange(
        gathered=start_gather(late, 1), extras=(gate_grad, down_grad, input_grad, swap(gains, 0))
    )
    gains = gains + other
    own = [0] + [1 << bit for bit in range(dp_bits())]
    splits = (width, width, width, quarters[0].shape[0] - 3 * width)
    halfway = finish(late, 1, splits, own)
    made = exchange(gathered=start_gather(late, 2), extras=(swap(gains, 1), up_grad, *halfway, output))
    gather_fully(late, 3)
    gains, up_grad, output = gains + made[0], made[1], made[-1]
    for bit in range(2, dp_bits()):
        gains = gains + swap(gains, bit)
    rest = [mask for mask in late[0].pieces if mask not in own]
    branch_gate_grad, branch_input_grad, block_grad, packed = finish(late, 1, splits, rest, made[2:-1])
    square, taps_grad, *lines = unpack_strips(packed, heads, width // heads)
    square = square.reshape(2, heads, *square.shape[1:])
    return (
        output,
        input_grad,
        gains[0],
        branch_gate_grad.T,
        branch_input_grad.T,
        taps_grad,
        lines[0],
        square[0],
        lines[1],
        square[1],
        lines[2],
        lines[3],
        block_grad,
        gains[1],
        gate_grad,
        up_grad,
        down_grad,
    )


def solution(mesh):
    rows = P(("dp", "mp"), None)
    out_columns = P(None, "mp")
    out_rows = P("mp", None)
    blocks = P("mp", None, None)
    vector = P("mp")
    in_specs = (
        rows, P("dp", None), P(), out_columns, out_columns, out_columns, vector, blocks, vector, blocks,
        vector, vector, out_rows, P(), out_columns, out_columns, out_rows, rows,
    )
    out_specs = (
        rows, rows, P(), out_columns, out_columns, out_columns, vector, blocks, vector, blocks,
        vector, vector, out_rows, P(), out_columns, out_columns, out_rows,
    )
    return jax.shard_map(local, mesh=mesh, in_specs=in_specs, out_specs=out_specs, check_vma=False)
```

```python
import itertools

import jax
import jax.numpy as jnp
from jax import lax
from jax.experimental import pallas as pl
from jax.experimental.pallas import tpu as pltpu
from jax.sharding import PartitionSpec as P

EPS = 1e-06
DECAY_SCALE = 8.0
GELU_RATE = 0.7978845608028654
GELU_CUBE = 0.044715
CHUNK = 48
SUB = 8
LOW = jnp.bfloat16
WIDE = jnp.float32
NO_COST = pl.CostEstimate(flops=0, bytes_accessed=0, transcendentals=0)
ROWS = 256
SPARE = 16
ROOM = 60
TILE = 512
LOAD = 384


def times(left, right):
    return jnp.dot(left, right, preferred_element_type=WIDE)


def times_transposed(left, right):
    return lax.dot_general(left, right, (((1,), (1,)), ((), ())), preferred_element_type=WIDE)


def transposed_times(left, right):
    return lax.dot_general(left, right, (((0,), (0,)), ((), ())), preferred_element_type=WIDE)


def gelu(v):
    return 0.5 * v * (1.0 + jnp.tanh(GELU_RATE * (v + GELU_CUBE * v * v * v)))


def gelu_pair(v):
    square = v * v
    bend = jnp.tanh(GELU_RATE * v * (1.0 + GELU_CUBE * square))
    half = 0.5 * (1.0 + bend)
    slope = half + 0.5 * v * (1.0 - bend * bend) * (GELU_RATE + 3.0 * GELU_RATE * GELU_CUBE * square)
    return v * half, slope


def norm_scale(values):
    return lax.rsqrt(jnp.mean(values * values, axis=-1, keepdims=True) + EPS)


def norm_back(values, scale, gain, grad):
    unit = values * scale
    lifted = gain * grad
    return scale * (lifted - unit * jnp.mean(lifted * unit, axis=-1, keepdims=True))


def one_minus_square(carry, y):
    series = 1.0 - y * (1.0 / 6.0)
    for order in range(5, 1, -1):
        series = 1.0 - y * (1.0 / order) * series
    return jnp.where(y < 0.25, y * series, 1.0 - carry * carry)


def row_positions(scalars_ref, base, rows, width):
    places = base + lax.broadcasted_iota(jnp.int32, (rows, width), 0)
    first = jnp.zeros_like(places)
    start = jnp.int32(0)
    for at in range(4, scalars_ref.shape[1] - 1):
        start = start + scalars_ref[0, at]
        first = jnp.where(places >= start, start, first)
    return places - first


def gates(rate, inlet, soft, fresh):
    log_a = -rate * soft
    carry = jnp.exp(log_a)
    scale = jnp.where(fresh, 1.0, jnp.sqrt(one_minus_square(carry, -2.0 * log_a)))
    return jnp.where(fresh, 0.0, carry), scale


def forward_kernel(scalars_ref, *refs):
    sources, (taps_ref, rate_w_ref, inlet_w_ref, extra_ref), refs = refs[:3], refs[3:7], refs[7:]
    out_refs, refs = refs[:7], refs[7:]
    first_ref, branches_ref, block_ref = refs[:3]
    partial_ref, mixed_ref, conv_ref, rate_ref, inlet_ref, state_ref, both_ref = refs[3:10]
    padded_ref, in_sems, out_sems = refs[10:]
    count, width = mixed_ref.shape
    features = first_ref.shape[1]
    pieces = count // LOAD
    arrivals = [
        *[
            pltpu.make_async_copy(
                sources[1].at[pl.ds(k * width, width), :], branches_ref.at[pl.ds(k * width, width), :], in_sems.at[pieces + k]
            )
            for k in range(2)
        ],
        *[
            pltpu.make_async_copy(sources[0].at[pl.ds(k * LOAD, LOAD), :], first_ref.at[pl.ds(k * LOAD, LOAD), :], in_sems.at[k])
            for k in range(pieces)
        ],
        pltpu.make_async_copy(sources[2], block_ref, in_sems.at[pieces + 2]),
    ]
    for arrival in arrivals:
        arrival.start()
    for arrival in arrivals[:2]:
        arrival.wait()
    for k in range(pieces):
        arrivals[2 + k].wait()
        here = pl.ds(k * LOAD, LOAD)
        both_ref[here, :] = times_transposed(first_ref[here, :], branches_ref[...])
    departures = [pltpu.make_async_copy(both_ref, out_refs[6], out_sems.at[0])]
    departures[0].start()

    padded_ref[pl.ds(0, SUB), :] = jnp.zeros((SUB, width), WIDE)
    padded_ref[pl.ds(SUB, count), :] = both_ref[:, width:]
    state_ref[pl.ds(0, SUB), :] = jnp.zeros((SUB, width), WIDE)
    taps = taps_ref[...]
    bias, rate_b, inlet_b, soft = (extra_ref[k : k + 1, :] for k in range(4))
    lanes = lax.broadcasted_iota(jnp.int32, (CHUNK, width), 0) % SUB

    def convolve(at, _):
        base = pl.multiple_of(at * CHUNK, SUB)
        pos = row_positions(scalars_ref, base, CHUNK, width)
        window = padded_ref[pl.ds(base, CHUNK + SUB), :]
        total = bias + taps[0:1] * window[SUB:]
        for k in range(1, taps.shape[0]):
            moved = window[SUB - k : SUB - k + CHUNK]
            total = total + jnp.where(pos >= k, taps[k : k + 1] * moved, 0.0)
        conv_ref[pl.ds(base, CHUNK), :] = total.astype(LOW)
        return _

    lax.fori_loop(0, count // CHUNK, convolve, 0)

    rate_ref[...] = jax.nn.sigmoid(times(conv_ref[...], rate_w_ref[...]) + rate_b)
    inlet_ref[...] = jax.nn.sigmoid(times(conv_ref[...], inlet_w_ref[...]) + inlet_b)
    for k, (ref, out_ref) in enumerate(((conv_ref, out_refs[2]), (rate_ref, out_refs[3]), (inlet_ref, out_refs[4]))):
        departures.append(pltpu.make_async_copy(ref, out_ref, out_sems.at[1 + k]))
        departures[-1].start()

    def step(at, before):
        base = pl.multiple_of(at * CHUNK, SUB)
        here = pl.ds(base, CHUNK)
        pos = row_positions(scalars_ref, base, CHUNK, width)
        a, scale = gates(rate_ref[here, :], inlet_ref[here, :], soft, pos == 0)
        b = scale * inlet_ref[here, :] * conv_ref[here, :].astype(WIDE)
        for k in (1, 2, 4):
            inside = lanes >= k
            b = b + jnp.where(inside, a * pltpu.roll(b, k, 0), 0.0)
            a = jnp.where(inside, a * pltpu.roll(a, k, 0), a)
        tiles = []
        for j in range(CHUNK // SUB):
            part = slice(j * SUB, (j + 1) * SUB)
            tile = a[part] * before + b[part]
            before = tile[SUB - 1 : SUB]
            tiles.append(tile)
        state = jnp.concatenate(tiles, axis=0)
        state_ref[pl.ds(base + SUB, CHUNK), :] = state
        mixed_ref[here, :] = (state * gelu(both_ref[here, :width])).astype(LOW)
        return before

    lax.fori_loop(0, count // CHUNK, step, jnp.zeros((1, width), WIDE))
    for k, (ref, out_ref) in enumerate(((mixed_ref, out_refs[1]), (state_ref, out_refs[5]))):
        departures.append(pltpu.make_async_copy(ref, out_ref, out_sems.at[4 + k]))
        departures[-1].start()
    arrivals[-1].wait()
    for k in range(features // TILE):
        here = pl.ds(k * TILE, TILE)
        partial_ref[:, here] = times(mixed_ref[...], block_ref[:, here]).astype(LOW)
        departures.append(pltpu.make_async_copy(partial_ref.at[:, here], out_refs[0].at[:, here], out_sems.at[6 + k]))
        departures[-1].start()
    for departure in departures:
        departure.wait()


def backward_kernel(heads, owners, scalars_ref, *refs):
    sources, small_refs, refs = refs[:10], refs[10:16], refs[16:]
    partial_out_ref, quarter_out_refs, held, refs = refs[0], refs[1:5], refs[5:15], refs[15:]
    grad_ref, back_ref, padded_ref, rate_low_ref, inlet_low_ref, stacked_ref, strips_ref = refs[:7]
    partials_ref, quarters_ref, in_sems, out_sems = refs[7:]
    taps_ref, rate_w_ref, inlet_w_ref, extra_ref, first_gain_ref, second_grad_ref = small_refs
    middle_ref, block_ref, both_ref, conv_ref, rate_ref, inlet_ref, state_ref, mixed_ref, first_ref, branches_ref = held
    arrivals = [pltpu.make_async_copy(*pair, in_sems.at[k]) for k, pair in enumerate(zip(sources, held))]
    for arrival in arrivals:
        arrival.start()
    for arrival in arrivals[:2]:
        arrival.wait()
    count, width = grad_ref.shape
    features = middle_ref.shape[1]

    def spread_rows(turn, _):
        here = pl.ds(pl.multiple_of(turn * ROWS, ROWS), ROWS)
        grad_ref[here, :] = times_transposed(middle_ref[here, :], block_ref[...])
        return _

    lax.fori_loop(0, count // ROWS, spread_rows, 0)
    for arrival in arrivals[2:7]:
        arrival.wait()
    padded_ref[pl.ds(0, SUB), :] = jnp.zeros((SUB, width), WIDE)
    padded_ref[pl.ds(SUB, count), :] = both_ref[:, width:]
    taps = taps_ref[...]
    soft = extra_ref[3:4, :]
    slope = extra_ref[4:5, :]
    lanes = lax.broadcasted_iota(jnp.int32, (CHUNK, width), 0) % SUB
    steps = count // CHUNK
    zero = jnp.zeros((1, width), WIDE)

    def column(values):
        return jnp.sum(values, axis=0, keepdims=True)

    def step(turn, held):
        after, late, beyond, sums = held
        base = pl.multiple_of((steps - 1 - turn) * CHUNK, SUB)
        here = pl.ds(base, CHUNK)
        wide_pos = row_positions(scalars_ref, base, CHUNK + SUB, width)
        pos = wide_pos[:CHUNK]
        fresh = pos == 0
        grad = grad_ref[here, :]
        value, bend = gelu_pair(both_ref[here, :width])
        window = state_ref[pl.ds(base, CHUNK + SUB), :]
        state = window[SUB:]
        earlier = window[SUB - 1 : SUB - 1 + CHUNK]
        back_ref[here, :width] = (grad * state * bend).astype(LOW)
        rate = rate_ref[here, :]
        inlet = inlet_ref[here, :]
        conv = conv_ref[here, :]
        conv_wide = conv.astype(WIDE)
        carry, scale = gates(rate, inlet, soft, fresh)
        b = grad * value
        a = jnp.concatenate([carry[1:], late], axis=0)
        for k in (1, 2, 4):
            inside = lanes < SUB - k
            b = b + jnp.where(inside, a * pltpu.roll(b, CHUNK - k, 0), 0.0)
            a = jnp.where(inside, a * pltpu.roll(a, CHUNK - k, 0), a)
        tiles = []
        for j in reversed(range(CHUNK // SUB)):
            part = slice(j * SUB, (j + 1) * SUB)
            tile = a[part] * after + b[part]
            after = tile[0:1]
            tiles.append(tile)
        total = jnp.concatenate(tiles[::-1], axis=0)
        late = carry[0:1]
        scaled = total * scale
        d_inlet = scaled * conv_wide
        d_scale = total * inlet * conv_wide
        d_log = jnp.where(fresh, 0.0, total * earlier * carry - d_scale * (carry * carry) / scale)
        leak = rate * d_log
        rate_low = (-soft * leak * (1.0 - rate)).astype(LOW)
        inlet_low = (d_inlet * inlet * (1.0 - inlet)).astype(LOW)
        rate_low_ref[here, :] = rate_low
        inlet_low_ref[here, :] = inlet_low
        spread = (
            scaled * inlet
            + times_transposed(rate_low, rate_w_ref[...])
            + times_transposed(inlet_low, inlet_w_ref[...])
        )
        ahead = jnp.concatenate([spread, beyond], axis=0)
        back = taps[0:1] * spread
        source = padded_ref[pl.ds(base, CHUNK + SUB), :]
        new = [column(spread), column(rate_low.astype(WIDE)), column(inlet_low.astype(WIDE)), column(leak)]
        new.append(column(spread * source[SUB:]))
        for k in range(1, taps.shape[0]):
            kept = jnp.where(wide_pos >= k, ahead, 0.0)
            back = back + taps[k : k + 1] * kept[k : k + CHUNK]
            new.append(column(kept[:CHUNK] * source[SUB - k : SUB - k + CHUNK]))
        back_ref[here, width:] = back.astype(LOW)
        return after, late, spread[:SUB], tuple(x + y for x, y in zip(sums, new))

    start = tuple(zero for _ in range(4 + taps.shape[0]))
    sums = lax.fori_loop(0, steps, step, (zero, zero, jnp.zeros((SUB, width), WIDE), start))[3]
    rows = list(sums)
    rows[3] = -slope * rows[3]
    size = width // heads
    strips, depth = strip_shape(features, heads, size, len(rows))
    stacked_ref[...] = jnp.zeros_like(stacked_ref)
    block = 0
    for low_ref in (rate_low_ref, inlet_low_ref):
        full = transposed_times(conv_ref[...], low_ref[...])
        for h in range(heads):
            part = slice(h * size, (h + 1) * size)
            stacked_ref[pl.ds(block * size, size), :] = full[part, part]
            block += 1
    small = jnp.concatenate(rows, axis=0)
    for h in range(heads):
        stacked_ref[pl.ds(block * size + h * SUB, len(rows)), :] = small[:, h * size : (h + 1) * size]
    strips_ref[...] = jnp.zeros_like(strips_ref)
    for k in range(strips):
        strips_ref[:, k * size : (k + 1) * size] = stacked_ref[pl.ds(k * depth, depth), :].astype(LOW)

    for arrival in arrivals[7:]:
        arrival.wait()
    share = count // owners
    quarter = features // 4
    departures = []
    for slot in range(4):
        if slot >= 2:
            for departure in departures[slot - 2]:
                departure.wait()
        partial_ref, quarter_ref = partials_ref.at[slot % 2], quarters_ref.at[slot % 2]
        here = pl.ds(pl.multiple_of(scalars_ref[0, slot] * quarter, quarter), quarter)
        branch_grad = transposed_times(back_ref[...], first_ref[:, here])
        quarter_ref[: 2 * width, :] = branch_grad.astype(LOW)
        quarter_ref[2 * width : 3 * width, :] = transposed_times(mixed_ref[...], middle_ref[:, here]).astype(LOW)
        quarter_ref[3 * width :, :] = strips_ref[:, here]
        gain = column(branch_grad * branches_ref[:, here].astype(WIDE)) / first_gain_ref[:, here]
        tops = []
        for value in (gain, second_grad_ref[:, here]):
            top = value.astype(LOW).astype(WIDE)
            tops += [top, value - top]
        tops = jnp.concatenate(tops + [jnp.zeros((SPARE - len(tops), quarter), WIDE)], axis=0).astype(LOW)
        partial = times(back_ref[...], branches_ref[:, here]).astype(LOW)
        for k in range(owners):
            base = k * (share + SPARE)
            partial_ref[base : base + share, :] = partial[k * share : (k + 1) * share]
            partial_ref[base + share : base + share + SPARE, :] = tops
        departures.append(
            [
                pltpu.make_async_copy(quarter_ref, quarter_out_refs[slot], out_sems.at[2 * slot]),
                pltpu.make_async_copy(partial_ref, partial_out_ref.at[:, here], out_sems.at[2 * slot + 1]),
            ]
        )
        for departure in departures[slot]:
            departure.start()
    for slot in (2, 3):
        for departure in departures[slot]:
            departure.wait()


def strip_shape(features, heads, size, small):
    strips = features // size
    rows = 2 * heads * size + heads * SUB
    return strips, -(-rows // (strips * 2 * SUB)) * 2 * SUB


def unpack_kernel(heads, strips, packed_ref, rate_ref, inlet_ref, taps_ref, *refs):
    line_refs, stacked_ref = refs[:-1], refs[-1]
    depth, size = packed_ref.shape[0], rate_ref.shape[-1]
    for k in range(strips):
        stacked_ref[pl.ds(k * depth, depth), :] = packed_ref[:, k * size : (k + 1) * size]
    for h in range(heads):
        rate_ref[h] = stacked_ref[pl.ds(h * size, size), :]
        inlet_ref[h] = stacked_ref[pl.ds((heads + h) * size, size), :]
    small = jnp.concatenate(
        [stacked_ref[pl.ds(2 * heads * size + h * SUB, SUB), :] for h in range(heads)], axis=1
    )
    taps_ref[...] = small[len(line_refs) :]
    for k, line_ref in enumerate(line_refs):
        line_ref[...] = small[k]


def unpack_strips(packed, heads, size):
    strips, depth = strip_shape(packed.shape[1], heads, size, SUB)
    return pl.pallas_call(
        lambda *refs: unpack_kernel(heads, strips, *refs),
        out_shape=[
            jax.ShapeDtypeStruct((heads, size, size), WIDE),
            jax.ShapeDtypeStruct((heads, size, size), WIDE),
            jax.ShapeDtypeStruct((SUB - 4, heads * size), WIDE),
        ]
        + [jax.ShapeDtypeStruct((heads * size,), WIDE)] * 4,
        scratch_shapes=[pltpu.VMEM((strips * depth, size), WIDE)],
        compiler_params=pltpu.CompilerParams(vmem_limit_bytes=16 * 1024 * 1024),
        cost_estimate=NO_COST,
    )(packed)


def in_vmem():
    return pl.BlockSpec(memory_space=pltpu.VMEM)


def run_kernel(body, outs, scratch, operands, room):
    return pl.pallas_call(
        body,
        in_specs=[pl.BlockSpec(memory_space=pltpu.SMEM)] + [in_vmem()] * (len(operands) - 1),
        out_specs=[in_vmem()] * len(outs),
        out_shape=outs,
        scratch_shapes=scratch,
        compiler_params=pltpu.CompilerParams(vmem_limit_bytes=room * 1024 * 1024),
        cost_estimate=NO_COST,
    )(*operands)


def forward_mix(scalars, first, branches, block, taps, rate_w, inlet_w, extra):
    count, features = first.shape
    width = block.shape[0]
    made = [
        ((count, features), LOW),
        ((count, width), LOW),
        ((count, width), LOW),
        ((count, width), WIDE),
        ((count, width), WIDE),
        ((count + SUB, width), WIDE),
        ((count, 2 * width), WIDE),
    ]
    anywhere = pl.BlockSpec(memory_space=pl.ANY)
    return pl.pallas_call(
        forward_kernel,
        in_specs=[pl.BlockSpec(memory_space=pltpu.SMEM)] + [anywhere] * 3 + [in_vmem()] * 4,
        out_specs=[anywhere] * len(made),
        out_shape=[jax.ShapeDtypeStruct(*one) for one in made],
        scratch_shapes=[pltpu.VMEM(array.shape, array.dtype) for array in (first, branches, block)]
        + [pltpu.VMEM(*one) for one in made]
        + [
            pltpu.VMEM((count + SUB, width), WIDE),
            pltpu.SemaphoreType.DMA((count // LOAD + 3,)),
            pltpu.SemaphoreType.DMA((6 + features // TILE,)),
        ],
        compiler_params=pltpu.CompilerParams(vmem_limit_bytes=ROOM * 1024 * 1024),
        cost_estimate=NO_COST,
    )(scalars, first, branches, block, taps, rate_w, inlet_w, extra)


def backward_mix(heads, owners, scalars, large, small):
    middle, block = large[:2]
    count, features = middle.shape
    width = block.shape[0]
    size = width // heads
    strips, depth = strip_shape(features, heads, size, SUB)
    rows, lines = count + owners * SPARE, 3 * width + depth
    narrow = pltpu.VMEM((count, width), LOW)
    anywhere = pl.BlockSpec(memory_space=pl.ANY)
    return pl.pallas_call(
        lambda *refs: backward_kernel(heads, owners, *refs),
        in_specs=[pl.BlockSpec(memory_space=pltpu.SMEM)] + [anywhere] * len(large) + [in_vmem()] * len(small),
        out_specs=[anywhere] * 5,
        out_shape=[jax.ShapeDtypeStruct((rows, features), LOW)] + [jax.ShapeDtypeStruct((lines, features // 4), LOW)] * 4,
        scratch_shapes=[pltpu.VMEM(array.shape, array.dtype) for array in large]
        + [
            pltpu.VMEM((count, width), WIDE),
            pltpu.VMEM((count, 2 * width), LOW),
            pltpu.VMEM((count + SUB, width), WIDE),
            narrow,
            narrow,
            pltpu.VMEM((strips * depth, size), WIDE),
            pltpu.VMEM((depth, features), LOW),
            pltpu.VMEM((2, rows, features // 4), LOW),
            pltpu.VMEM((2, lines, features // 4), LOW),
            pltpu.SemaphoreType.DMA((len(large),)),
            pltpu.SemaphoreType.DMA((8,)),
        ],
        compiler_params=pltpu.CompilerParams(vmem_limit_bytes=ROOM * 1024 * 1024),
        cost_estimate=NO_COST,
    )(scalars, *large, *small)


def call_blocks(body, grid, spots, inputs, outputs, operands, room):
    return pl.pallas_call(
        body,
        grid_spec=pltpu.PrefetchScalarGridSpec(
            num_scalar_prefetch=1,
            grid=(grid,),
            in_specs=[pl.BlockSpec(shape, index) for shape, index in inputs],
            out_specs=[pl.BlockSpec(shape, index) for _, shape, index in outputs],
        ),
        out_shape=[made for made, _, _ in outputs],
        compiler_params=pltpu.CompilerParams(vmem_limit_bytes=room * 1024 * 1024),
        cost_estimate=NO_COST,
    )(spots, *operands)


def whole(_, at):
    return (0, 0)


def across(k, at):
    return (0, k)


def down(k, at):
    return (k, 0)


def across_spot(k, at):
    return (0, at[k])


def down_spot(k, at):
    return (at[k], 0)


def early_kernel(spots_ref, *refs):
    rows_hbm, lows_hbm, weights_hbm, refs = refs[0], refs[1:3], refs[3:5], refs[5:]
    partial_hbm, sends_hbm, refs = refs[0], refs[1:3], refs[3:]
    rows_refs, low_refs, weight_refs, partial_ref, send_refs = refs[0:2], refs[2:4], refs[4:6], refs[6], refs[7:9]
    in_sems, out_sems = refs[9:]
    features = partial_ref.shape[1]
    tiles = features // TILE
    half = features // 2
    low_copies = [pltpu.make_async_copy(lows_hbm[k], low_refs[k], in_sems.at[k]) for k in range(2)]
    weight_copies = [
        [
            pltpu.make_async_copy(
                weights_hbm[k].at[pl.ds(t * TILE, TILE), :],
                weight_refs[k].at[pl.ds(t * TILE, TILE), :],
                in_sems.at[2 + 2 * t + k],
            )
            for k in range(2)
        ]
        for t in range(tiles)
    ]
    row_copies = [
        pltpu.make_async_copy(
            rows_hbm.at[:, pl.ds(pl.multiple_of(spots_ref[k] * half, half), half)],
            rows_refs[k],
            in_sems.at[2 + 2 * tiles + k],
        )
        for k in range(2)
    ]
    for copy in low_copies + [copy for pair in weight_copies for copy in pair] + row_copies:
        copy.start()
    for copy in low_copies:
        copy.wait()
    departures = []
    for t in range(tiles):
        here = pl.ds(t * TILE, TILE)
        for copy in weight_copies[t]:
            copy.wait()
        total = times_transposed(low_refs[0][...], weight_refs[0][here, :])
        total += times_transposed(low_refs[1][...], weight_refs[1][here, :])
        partial_ref[:, here] = total.astype(LOW)
        departures.append(pltpu.make_async_copy(partial_ref.at[:, here], partial_hbm.at[:, here], out_sems.at[t]))
        departures[-1].start()
    for k in range(2):
        row_copies[k].wait()
        for t in range(half // TILE):
            here = pl.ds(t * TILE, TILE)
            send_refs[k][here, :] = transposed_times(rows_refs[k][:, here], low_refs[k][...]).astype(LOW)
            departures.append(
                pltpu.make_async_copy(
                    send_refs[k].at[here, :], sends_hbm[k].at[here, :], out_sems.at[tiles + k * (half // TILE) + t]
                )
            )
            departures[-1].start()
    for departure in departures:
        departure.wait()


def early_products(rows, gate_low, up_low, gate_weight, up_weight, spots):
    count, features = rows.shape
    units = gate_low.shape[1]
    half = features // 2
    made = [((count, features), LOW), ((half, units), LOW), ((half, units), LOW)]
    anywhere = pl.BlockSpec(memory_space=pl.ANY)
    return pl.pallas_call(
        early_kernel,
        in_specs=[pl.BlockSpec(memory_space=pltpu.SMEM)] + [anywhere] * 5,
        out_specs=[anywhere] * 3,
        out_shape=[jax.ShapeDtypeStruct(*one) for one in made],
        scratch_shapes=[pltpu.VMEM((count, half), LOW)] * 2
        + [pltpu.VMEM((count, units), LOW)] * 2
        + [pltpu.VMEM((features, units), LOW)] * 2
        + [pltpu.VMEM(*one) for one in made]
        + [
            pltpu.SemaphoreType.DMA((4 + 2 * (features // TILE),)),
            pltpu.SemaphoreType.DMA((2 * (features // TILE),)),
        ],
        compiler_params=pltpu.CompilerParams(vmem_limit_bytes=ROOM * 1024 * 1024),
        cost_estimate=NO_COST,
    )(spots, rows, gate_low, up_low, gate_weight, up_weight)


def gradient_kernel(_, left_ref, right_ref, out_ref):
    out_ref[...] = transposed_times(left_ref[...], right_ref[...]).astype(LOW)


def gradient_half(left, right, which):
    count, features = left.shape
    units = right.shape[1]
    block = features // 4
    spots = jnp.stack([2 * which, 2 * which + 1]).astype(jnp.int32)
    return call_blocks(
        gradient_kernel,
        2,
        spots,
        [((count, block), across_spot), ((count, units), whole)],
        [(jax.ShapeDtypeStruct((2 * block, units), LOW), (block, units), down)],
        (left, right),
        ROOM,
    )[0]


def norm_kernel(_, start_ref, added_ref, gain_ref, *out_refs):
    values = start_ref[...].astype(WIDE)
    if len(out_refs) == 2:
        values = values + added_ref[...].astype(WIDE)
        out_refs[1][...] = values
    out_refs[0][...] = (values * norm_scale(values) * gain_ref[...]).astype(LOW)


def normed(start, gain, added=None):
    rows, features = start.shape
    block = (rows // 2, features)
    outs = [(jax.ShapeDtypeStruct((rows, features), kind), block, down) for kind in (LOW, WIDE)]
    return call_blocks(
        norm_kernel,
        2,
        jnp.zeros((1,), jnp.int32),
        [(block, down), (block, down), ((1, features), whole)],
        outs if added is not None else outs[:1],
        (start, start if added is None else added, gain[None]),
        ROOM,
    )


def norm_back_kernel(_, start_ref, grad_ref, added_ref, gain_ref, low_ref, total_ref, gain_grad_ref):
    values, grad = start_ref[...], grad_ref[...].astype(WIDE)
    scale = norm_scale(values)
    total = added_ref[...].astype(WIDE) + norm_back(values, scale, gain_ref[...], grad)
    total_ref[...] = total
    low_ref[...] = total.astype(LOW)
    part = jnp.sum(grad * values * scale, axis=0, keepdims=True)

    @pl.when(pl.program_id(0) == 0)
    def _():
        gain_grad_ref[...] = part

    @pl.when(pl.program_id(0) > 0)
    def _():
        gain_grad_ref[...] += part


def normed_back(start, grad, added, gain):
    rows, features = start.shape
    block = (rows // 2, features)
    line = (1, features)
    return call_blocks(
        norm_back_kernel,
        2,
        jnp.zeros((1,), jnp.int32),
        [(block, down)] * 3 + [(line, whole)],
        [(jax.ShapeDtypeStruct((rows, features), kind), block, down) for kind in (LOW, WIDE)]
        + [(jax.ShapeDtypeStruct(line, WIDE), line, whole)],
        (start, grad, added, gain[None]),
        ROOM,
    )


def spread_blocks(weights):
    heads, size, _ = weights.shape
    full = jnp.zeros((heads, size, heads, size), weights.dtype)
    for h in range(heads):
        full = full.at[h, :, h, :].set(weights[h])
    return full.reshape(heads * size, heads * size)


def sum_rows(values):
    return lax.psum_scatter(values.astype(LOW), "mp", scatter_dimension=0, tiled=True)


def all_rows(values):
    return lax.all_gather(values, "mp", axis=0, tiled=True)


def place_kernel(count, axis, splits, kept, spots_ref, *refs):
    sources, outs, refs = refs[:count], refs[count + kept : count + kept + len(splits)], refs[count + kept + len(splits) :]
    in_sems, out_sems = refs[-2:]
    size = sources[0].shape[axis]
    same = sources[0].dtype == outs[0].dtype
    held, wide = ((), ()) if same else (refs[:count], refs[count : 2 * count])
    arrivals = [pltpu.make_async_copy(sources[k], held[k], in_sems.at[k]) for k in range(len(held))]
    for arrival in arrivals:
        arrival.start()
    departures = []
    for k in range(count):
        if not same:
            arrivals[k].wait()
            wide[k][...] = held[k][...].astype(wide[k].dtype)
        here = pl.ds(pl.multiple_of(spots_ref[k] * size, size), size)
        start = 0
        for j, rows in enumerate(splits):
            part = (sources[k] if same else wide[k]).at[pl.ds(start, rows), :]
            target = outs[j].at[here, :] if axis == 0 else outs[j].at[:, here]
            departures.append(pltpu.make_async_copy(part, target, out_sems.at[k * len(splits) + j]))
            departures[-1].start()
            start += rows
    for departure in departures:
        departure.wait()


def place(pieces, spots, total, axis, splits, kind, onto=()):
    count = len(pieces)
    rows, columns = pieces[0].shape
    splits = splits or (rows,)
    outs = [
        jax.ShapeDtypeStruct((r * total, columns) if axis == 0 else (r, columns * total), kind) for r in splits
    ]
    anywhere = pl.BlockSpec(memory_space=pl.ANY)
    scratch = [] if pieces[0].dtype == kind else [pltpu.VMEM((rows, columns), LOW)] * count + [pltpu.VMEM((rows, columns), kind)] * count
    return pl.pallas_call(
        lambda *refs: place_kernel(count, axis, splits, len(onto), *refs),
        in_specs=[pl.BlockSpec(memory_space=pltpu.SMEM)] + [anywhere] * (count + len(onto)),
        out_specs=[anywhere] * len(outs),
        out_shape=outs,
        scratch_shapes=scratch
        + [pltpu.SemaphoreType.DMA((count,)), pltpu.SemaphoreType.DMA((count * len(splits),))],
        input_output_aliases={1 + count + k: k for k in range(len(onto))},
        compiler_params=pltpu.CompilerParams(
            vmem_limit_bytes=ROOM * 1024 * 1024 if onto else rows * columns * 6 * count + 4 * 1024 * 1024
        ),
        cost_estimate=NO_COST,
    )(jnp.stack(spots).astype(jnp.int32), *pieces, *onto)


def dp_bits():
    return lax.axis_size("dp").bit_length() - 1


def swap(values, bit):
    count = lax.axis_size("dp")
    return lax.ppermute(values, "dp", [(i, i ^ (1 << bit)) for i in range(count)])


def order_of(turn):
    bits = dp_bits()
    return [(turn + k) % bits for k in range(bits)]


def upper_of(bit):
    return (lax.axis_index("dp") >> bit) & 1


def quarter_spots():
    left, right = (upper_of(order_of(turn)[0]) for turn in range(2))
    return jnp.stack([1 - left, left, 3 - right, 2 + right]).astype(jnp.int32)


def halves(values, axis):
    size = values.shape[axis] // 2
    return lax.slice_in_dim(values, 0, size, axis=axis), lax.slice_in_dim(values, size, 2 * size, axis=axis)


def split_for(values, axis, bit):
    first, second = halves(values, axis)
    upper = upper_of(bit) == 1
    return jnp.where(upper, first, second), jnp.where(upper, second, first)


class Part:
    def __init__(self, send, kept, axis, turn):
        self.send, self.kept = send, kept
        self.axis, self.order = axis, order_of(turn)
        self.step = 0

    def reduce(self):
        return swap(self.send, self.order[self.step])

    def land(self, got):
        self.step += 1
        if self.step < len(self.order):
            bit = self.order[self.step]
            kept, sent = (split_for(values, self.axis, bit)[0] for values in (self.kept, got))
            self.send = (kept.astype(WIDE) + sent.astype(WIDE)).astype(LOW)
            kept, got, _ = lax.optimization_barrier((self.kept, got, self.send))
            kept, got = (split_for(values, self.axis, bit)[1] for values in (kept, got))
            self.kept = (kept.astype(WIDE) + got.astype(WIDE)).astype(LOW)
        else:
            self.pieces = {0: (self.kept.astype(WIDE) + got.astype(WIDE)).astype(LOW)}

    def forwards(self, level):
        made = []
        for chosen in itertools.combinations(reversed(self.order), level):
            made.append((sum(1 << bit for bit in chosen[:-1]), chosen[-1]))
        return made

    def spot(self, mask):
        owner = lax.axis_index("dp") ^ mask
        bits = len(self.order)
        return sum(((owner >> self.order[k]) & 1) << (bits - 1 - k) for k in range(bits))


def start_gather(parts, level):
    return [(part, mask ^ (1 << bit), swap(part.pieces[mask], bit)) for part in parts for mask, bit in part.forwards(level)]


def exchange(reducing=(), gathered=(), extras=()):
    gots = [part.reduce() for part in reducing]
    made = lax.optimization_barrier(
        (*[part.kept for part in reducing], *gots, *[piece for _, _, piece in gathered], *extras)
    )
    for part, kept in zip(reducing, made):
        part.kept = kept
    made = made[len(gots) :]
    for part, got in zip(reducing, made):
        part.land(got)
    made = made[len(gots) :]
    for (part, mask, _), piece in zip(gathered, made):
        part.pieces[mask] = piece
    return made[len(gathered) :]


def reduce_fully(parts):
    while parts[0].step < len(parts[0].order):
        exchange(parts)


def gather_fully(parts, level):
    for more in range(level, dp_bits() + 1):
        exchange(gathered=start_gather(parts, more))


def finish(parts, axis, splits=None, masks=None, onto=()):
    count = 1 << dp_bits()
    chosen = [(turn, mask) for turn, part in enumerate(parts) for mask in part.pieces if masks is None or mask in masks]
    spots = [parts[turn].spot(mask) + turn * count for turn, mask in chosen]
    blocks = [parts[turn].pieces[mask] for turn, mask in chosen]
    return place(blocks, spots, len(parts) * count, axis, splits, WIDE, onto)


def column_parts(quarters):
    return [Part(quarters[2 * turn], quarters[2 * turn + 1], 1, turn) for turn in range(2)]


def next_chip(values, step):
    count = lax.axis_size("mp")
    return lax.ppermute(values, "mp", [(i, (i + 2 * step) % count) for i in range(count)])


def other_core(values):
    return lax.ppermute(values, "mp", [(i, i ^ 1) for i in range(lax.axis_size("mp"))])


def tie(values, *others):
    return lax.optimization_barrier((values,) + others)[0]


def local(
    tokens,
    lengths,
    first_gain,
    branch_gate,
    branch_input,
    conv_weight,
    conv_bias,
    rate_weight,
    rate_bias,
    inlet_weight,
    inlet_bias,
    decay_param,
    block_out,
    second_gain,
    gate_weight,
    up_weight,
    down_weight,
    out_grad,
):
    heads = rate_weight.shape[0]
    width = decay_param.shape[0]
    features = tokens.shape[1]
    taps_count = conv_weight.shape[0]
    own_count = tokens.shape[0]
    own_input = tokens.astype(WIDE)
    own_grad = out_grad.astype(WIDE)
    first_rows = all_rows(normed(tokens, first_gain)[0])
    soft = DECAY_SCALE * jax.nn.softplus(decay_param)
    slope = DECAY_SCALE * jax.nn.sigmoid(decay_param)
    extra = jnp.stack([conv_bias, rate_bias, inlet_bias, soft, slope])
    rate_w = spread_blocks(rate_weight)
    inlet_w = spread_blocks(inlet_weight)
    branches = jnp.concatenate([branch_gate.T, branch_input.T])

    scalars = jnp.concatenate([quarter_spots(), lengths[0]])[None]
    first_rows = tie(first_rows, rate_w, inlet_w, extra, branches, scalars)
    block_partial, mixed, conv, rate, inlet, state, both = forward_mix(
        scalars, first_rows, branches, block_out, conv_weight, rate_w, inlet_w, extra
    )
    chips = lax.axis_size("mp") // 2
    onward, backward = {0: tie(out_grad, first_rows)}, {}
    onward[1], backward[1] = next_chip(onward[0], 1), next_chip(onward[0], -1)
    block_partial, onward[1], backward[1] = lax.optimization_barrier((block_partial, onward[1], backward[1]))

    block_sum = sum_rows(block_partial)
    shards = {hop: piece for hop, piece in onward.items()} | {-hop: piece for hop, piece in backward.items()}
    made = lax.optimization_barrier((block_sum, *[other_core(piece) for piece in shards.values()]))
    block_sum = made[0]
    others = dict(zip(shards, made[1:]))
    own_second, own_middle = normed(tokens, second_gain, block_sum)
    second_rows = all_rows(own_second)

    onward[1], backward[1] = lax.optimization_barrier((onward[1], backward[1], own_second))[:2]
    for hop in range(2, chips // 2 + 1):
        onward[hop] = next_chip(onward[hop - 1], 1)
        shards[hop], others[hop] = onward[hop], other_core(onward[hop])
        if 2 * hop < chips:
            backward[hop] = next_chip(backward[hop - 1], -1)
            shards[-hop], others[-hop] = backward[hop], other_core(backward[hop])
    me = lax.axis_index("mp")
    blocks, places = [], []
    for hop in shards:
        base = 2 * ((me // 2 + chips - hop) % chips)
        blocks += [shards[hop], others[hop]]
        places += [base + me % 2, base + 1 - me % 2]
    (grad_rows,) = place(blocks, places, 2 * chips, 0, None, LOW)
    d_hidden = times_transposed(grad_rows, down_weight)
    second_rows, d_hidden = lax.optimization_barrier((second_rows, d_hidden))
    gate_act = times(second_rows, gate_weight)
    up_act = times(second_rows, up_weight)
    hidden = (gelu(gate_act) * up_act).astype(LOW)
    down_parts = []
    for turn, half in enumerate(halves(transposed_times(hidden, grad_rows).astype(LOW), 1)):
        down_parts.append(Part(*split_for(half, 1, order_of(turn)[0]), 1, turn))
    gate_act, up_act, d_hidden = lax.optimization_barrier(
        (gate_act, up_act, d_hidden, *[part.send for part in down_parts])
    )[:3]
    value, bend = gelu_pair(gate_act)
    gate_low = (d_hidden * up_act * bend).astype(LOW)
    up_low = (d_hidden * value).astype(LOW)

    late_rows = tie(second_rows, *[part.send for part in down_parts])
    uppers = [upper_of(order_of(turn)[0]) for turn in range(2)]
    spots = jnp.stack([1 - upper for upper in uppers]).astype(jnp.int32)
    made = early_products(late_rows, gate_low, up_low, gate_weight, up_weight, spots)
    partial, gate_send, up_send = exchange(down_parts, extras=made)

    second_input = sum_rows(partial)
    late_rows = tie(second_rows, partial)
    wide_parts = [
        Part(gate_send, gradient_half(late_rows, gate_low, uppers[0]), 0, 0),
        Part(up_send, gradient_half(late_rows, up_low, uppers[1]), 0, 1),
    ]
    mlp = down_parts + wide_parts
    middle_low, middle_grad, second_gain_grad = normed_back(own_middle, second_input, out_grad, second_gain)
    made = exchange(down_parts + wide_parts, extras=(middle_low, middle_grad, second_gain_grad))
    middle_low, middle_grad, second_gain_grad = made
    middle_rows = all_rows(middle_low)

    reduce_fully(down_parts)
    out_partial = times(tie(hidden, middle_low), down_weight)
    middle_rows, out_partial = exchange(wide_parts, start_gather(down_parts, 1), (middle_rows, out_partial))
    out_sum = sum_rows(out_partial)

    reduce_fully(wide_parts)
    owners = lax.axis_size("mp")
    made = backward_mix(
        heads,
        owners,
        scalars,
        (middle_rows, block_out, both, conv, rate, inlet, state, mixed, first_rows, branches),
        (conv_weight, rate_w, inlet_w, extra, first_gain[None], second_gain_grad),
    )
    first_partial, *quarters = made
    (first_partial,) = exchange(gathered=start_gather(wide_parts, 1), extras=(first_partial,))
    first_input = sum_rows(first_partial)
    output = (own_middle + out_sum.astype(WIDE)).astype(LOW)

    late = column_parts(quarters)
    wide_rest = start_gather(wide_parts, 2)
    exchange(late)
    down_rest = start_gather(down_parts, 2)
    (first_input,) = exchange(late, wide_rest + down_rest, (first_input,))
    gather_fully(mlp, 3)
    reduce_fully(late)
    first_input = first_input.astype(WIDE)
    first_scale = norm_scale(own_input)
    sums = first_input[own_count:]
    gains = jnp.stack([sums[0] + sums[1], sums[2] + sums[3]])
    input_grad = middle_grad + norm_back(own_input, first_scale, first_gain, first_input[:own_count])
    (gate_grad,) = finish([wide_parts[0]], 0)
    (up_grad,) = finish([wide_parts[1]], 0)
    (down_grad,) = finish(down_parts, 1)
    gate_grad, down_grad, input_grad, other = exchange(
        gathered=start_gather(late, 1), extras=(gate_grad, down_grad, input_grad, swap(gains, 0))
    )
    gains = gains + other
    own = [0] + [1 << bit for bit in range(dp_bits())]
    splits = (width, width, width, quarters[0].shape[0] - 3 * width)
    halfway = finish(late, 1, splits, own)
    made = exchange(gathered=start_gather(late, 2), extras=(swap(gains, 1), up_grad, *halfway, output))
    gather_fully(late, 3)
    gains, up_grad, output = gains + made[0], made[1], made[-1]
    for bit in range(2, dp_bits()):
        gains = gains + swap(gains, bit)
    rest = [mask for mask in late[0].pieces if mask not in own]
    branch_gate_grad, branch_input_grad, block_grad, packed = finish(late, 1, splits, rest, made[2:-1])
    rate_w_grad, inlet_w_grad, taps_grad, *lines = unpack_strips(packed, heads, width // heads)
    return (
        output,
        input_grad,
        gains[0],
        branch_gate_grad.T,
        branch_input_grad.T,
        taps_grad,
        lines[0],
        rate_w_grad,
        lines[1],
        inlet_w_grad,
        lines[2],
        lines[3],
        block_grad,
        gains[1],
        gate_grad,
        up_grad,
        down_grad,
    )


def solution(mesh):
    rows = P(("dp", "mp"), None)
    out_columns = P(None, "mp")
    out_rows = P("mp", None)
    blocks = P("mp", None, None)
    vector = P("mp")
    in_specs = (
        rows, P("dp", None), P(), out_columns, out_columns, out_columns, vector, blocks, vector, blocks,
        vector, vector, out_rows, P(), out_columns, out_columns, out_rows, rows,
    )
    out_specs = (
        rows, rows, P(), out_columns, out_columns, out_columns, vector, blocks, vector, blocks,
        vector, vector, out_rows, P(), out_columns, out_columns, out_rows,
    )
    return jax.shard_map(local, mesh=mesh, in_specs=in_specs, out_specs=out_specs, check_vma=False)
```

```python
import itertools

import jax
import jax.numpy as jnp
from jax import lax
from jax.experimental import pallas as pl
from jax.experimental.pallas import tpu as pltpu
from jax.sharding import PartitionSpec as P

EPS = 1e-06
DECAY_SCALE = 8.0
GELU_RATE = 0.7978845608028654
GELU_CUBE = 0.044715
CHUNK = 48
SUB = 8
LOW = jnp.bfloat16
WIDE = jnp.float32
NO_COST = pl.CostEstimate(flops=0, bytes_accessed=0, transcendentals=0)
ROWS = 256
SPARE = 16
ROOM = 60
TILE = 512
LOAD = 384


def times(left, right):
    return jnp.dot(left, right, preferred_element_type=WIDE)


def times_transposed(left, right):
    return lax.dot_general(left, right, (((1,), (1,)), ((), ())), preferred_element_type=WIDE)


def transposed_times(left, right):
    return lax.dot_general(left, right, (((0,), (0,)), ((), ())), preferred_element_type=WIDE)


def gelu(v):
    return 0.5 * v * (1.0 + jnp.tanh(GELU_RATE * (v + GELU_CUBE * v * v * v)))


def gelu_pair(v):
    square = v * v
    bend = jnp.tanh(GELU_RATE * v * (1.0 + GELU_CUBE * square))
    half = 0.5 * (1.0 + bend)
    slope = half + 0.5 * v * (1.0 - bend * bend) * (GELU_RATE + 3.0 * GELU_RATE * GELU_CUBE * square)
    return v * half, slope


def norm_scale(values):
    return lax.rsqrt(jnp.mean(values * values, axis=-1, keepdims=True) + EPS)


def norm_back(values, scale, gain, grad):
    unit = values * scale
    lifted = gain * grad
    return scale * (lifted - unit * jnp.mean(lifted * unit, axis=-1, keepdims=True))


def one_minus_square(carry, y):
    series = 1.0 - y * (1.0 / 6.0)
    for order in range(5, 1, -1):
        series = 1.0 - y * (1.0 / order) * series
    return jnp.where(y < 0.25, y * series, 1.0 - carry * carry)


def row_positions(scalars_ref, base, rows, width):
    places = base + lax.broadcasted_iota(jnp.int32, (rows, width), 0)
    first = jnp.zeros_like(places)
    start = jnp.int32(0)
    for at in range(4, scalars_ref.shape[1] - 1):
        start = start + scalars_ref[0, at]
        first = jnp.where(places >= start, start, first)
    return places - first


def gates(rate, inlet, soft, fresh):
    log_a = -rate * soft
    carry = jnp.exp(log_a)
    scale = jnp.where(fresh, 1.0, jnp.sqrt(one_minus_square(carry, -2.0 * log_a)))
    return jnp.where(fresh, 0.0, carry), scale


def forward_kernel(scalars_ref, *refs):
    sources, (taps_ref, rate_w_ref, inlet_w_ref, extra_ref), refs = refs[:3], refs[3:7], refs[7:]
    out_refs, refs = refs[:7], refs[7:]
    first_ref, branches_ref, block_ref = refs[:3]
    partial_ref, mixed_ref, conv_ref, rate_ref, inlet_ref, state_ref, both_ref = refs[3:10]
    padded_ref, in_sems, out_sems = refs[10:]
    count, width = mixed_ref.shape
    features = first_ref.shape[1]
    pieces = count // LOAD
    arrivals = [
        *[
            pltpu.make_async_copy(
                sources[1].at[pl.ds(k * width, width), :], branches_ref.at[pl.ds(k * width, width), :], in_sems.at[pieces + k]
            )
            for k in range(2)
        ],
        *[
            pltpu.make_async_copy(sources[0].at[pl.ds(k * LOAD, LOAD), :], first_ref.at[pl.ds(k * LOAD, LOAD), :], in_sems.at[k])
            for k in range(pieces)
        ],
        pltpu.make_async_copy(sources[2], block_ref, in_sems.at[pieces + 2]),
    ]
    for arrival in arrivals:
        arrival.start()
    for arrival in arrivals[:2]:
        arrival.wait()
    for k in range(pieces):
        arrivals[2 + k].wait()
        here = pl.ds(k * LOAD, LOAD)
        both_ref[here, :] = times_transposed(first_ref[here, :], branches_ref[...])
    departures = [pltpu.make_async_copy(both_ref, out_refs[6], out_sems.at[0])]
    departures[0].start()

    padded_ref[pl.ds(0, SUB), :] = jnp.zeros((SUB, width), WIDE)
    padded_ref[pl.ds(SUB, count), :] = both_ref[:, width:]
    state_ref[pl.ds(0, SUB), :] = jnp.zeros((SUB, width), WIDE)
    taps = taps_ref[...]
    bias, rate_b, inlet_b, soft = (extra_ref[k : k + 1, :] for k in range(4))
    lanes = lax.broadcasted_iota(jnp.int32, (CHUNK, width), 0) % SUB

    def convolve(at, _):
        base = pl.multiple_of(at * CHUNK, SUB)
        pos = row_positions(scalars_ref, base, CHUNK, width)
        window = padded_ref[pl.ds(base, CHUNK + SUB), :]
        total = bias + taps[0:1] * window[SUB:]
        for k in range(1, taps.shape[0]):
            moved = window[SUB - k : SUB - k + CHUNK]
            total = total + jnp.where(pos >= k, taps[k : k + 1] * moved, 0.0)
        conv_ref[pl.ds(base, CHUNK), :] = total.astype(LOW)
        return _

    lax.fori_loop(0, count // CHUNK, convolve, 0)

    rate_ref[...] = jax.nn.sigmoid(times(conv_ref[...], rate_w_ref[...]) + rate_b)
    inlet_ref[...] = jax.nn.sigmoid(times(conv_ref[...], inlet_w_ref[...]) + inlet_b)
    for k, (ref, out_ref) in enumerate(((conv_ref, out_refs[2]), (rate_ref, out_refs[3]), (inlet_ref, out_refs[4]))):
        departures.append(pltpu.make_async_copy(ref, out_ref, out_sems.at[1 + k]))
        departures[-1].start()

    def step(at, before):
        base = pl.multiple_of(at * CHUNK, SUB)
        here = pl.ds(base, CHUNK)
        pos = row_positions(scalars_ref, base, CHUNK, width)
        a, scale = gates(rate_ref[here, :], inlet_ref[here, :], soft, pos == 0)
        b = scale * inlet_ref[here, :] * conv_ref[here, :].astype(WIDE)
        for k in (1, 2, 4):
            inside = lanes >= k
            b = b + jnp.where(inside, a * pltpu.roll(b, k, 0), 0.0)
            a = jnp.where(inside, a * pltpu.roll(a, k, 0), a)
        tiles = []
        for j in range(CHUNK // SUB):
            part = slice(j * SUB, (j + 1) * SUB)
            tile = a[part] * before + b[part]
            before = tile[SUB - 1 : SUB]
            tiles.append(tile)
        state = jnp.concatenate(tiles, axis=0)
        state_ref[pl.ds(base + SUB, CHUNK), :] = state
        mixed_ref[here, :] = (state * gelu(both_ref[here, :width])).astype(LOW)
        return before

    lax.fori_loop(0, count // CHUNK, step, jnp.zeros((1, width), WIDE))
    for k, (ref, out_ref) in enumerate(((mixed_ref, out_refs[1]), (state_ref, out_refs[5]))):
        departures.append(pltpu.make_async_copy(ref, out_ref, out_sems.at[4 + k]))
        departures[-1].start()
    arrivals[-1].wait()
    for k in range(features // TILE):
        here = pl.ds(k * TILE, TILE)
        partial_ref[:, here] = times(mixed_ref[...], block_ref[:, here]).astype(LOW)
        departures.append(pltpu.make_async_copy(partial_ref.at[:, here], out_refs[0].at[:, here], out_sems.at[6 + k]))
        departures[-1].start()
    for departure in departures:
        departure.wait()


def backward_kernel(heads, owners, scalars_ref, *refs):
    sources, small_refs, refs = refs[:10], refs[10:16], refs[16:]
    partial_out_ref, quarter_out_refs, held, refs = refs[0], refs[1:5], refs[5:15], refs[15:]
    grad_ref, back_ref, padded_ref, rate_low_ref, inlet_low_ref, stacked_ref, strips_ref = refs[:7]
    partials_ref, quarters_ref, in_sems, out_sems = refs[7:]
    taps_ref, rate_w_ref, inlet_w_ref, extra_ref, first_gain_ref, second_grad_ref = small_refs
    middle_ref, block_ref, both_ref, conv_ref, rate_ref, inlet_ref, state_ref, mixed_ref, first_ref, branches_ref = held
    arrivals = [pltpu.make_async_copy(*pair, in_sems.at[k]) for k, pair in enumerate(zip(sources, held))]
    for arrival in arrivals:
        arrival.start()
    for arrival in arrivals[:2]:
        arrival.wait()
    count, width = grad_ref.shape
    features = middle_ref.shape[1]

    def spread_rows(turn, _):
        here = pl.ds(pl.multiple_of(turn * ROWS, ROWS), ROWS)
        grad_ref[here, :] = times_transposed(middle_ref[here, :], block_ref[...])
        return _

    lax.fori_loop(0, count // ROWS, spread_rows, 0)
    for arrival in arrivals[2:7]:
        arrival.wait()
    padded_ref[pl.ds(0, SUB), :] = jnp.zeros((SUB, width), WIDE)
    padded_ref[pl.ds(SUB, count), :] = both_ref[:, width:]
    taps = taps_ref[...]
    soft = extra_ref[3:4, :]
    slope = extra_ref[4:5, :]
    lanes = lax.broadcasted_iota(jnp.int32, (CHUNK, width), 0) % SUB
    steps = count // CHUNK
    zero = jnp.zeros((1, width), WIDE)

    def column(values):
        return jnp.sum(values, axis=0, keepdims=True)

    def step(turn, held):
        after, late, beyond, sums = held
        base = pl.multiple_of((steps - 1 - turn) * CHUNK, SUB)
        here = pl.ds(base, CHUNK)
        wide_pos = row_positions(scalars_ref, base, CHUNK + SUB, width)
        pos = wide_pos[:CHUNK]
        fresh = pos == 0
        grad = grad_ref[here, :]
        value, bend = gelu_pair(both_ref[here, :width])
        window = state_ref[pl.ds(base, CHUNK + SUB), :]
        state = window[SUB:]
        earlier = window[SUB - 1 : SUB - 1 + CHUNK]
        back_ref[here, :width] = (grad * state * bend).astype(LOW)
        rate = rate_ref[here, :]
        inlet = inlet_ref[here, :]
        conv = conv_ref[here, :]
        conv_wide = conv.astype(WIDE)
        carry, scale = gates(rate, inlet, soft, fresh)
        b = grad * value
        a = jnp.concatenate([carry[1:], late], axis=0)
        for k in (1, 2, 4):
            inside = lanes < SUB - k
            b = b + jnp.where(inside, a * pltpu.roll(b, CHUNK - k, 0), 0.0)
            a = jnp.where(inside, a * pltpu.roll(a, CHUNK - k, 0), a)
        tiles = []
        for j in reversed(range(CHUNK // SUB)):
            part = slice(j * SUB, (j + 1) * SUB)
            tile = a[part] * after + b[part]
            after = tile[0:1]
            tiles.append(tile)
        total = jnp.concatenate(tiles[::-1], axis=0)
        late = carry[0:1]
        scaled = total * scale
        d_inlet = scaled * conv_wide
        d_scale = total * inlet * conv_wide
        d_log = jnp.where(fresh, 0.0, total * earlier * carry - d_scale * (carry * carry) / scale)
        leak = rate * d_log
        rate_low = (-soft * leak * (1.0 - rate)).astype(LOW)
        inlet_low = (d_inlet * inlet * (1.0 - inlet)).astype(LOW)
        rate_low_ref[here, :] = rate_low
        inlet_low_ref[here, :] = inlet_low
        spread = (
            scaled * inlet
            + times_transposed(rate_low, rate_w_ref[...])
            + times_transposed(inlet_low, inlet_w_ref[...])
        )
        ahead = jnp.concatenate([spread, beyond], axis=0)
        back = taps[0:1] * spread
        source = padded_ref[pl.ds(base, CHUNK + SUB), :]
        new = [column(spread), column(rate_low.astype(WIDE)), column(inlet_low.astype(WIDE)), column(leak)]
        new.append(column(spread * source[SUB:]))
        for k in range(1, taps.shape[0]):
            kept = jnp.where(wide_pos >= k, ahead, 0.0)
            back = back + taps[k : k + 1] * kept[k : k + CHUNK]
            new.append(column(kept[:CHUNK] * source[SUB - k : SUB - k + CHUNK]))
        back_ref[here, width:] = back.astype(LOW)
        return after, late, spread[:SUB], tuple(x + y for x, y in zip(sums, new))

    start = tuple(zero for _ in range(4 + taps.shape[0]))
    sums = lax.fori_loop(0, steps, step, (zero, zero, jnp.zeros((SUB, width), WIDE), start))[3]
    rows = list(sums)
    rows[3] = -slope * rows[3]
    size = width // heads
    strips, depth = strip_shape(features, heads, size, len(rows))
    stacked_ref[...] = jnp.zeros_like(stacked_ref)
    block = 0
    for low_ref in (rate_low_ref, inlet_low_ref):
        full = transposed_times(conv_ref[...], low_ref[...])
        for h in range(heads):
            part = slice(h * size, (h + 1) * size)
            stacked_ref[pl.ds(block * size, size), :] = full[part, part]
            block += 1
    small = jnp.concatenate(rows, axis=0)
    for h in range(heads):
        stacked_ref[pl.ds(block * size + h * SUB, len(rows)), :] = small[:, h * size : (h + 1) * size]
    strips_ref[...] = jnp.zeros_like(strips_ref)
    for k in range(strips):
        strips_ref[:, k * size : (k + 1) * size] = stacked_ref[pl.ds(k * depth, depth), :].astype(LOW)

    for arrival in arrivals[7:]:
        arrival.wait()
    share = count // owners
    quarter = features // 4
    departures = []
    for slot in range(4):
        if slot >= 2:
            for departure in departures[slot - 2]:
                departure.wait()
        partial_ref, quarter_ref = partials_ref.at[slot % 2], quarters_ref.at[slot % 2]
        here = pl.ds(pl.multiple_of(scalars_ref[0, slot] * quarter, quarter), quarter)
        branch_grad = transposed_times(back_ref[...], first_ref[:, here])
        quarter_ref[: 2 * width, :] = branch_grad.astype(LOW)
        quarter_ref[2 * width : 3 * width, :] = transposed_times(mixed_ref[...], middle_ref[:, here]).astype(LOW)
        quarter_ref[3 * width :, :] = strips_ref[:, here]
        gain = column(branch_grad * branches_ref[:, here].astype(WIDE)) / first_gain_ref[:, here]
        tops = []
        for value in (gain, second_grad_ref[:, here]):
            top = value.astype(LOW).astype(WIDE)
            tops += [top, value - top]
        tops = jnp.concatenate(tops + [jnp.zeros((SPARE - len(tops), quarter), WIDE)], axis=0).astype(LOW)
        partial = times(back_ref[...], branches_ref[:, here]).astype(LOW)
        for k in range(owners):
            base = k * (share + SPARE)
            partial_ref[base : base + share, :] = partial[k * share : (k + 1) * share]
            partial_ref[base + share : base + share + SPARE, :] = tops
        departures.append(
            [
                pltpu.make_async_copy(quarter_ref, quarter_out_refs[slot], out_sems.at[2 * slot]),
                pltpu.make_async_copy(partial_ref, partial_out_ref.at[:, here], out_sems.at[2 * slot + 1]),
            ]
        )
        for departure in departures[slot]:
            departure.start()
    for slot in (2, 3):
        for departure in departures[slot]:
            departure.wait()


def strip_shape(features, heads, size, small):
    strips = features // size
    rows = 2 * heads * size + heads * SUB
    return strips, -(-rows // (strips * 2 * SUB)) * 2 * SUB


def unpack_kernel(heads, strips, packed_ref, rate_ref, inlet_ref, taps_ref, *refs):
    line_refs, stacked_ref = refs[:-1], refs[-1]
    depth, size = packed_ref.shape[0], rate_ref.shape[-1]
    for k in range(strips):
        stacked_ref[pl.ds(k * depth, depth), :] = packed_ref[:, k * size : (k + 1) * size]
    for h in range(heads):
        rate_ref[h] = stacked_ref[pl.ds(h * size, size), :]
        inlet_ref[h] = stacked_ref[pl.ds((heads + h) * size, size), :]
    small = jnp.concatenate(
        [stacked_ref[pl.ds(2 * heads * size + h * SUB, SUB), :] for h in range(heads)], axis=1
    )
    taps_ref[...] = small[len(line_refs) :]
    for k, line_ref in enumerate(line_refs):
        line_ref[...] = small[k]


def unpack_strips(packed, heads, size):
    strips, depth = strip_shape(packed.shape[1], heads, size, SUB)
    return pl.pallas_call(
        lambda *refs: unpack_kernel(heads, strips, *refs),
        out_shape=[
            jax.ShapeDtypeStruct((heads, size, size), WIDE),
            jax.ShapeDtypeStruct((heads, size, size), WIDE),
            jax.ShapeDtypeStruct((SUB - 4, heads * size), WIDE),
        ]
        + [jax.ShapeDtypeStruct((heads * size,), WIDE)] * 4,
        scratch_shapes=[pltpu.VMEM((strips * depth, size), WIDE)],
        compiler_params=pltpu.CompilerParams(vmem_limit_bytes=16 * 1024 * 1024),
        cost_estimate=NO_COST,
    )(packed)


def in_vmem():
    return pl.BlockSpec(memory_space=pltpu.VMEM)


def run_kernel(body, outs, scratch, operands, room):
    return pl.pallas_call(
        body,
        in_specs=[pl.BlockSpec(memory_space=pltpu.SMEM)] + [in_vmem()] * (len(operands) - 1),
        out_specs=[in_vmem()] * len(outs),
        out_shape=outs,
        scratch_shapes=scratch,
        compiler_params=pltpu.CompilerParams(vmem_limit_bytes=room * 1024 * 1024),
        cost_estimate=NO_COST,
    )(*operands)


def forward_mix(scalars, first, branches, block, taps, rate_w, inlet_w, extra):
    count, features = first.shape
    width = block.shape[0]
    made = [
        ((count, features), LOW),
        ((count, width), LOW),
        ((count, width), LOW),
        ((count, width), WIDE),
        ((count, width), WIDE),
        ((count + SUB, width), WIDE),
        ((count, 2 * width), WIDE),
    ]
    anywhere = pl.BlockSpec(memory_space=pl.ANY)
    return pl.pallas_call(
        forward_kernel,
        in_specs=[pl.BlockSpec(memory_space=pltpu.SMEM)] + [anywhere] * 3 + [in_vmem()] * 4,
        out_specs=[anywhere] * len(made),
        out_shape=[jax.ShapeDtypeStruct(*one) for one in made],
        scratch_shapes=[pltpu.VMEM(array.shape, array.dtype) for array in (first, branches, block)]
        + [pltpu.VMEM(*one) for one in made]
        + [
            pltpu.VMEM((count + SUB, width), WIDE),
            pltpu.SemaphoreType.DMA((count // LOAD + 3,)),
            pltpu.SemaphoreType.DMA((6 + features // TILE,)),
        ],
        compiler_params=pltpu.CompilerParams(vmem_limit_bytes=ROOM * 1024 * 1024),
        cost_estimate=NO_COST,
    )(scalars, first, branches, block, taps, rate_w, inlet_w, extra)


def backward_mix(heads, owners, scalars, large, small):
    middle, block = large[:2]
    count, features = middle.shape
    width = block.shape[0]
    size = width // heads
    strips, depth = strip_shape(features, heads, size, SUB)
    rows, lines = count + owners * SPARE, 3 * width + depth
    narrow = pltpu.VMEM((count, width), LOW)
    anywhere = pl.BlockSpec(memory_space=pl.ANY)
    return pl.pallas_call(
        lambda *refs: backward_kernel(heads, owners, *refs),
        in_specs=[pl.BlockSpec(memory_space=pltpu.SMEM)] + [anywhere] * len(large) + [in_vmem()] * len(small),
        out_specs=[anywhere] * 5,
        out_shape=[jax.ShapeDtypeStruct((rows, features), LOW)] + [jax.ShapeDtypeStruct((lines, features // 4), LOW)] * 4,
        scratch_shapes=[pltpu.VMEM(array.shape, array.dtype) for array in large]
        + [
            pltpu.VMEM((count, width), WIDE),
            pltpu.VMEM((count, 2 * width), LOW),
            pltpu.VMEM((count + SUB, width), WIDE),
            narrow,
            narrow,
            pltpu.VMEM((strips * depth, size), WIDE),
            pltpu.VMEM((depth, features), LOW),
            pltpu.VMEM((2, rows, features // 4), LOW),
            pltpu.VMEM((2, lines, features // 4), LOW),
            pltpu.SemaphoreType.DMA((len(large),)),
            pltpu.SemaphoreType.DMA((8,)),
        ],
        compiler_params=pltpu.CompilerParams(vmem_limit_bytes=ROOM * 1024 * 1024),
        cost_estimate=NO_COST,
    )(scalars, *large, *small)


def call_blocks(body, grid, spots, inputs, outputs, operands, room):
    return pl.pallas_call(
        body,
        grid_spec=pltpu.PrefetchScalarGridSpec(
            num_scalar_prefetch=1,
            grid=(grid,),
            in_specs=[pl.BlockSpec(shape, index) for shape, index in inputs],
            out_specs=[pl.BlockSpec(shape, index) for _, shape, index in outputs],
        ),
        out_shape=[made for made, _, _ in outputs],
        compiler_params=pltpu.CompilerParams(vmem_limit_bytes=room * 1024 * 1024),
        cost_estimate=NO_COST,
    )(spots, *operands)


def whole(_, at):
    return (0, 0)


def across(k, at):
    return (0, k)


def down(k, at):
    return (k, 0)


def across_spot(k, at):
    return (0, at[k])


def down_spot(k, at):
    return (at[k], 0)


def early_kernel(spots_ref, *refs):
    rows_hbm, lows_hbm, weights_hbm, refs = refs[0], refs[1:3], refs[3:5], refs[5:]
    partial_hbm, sends_hbm, refs = refs[0], refs[1:3], refs[3:]
    rows_refs, low_refs, weight_refs, partial_ref, send_refs = refs[0:2], refs[2:4], refs[4:6], refs[6], refs[7:9]
    in_sems, out_sems = refs[9:]
    features = partial_ref.shape[1]
    tiles = features // TILE
    half = features // 2
    low_copies = [pltpu.make_async_copy(lows_hbm[k], low_refs[k], in_sems.at[k]) for k in range(2)]
    weight_copies = [
        [
            pltpu.make_async_copy(
                weights_hbm[k].at[pl.ds(t * TILE, TILE), :],
                weight_refs[k].at[pl.ds(t * TILE, TILE), :],
                in_sems.at[2 + 2 * t + k],
            )
            for k in range(2)
        ]
        for t in range(tiles)
    ]
    row_copies = [
        pltpu.make_async_copy(
            rows_hbm.at[:, pl.ds(pl.multiple_of(spots_ref[k] * half, half), half)],
            rows_refs[k],
            in_sems.at[2 + 2 * tiles + k],
        )
        for k in range(2)
    ]
    for copy in low_copies + [copy for pair in weight_copies for copy in pair] + row_copies:
        copy.start()
    for copy in low_copies:
        copy.wait()
    departures = []
    for t in range(tiles):
        here = pl.ds(t * TILE, TILE)
        for copy in weight_copies[t]:
            copy.wait()
        total = times_transposed(low_refs[0][...], weight_refs[0][here, :])
        total += times_transposed(low_refs[1][...], weight_refs[1][here, :])
        partial_ref[:, here] = total.astype(LOW)
        departures.append(pltpu.make_async_copy(partial_ref.at[:, here], partial_hbm.at[:, here], out_sems.at[t]))
        departures[-1].start()
    for k in range(2):
        row_copies[k].wait()
        for t in range(half // TILE):
            here = pl.ds(t * TILE, TILE)
            send_refs[k][here, :] = transposed_times(rows_refs[k][:, here], low_refs[k][...]).astype(LOW)
            departures.append(
                pltpu.make_async_copy(
                    send_refs[k].at[here, :], sends_hbm[k].at[here, :], out_sems.at[tiles + k * (half // TILE) + t]
                )
            )
            departures[-1].start()
    for departure in departures:
        departure.wait()


def early_products(rows, gate_low, up_low, gate_weight, up_weight, spots):
    count, features = rows.shape
    units = gate_low.shape[1]
    half = features // 2
    made = [((count, features), LOW), ((half, units), LOW), ((half, units), LOW)]
    anywhere = pl.BlockSpec(memory_space=pl.ANY)
    return pl.pallas_call(
        early_kernel,
        in_specs=[pl.BlockSpec(memory_space=pltpu.SMEM)] + [anywhere] * 5,
        out_specs=[anywhere] * 3,
        out_shape=[jax.ShapeDtypeStruct(*one) for one in made],
        scratch_shapes=[pltpu.VMEM((count, half), LOW)] * 2
        + [pltpu.VMEM((count, units), LOW)] * 2
        + [pltpu.VMEM((features, units), LOW)] * 2
        + [pltpu.VMEM(*one) for one in made]
        + [
            pltpu.SemaphoreType.DMA((4 + 2 * (features // TILE),)),
            pltpu.SemaphoreType.DMA((2 * (features // TILE),)),
        ],
        compiler_params=pltpu.CompilerParams(vmem_limit_bytes=ROOM * 1024 * 1024),
        cost_estimate=NO_COST,
    )(spots, rows, gate_low, up_low, gate_weight, up_weight)


def gradient_kernel(_, left_ref, right_ref, out_ref):
    out_ref[...] = transposed_times(left_ref[...], right_ref[...]).astype(LOW)


def gradient_half(left, right, which):
    count, features = left.shape
    units = right.shape[1]
    block = features // 4
    spots = jnp.stack([2 * which, 2 * which + 1]).astype(jnp.int32)
    return call_blocks(
        gradient_kernel,
        2,
        spots,
        [((count, block), across_spot), ((count, units), whole)],
        [(jax.ShapeDtypeStruct((2 * block, units), LOW), (block, units), down)],
        (left, right),
        ROOM,
    )[0]


def norm_kernel(_, start_ref, added_ref, gain_ref, *out_refs):
    values = start_ref[...].astype(WIDE)
    if len(out_refs) == 2:
        values = values + added_ref[...].astype(WIDE)
        out_refs[1][...] = values
    out_refs[0][...] = (values * norm_scale(values) * gain_ref[...]).astype(LOW)


def normed(start, gain, added=None):
    rows, features = start.shape
    block = (rows // 2, features)
    outs = [(jax.ShapeDtypeStruct((rows, features), kind), block, down) for kind in (LOW, WIDE)]
    return call_blocks(
        norm_kernel,
        2,
        jnp.zeros((1,), jnp.int32),
        [(block, down), (block, down), ((1, features), whole)],
        outs if added is not None else outs[:1],
        (start, start if added is None else added, gain[None]),
        ROOM,
    )


def norm_back_kernel(_, start_ref, grad_ref, added_ref, gain_ref, low_ref, total_ref, gain_grad_ref):
    values, grad = start_ref[...], grad_ref[...].astype(WIDE)
    scale = norm_scale(values)
    total = added_ref[...].astype(WIDE) + norm_back(values, scale, gain_ref[...], grad)
    total_ref[...] = total
    low_ref[...] = total.astype(LOW)
    part = jnp.sum(grad * values * scale, axis=0, keepdims=True)

    @pl.when(pl.program_id(0) == 0)
    def _():
        gain_grad_ref[...] = part

    @pl.when(pl.program_id(0) > 0)
    def _():
        gain_grad_ref[...] += part


def normed_back(start, grad, added, gain):
    rows, features = start.shape
    block = (rows // 2, features)
    line = (1, features)
    return call_blocks(
        norm_back_kernel,
        2,
        jnp.zeros((1,), jnp.int32),
        [(block, down)] * 3 + [(line, whole)],
        [(jax.ShapeDtypeStruct((rows, features), kind), block, down) for kind in (LOW, WIDE)]
        + [(jax.ShapeDtypeStruct(line, WIDE), line, whole)],
        (start, grad, added, gain[None]),
        ROOM,
    )


def spread_blocks(weights):
    heads, size, _ = weights.shape
    full = jnp.zeros((heads, size, heads, size), weights.dtype)
    for h in range(heads):
        full = full.at[h, :, h, :].set(weights[h])
    return full.reshape(heads * size, heads * size)


def sum_rows(values):
    return lax.psum_scatter(values.astype(LOW), "mp", scatter_dimension=0, tiled=True)


def all_rows(values):
    return lax.all_gather(values, "mp", axis=0, tiled=True)


def place_kernel(count, axis, splits, kept, spots_ref, *refs):
    sources, outs, refs = refs[:count], refs[count + kept : count + kept + len(splits)], refs[count + kept + len(splits) :]
    in_sems, out_sems = refs[-2:]
    size = sources[0].shape[axis]
    same = sources[0].dtype == outs[0].dtype
    held, wide = ((), ()) if same else (refs[:count], refs[count : 2 * count])
    arrivals = [pltpu.make_async_copy(sources[k], held[k], in_sems.at[k]) for k in range(len(held))]
    for arrival in arrivals:
        arrival.start()
    departures = []
    for k in range(count):
        if not same:
            arrivals[k].wait()
            wide[k][...] = held[k][...].astype(wide[k].dtype)
        here = pl.ds(pl.multiple_of(spots_ref[k] * size, size), size)
        start = 0
        for j, rows in enumerate(splits):
            part = (sources[k] if same else wide[k]).at[pl.ds(start, rows), :]
            target = outs[j].at[here, :] if axis == 0 else outs[j].at[:, here]
            departures.append(pltpu.make_async_copy(part, target, out_sems.at[k * len(splits) + j]))
            departures[-1].start()
            start += rows
    for departure in departures:
        departure.wait()


def place(pieces, spots, total, axis, splits, kind, onto=()):
    count = len(pieces)
    rows, columns = pieces[0].shape
    splits = splits or (rows,)
    outs = [
        jax.ShapeDtypeStruct((r * total, columns) if axis == 0 else (r, columns * total), kind) for r in splits
    ]
    anywhere = pl.BlockSpec(memory_space=pl.ANY)
    scratch = [] if pieces[0].dtype == kind else [pltpu.VMEM((rows, columns), LOW)] * count + [pltpu.VMEM((rows, columns), kind)] * count
    return pl.pallas_call(
        lambda *refs: place_kernel(count, axis, splits, len(onto), *refs),
        in_specs=[pl.BlockSpec(memory_space=pltpu.SMEM)] + [anywhere] * (count + len(onto)),
        out_specs=[anywhere] * len(outs),
        out_shape=outs,
        scratch_shapes=scratch
        + [pltpu.SemaphoreType.DMA((count,)), pltpu.SemaphoreType.DMA((count * len(splits),))],
        input_output_aliases={1 + count + k: k for k in range(len(onto))},
        compiler_params=pltpu.CompilerParams(
            vmem_limit_bytes=ROOM * 1024 * 1024 if onto else rows * columns * 6 * count + 4 * 1024 * 1024
        ),
        cost_estimate=NO_COST,
    )(jnp.stack(spots).astype(jnp.int32), *pieces, *onto)


def dp_bits():
    return lax.axis_size("dp").bit_length() - 1


def swap(values, bit):
    count = lax.axis_size("dp")
    return lax.ppermute(values, "dp", [(i, i ^ (1 << bit)) for i in range(count)])


def order_of(turn):
    bits = dp_bits()
    return [(turn + k) % bits for k in range(bits)]


def upper_of(bit):
    return (lax.axis_index("dp") >> bit) & 1


def quarter_spots():
    left, right = (upper_of(order_of(turn)[0]) for turn in range(2))
    return jnp.stack([1 - left, left, 3 - right, 2 + right]).astype(jnp.int32)


def halves(values, axis):
    size = values.shape[axis] // 2
    return lax.slice_in_dim(values, 0, size, axis=axis), lax.slice_in_dim(values, size, 2 * size, axis=axis)


def split_for(values, axis, bit):
    first, second = halves(values, axis)
    upper = upper_of(bit) == 1
    return jnp.where(upper, first, second), jnp.where(upper, second, first)


class Part:
    def __init__(self, send, kept, axis, turn):
        self.send, self.kept = send, kept
        self.axis, self.order = axis, order_of(turn)
        self.step = 0

    def reduce(self):
        return swap(self.send, self.order[self.step])

    def land(self, got):
        self.step += 1
        if self.step < len(self.order):
            bit = self.order[self.step]
            kept, sent = (split_for(values, self.axis, bit)[0] for values in (self.kept, got))
            self.send = (kept.astype(WIDE) + sent.astype(WIDE)).astype(LOW)
            kept, got, _ = lax.optimization_barrier((self.kept, got, self.send))
            kept, got = (split_for(values, self.axis, bit)[1] for values in (kept, got))
            self.kept = (kept.astype(WIDE) + got.astype(WIDE)).astype(LOW)
        else:
            self.pieces = {0: (self.kept.astype(WIDE) + got.astype(WIDE)).astype(LOW)}

    def forwards(self, level):
        made = []
        for chosen in itertools.combinations(reversed(self.order), level):
            made.append((sum(1 << bit for bit in chosen[:-1]), chosen[-1]))
        return made

    def spot(self, mask):
        owner = lax.axis_index("dp") ^ mask
        bits = len(self.order)
        return sum(((owner >> self.order[k]) & 1) << (bits - 1 - k) for k in range(bits))


def start_gather(parts, level):
    return [(part, mask ^ (1 << bit), swap(part.pieces[mask], bit)) for part in parts for mask, bit in part.forwards(level)]


def exchange(reducing=(), gathered=(), extras=()):
    gots = [part.reduce() for part in reducing]
    made = lax.optimization_barrier(
        (*[part.kept for part in reducing], *gots, *[piece for _, _, piece in gathered], *extras)
    )
    for part, kept in zip(reducing, made):
        part.kept = kept
    made = made[len(gots) :]
    for part, got in zip(reducing, made):
        part.land(got)
    made = made[len(gots) :]
    for (part, mask, _), piece in zip(gathered, made):
        part.pieces[mask] = piece
    return made[len(gathered) :]


def reduce_fully(parts):
    while parts[0].step < len(parts[0].order):
        exchange(parts)


def gather_fully(parts, level):
    for more in range(level, dp_bits() + 1):
        exchange(gathered=start_gather(parts, more))


def finish(parts, axis, splits=None, masks=None, onto=()):
    count = 1 << dp_bits()
    chosen = [(turn, mask) for turn, part in enumerate(parts) for mask in part.pieces if masks is None or mask in masks]
    spots = [parts[turn].spot(mask) + turn * count for turn, mask in chosen]
    blocks = [parts[turn].pieces[mask] for turn, mask in chosen]
    return place(blocks, spots, len(parts) * count, axis, splits, WIDE, onto)


def column_parts(quarters):
    return [Part(quarters[2 * turn], quarters[2 * turn + 1], 1, turn) for turn in range(2)]


def next_chip(values, step):
    count = lax.axis_size("mp")
    return lax.ppermute(values, "mp", [(i, (i + 2 * step) % count) for i in range(count)])


def other_core(values):
    return lax.ppermute(values, "mp", [(i, i ^ 1) for i in range(lax.axis_size("mp"))])


def tie(values, *others):
    return lax.optimization_barrier((values,) + others)[0]


def local(
    tokens,
    lengths,
    first_gain,
    branch_gate,
    branch_input,
    conv_weight,
    conv_bias,
    rate_weight,
    rate_bias,
    inlet_weight,
    inlet_bias,
    decay_param,
    block_out,
    second_gain,
    gate_weight,
    up_weight,
    down_weight,
    out_grad,
):
    heads = rate_weight.shape[0]
    width = decay_param.shape[0]
    features = tokens.shape[1]
    taps_count = conv_weight.shape[0]
    own_count = tokens.shape[0]
    own_input = tokens.astype(WIDE)
    own_grad = out_grad.astype(WIDE)
    first_rows = all_rows(normed(tokens, first_gain)[0])
    soft = DECAY_SCALE * jax.nn.softplus(decay_param)
    slope = DECAY_SCALE * jax.nn.sigmoid(decay_param)
    extra = jnp.stack([conv_bias, rate_bias, inlet_bias, soft, slope])
    rate_w = spread_blocks(rate_weight)
    inlet_w = spread_blocks(inlet_weight)
    branches = jnp.concatenate([branch_gate.T, branch_input.T])

    scalars = jnp.concatenate([quarter_spots(), lengths[0]])[None]
    onward = {0: out_grad}
    first_rows, onward[1] = lax.optimization_barrier(
        (first_rows, next_chip(out_grad, 1), rate_w, inlet_w, extra, branches, scalars)
    )[:2]
    block_partial, mixed, conv, rate, inlet, state, both = forward_mix(
        scalars, first_rows, branches, block_out, conv_weight, rate_w, inlet_w, extra
    )
    chips = lax.axis_size("mp") // 2
    backward = {1: next_chip(tie(onward[0], first_rows), -1)}
    block_partial, backward[1] = lax.optimization_barrier((block_partial, backward[1]))

    block_sum = sum_rows(block_partial)
    shards = {hop: piece for hop, piece in onward.items()} | {-hop: piece for hop, piece in backward.items()}
    made = lax.optimization_barrier((block_sum, *[other_core(piece) for piece in shards.values()]))
    block_sum = made[0]
    others = dict(zip(shards, made[1:]))
    own_second, own_middle = normed(tokens, second_gain, block_sum)
    second_rows = all_rows(own_second)

    onward[1], backward[1] = lax.optimization_barrier((onward[1], backward[1], own_second))[:2]
    for hop in range(2, chips // 2 + 1):
        onward[hop] = next_chip(onward[hop - 1], 1)
        shards[hop], others[hop] = onward[hop], other_core(onward[hop])
        if 2 * hop < chips:
            backward[hop] = next_chip(backward[hop - 1], -1)
            shards[-hop], others[-hop] = backward[hop], other_core(backward[hop])
    me = lax.axis_index("mp")
    blocks, places = [], []
    for hop in shards:
        base = 2 * ((me // 2 + chips - hop) % chips)
        blocks += [shards[hop], others[hop]]
        places += [base + me % 2, base + 1 - me % 2]
    (grad_rows,) = place(blocks, places, 2 * chips, 0, None, LOW)
    d_hidden = times_transposed(grad_rows, down_weight)
    second_rows, d_hidden = lax.optimization_barrier((second_rows, d_hidden))
    gate_act = times(second_rows, gate_weight)
    up_act = times(second_rows, up_weight)
    hidden = (gelu(gate_act) * up_act).astype(LOW)
    down_parts = []
    for turn, half in enumerate(halves(transposed_times(hidden, grad_rows).astype(LOW), 1)):
        down_parts.append(Part(*split_for(half, 1, order_of(turn)[0]), 1, turn))
    gate_act, up_act, d_hidden = lax.optimization_barrier(
        (gate_act, up_act, d_hidden, *[part.send for part in down_parts])
    )[:3]
    value, bend = gelu_pair(gate_act)
    gate_low = (d_hidden * up_act * bend).astype(LOW)
    up_low = (d_hidden * value).astype(LOW)

    late_rows = tie(second_rows, *[part.send for part in down_parts])
    uppers = [upper_of(order_of(turn)[0]) for turn in range(2)]
    spots = jnp.stack([1 - upper for upper in uppers]).astype(jnp.int32)
    made = early_products(late_rows, gate_low, up_low, gate_weight, up_weight, spots)
    partial, gate_send, up_send = exchange(down_parts, extras=made)

    second_input = sum_rows(partial)
    late_rows = tie(second_rows, partial)
    wide_parts = [
        Part(gate_send, gradient_half(late_rows, gate_low, uppers[0]), 0, 0),
        Part(up_send, gradient_half(late_rows, up_low, uppers[1]), 0, 1),
    ]
    mlp = down_parts + wide_parts
    middle_low, middle_grad, second_gain_grad = normed_back(own_middle, second_input, out_grad, second_gain)
    made = exchange(down_parts + wide_parts, extras=(middle_low, middle_grad, second_gain_grad))
    middle_low, middle_grad, second_gain_grad = made
    middle_rows = all_rows(middle_low)

    reduce_fully(down_parts)
    out_partial = times(tie(hidden, middle_low), down_weight)
    middle_rows, out_partial = exchange(wide_parts, start_gather(down_parts, 1), (middle_rows, out_partial))
    out_sum = sum_rows(out_partial)

    reduce_fully(wide_parts)
    owners = lax.axis_size("mp")
    made = backward_mix(
        heads,
        owners,
        scalars,
        (middle_rows, block_out, both, conv, rate, inlet, state, mixed, first_rows, branches),
        (conv_weight, rate_w, inlet_w, extra, first_gain[None], second_gain_grad),
    )
    first_partial, *quarters = made
    (first_partial,) = exchange(gathered=start_gather(wide_parts, 1), extras=(first_partial,))
    first_input = sum_rows(first_partial)
    output = (own_middle + out_sum.astype(WIDE)).astype(LOW)

    late = column_parts(quarters)
    wide_rest = start_gather(wide_parts, 2)
    exchange(late)
    down_rest = start_gather(down_parts, 2)
    (first_input,) = exchange(late, wide_rest + down_rest, (first_input,))
    gather_fully(mlp, 3)
    reduce_fully(late)
    first_input = first_input.astype(WIDE)
    first_scale = norm_scale(own_input)
    sums = first_input[own_count:]
    gains = jnp.stack([sums[0] + sums[1], sums[2] + sums[3]])
    input_grad = middle_grad + norm_back(own_input, first_scale, first_gain, first_input[:own_count])
    (gate_grad,) = finish([wide_parts[0]], 0)
    (up_grad,) = finish([wide_parts[1]], 0)
    (down_grad,) = finish(down_parts, 1)
    gate_grad, down_grad, input_grad, other = exchange(
        gathered=start_gather(late, 1), extras=(gate_grad, down_grad, input_grad, swap(gains, 0))
    )
    gains = gains + other
    own = [0] + [1 << bit for bit in range(dp_bits())]
    splits = (width, width, width, quarters[0].shape[0] - 3 * width)
    halfway = finish(late, 1, splits, own)
    made = exchange(gathered=start_gather(late, 2), extras=(swap(gains, 1), up_grad, *halfway, output))
    gather_fully(late, 3)
    gains, up_grad, output = gains + made[0], made[1], made[-1]
    for bit in range(2, dp_bits()):
        gains = gains + swap(gains, bit)
    rest = [mask for mask in late[0].pieces if mask not in own]
    branch_gate_grad, branch_input_grad, block_grad, packed = finish(late, 1, splits, rest, made[2:-1])
    rate_w_grad, inlet_w_grad, taps_grad, *lines = unpack_strips(packed, heads, width // heads)
    return (
        output,
        input_grad,
        gains[0],
        branch_gate_grad.T,
        branch_input_grad.T,
        taps_grad,
        lines[0],
        rate_w_grad,
        lines[1],
        inlet_w_grad,
        lines[2],
        lines[3],
        block_grad,
        gains[1],
        gate_grad,
        up_grad,
        down_grad,
    )


def solution(mesh):
    rows = P(("dp", "mp"), None)
    out_columns = P(None, "mp")
    out_rows = P("mp", None)
    blocks = P("mp", None, None)
    vector = P("mp")
    in_specs = (
        rows, P("dp", None), P(), out_columns, out_columns, out_columns, vector, blocks, vector, blocks,
        vector, vector, out_rows, P(), out_columns, out_columns, out_rows, rows,
    )
    out_specs = (
        rows, rows, P(), out_columns, out_columns, out_columns, vector, blocks, vector, blocks,
        vector, vector, out_rows, P(), out_columns, out_columns, out_rows,
    )
    return jax.shard_map(local, mesh=mesh, in_specs=in_specs, out_specs=out_specs, check_vma=False)
```
